256 devices in a mesh: line: 4 (over x), plane: 64 (over y, z, core).
Axes of the slice: x: 4, y: 4, z: 8, core: 2. Of those that a mesh axis runs over, the one named last changes fastest.
Arguments:
- adjoint: float32 [5, 64, 512, 256], P(None, 'line', 'plane'), may hold values from -6 to 6
- forcing: float32 [5, 64, 512, 256], P(None, 'line', 'plane'), may hold values from -6 to 6
- eigen_values: float32 [5, 64, 512, 256], P(None, 'line', 'plane'), may hold values from -1.5 to 1.5
- face_masks: int32 [2, 512, 256], P(None, 'plane'), may hold values 0 or 1
- line_coeffs: float32 [5, 6, 64, 256], P(None, None, 'line'), may hold values from 0 to 1, as said below
- cross_coeffs: float32 [5, 4, 512, 256], P(None, None, 'plane'), may hold values from 0 to 1, as said below
Outputs:
- update: float32 [5, 64, 512, 256], P(None, 'line', 'plane')
The draws below stay inside these ranges and needn't reach their ends.
Inputs may be any that keep to these rules, and one draw needn't show every extreme that they name: `line_coeffs`: every entry lies in [0, 1]; for each point the two lower coefficients and their diagonal inverse sum to 1, likewise the upper ones. `cross_coeffs`: every entry lies in [0, 1]; for each point a coefficient and its diagonal inverse sum to 1.
All inputs are finite; a program needn't handle non-finite values. No bound on the sum of `face_masks` on one device may be relied on, other than what follows from the above.
Results may differ from the reference program's by a relative error of at most 0.000022.
Values sent between devices are 32-bit elements; how exact they have to be, the bound alone decides.
No kernel may reach another device: no remote copies, remote signals or barrier semaphores. Data moves between devices by JAX's collectives and lax.ppermute only.
A program may use at most 64 MiB of HBM per device.

```python
import jax
import jax.numpy as jnp
from jax import lax

CHAR_VARIABLES = 5
NK = 256
NI = 64
NJ = 512


def retention(key, shape, line_length, slow_share):
    pick_key, slow_key, fast_key = jax.random.split(key, 3)
    slow_gap = jnp.exp(jax.random.uniform(slow_key, shape, jnp.float32, jnp.log(0.3 / line_length), jnp.log(2.0 / line_length)))
    fast_gap = jnp.exp(jax.random.uniform(fast_key, shape, jnp.float32, jnp.log(0.02), jnp.log(0.1)))
    chosen = jax.random.uniform(pick_key, shape, jnp.float32) < slow_share
    return jnp.where(chosen, slow_gap, fast_gap)


def rough_rate(key, gap, line_length):
    coarse_random_key, spike_random_key = jax.random.split(key, 2)
    decay_rate = 1.0 - gap * (0.5 + jax.random.uniform(coarse_random_key, (CHAR_VARIABLES, line_length, NK), jnp.float32))
    spike_event = jax.random.uniform(spike_random_key, (CHAR_VARIABLES, line_length, 1), jnp.float32) < 3.0 / line_length
    return jnp.where(spike_event, 0.6 * decay_rate, decay_rate)


def second_order(key, line_length, slow_share):
    gap_key, rate_key, share_key = jax.random.split(key, 3)
    gap = retention(gap_key, (CHAR_VARIABLES, 1, NK), line_length, slow_share)
    decay_rate = rough_rate(rate_key, gap, line_length)
    first = decay_rate * (0.75 + 0.2 * jax.random.uniform(share_key, (CHAR_VARIABLES, line_length, NK), jnp.float32))
    second = decay_rate - first
    return (first, second, 1.0 - first - second)


def first_order(key, line_length, slow_share):
    gap_key, rate_key = jax.random.split(key, 2)
    gap = retention(gap_key, (CHAR_VARIABLES, 1, NK), line_length, slow_share)
    decay_rate = rough_rate(rate_key, gap, line_length)
    return (decay_rate, 1.0 - decay_rate)


def draw_line_coeffs(key, part):
    key = jax.random.fold_in(key, 5)
    slow_share = 0.5
    lower_key, upper_key = jax.random.split(key, 2)
    lower = second_order(lower_key, NI, slow_share)
    upper = second_order(upper_key, NI, slow_share)
    return jnp.stack([lower[0], lower[1], lower[2], upper[0], upper[1], upper[2]], axis=1)


def draw_cross_coeffs(key, part):
    key = jax.random.fold_in(key, 9)
    slow_share = 0.5
    forward_key, backward_key = jax.random.split(key, 2)
    forward = first_order(forward_key, NJ, slow_share)
    backward = first_order(backward_key, NJ, slow_share)
    return jnp.stack([forward[0], forward[1], backward[0], backward[1]], axis=1)


def touch_ends(values, own_key, low, top_value):
    shape = values.shape
    index_at = [jax.random.randint(jax.random.fold_in(own_key, axis), (), 0, shape[axis]) for axis in range(len(shape))]
    values = values.at[tuple(index_at)].set(low)
    longest = shape.index(max(shape))
    index_at[longest] = (index_at[longest] + 1) % shape[longest]
    return values.at[tuple(index_at)].set(top_value)


def shard_levels(rng, extent, shards, smallest, top_value):
    factor_of, own = 1.0, jax.random.fold_in(rng, 6)
    for position, parts in shards:
        heights = jnp.exp(jax.random.uniform(jax.random.fold_in(own, position), (parts,), jnp.float32, smallest / len(shards), top_value / len(shards)))
        factor_of = factor_of * jnp.repeat(heights, extent[position] // parts).reshape([-1 if axis == position else 1 for axis in range(len(extent))])
    return factor_of


def centred(rng, shape, deviation, reach, shards=(), kind=jnp.bfloat16):
    drawn = jax.random.normal(rng, shape, jnp.float32) * deviation
    if len(shards) > 0:
        drawn = shard_levels(rng, shape, shards, -0.22, 0.18) * drawn
    return jnp.clip(drawn, min=-reach, max=reach).astype(kind)


def setup_inputs(seed: int = 0) -> dict:
    arg_keys = jax.random.split(jax.random.key(seed), 7)
    adjoint = centred(arg_keys[0], (CHAR_VARIABLES, NI, NJ, NK), 1.0, 6.0, ((1, 4), (2, 64)), jnp.float32)
    forcing = centred(arg_keys[1], (CHAR_VARIABLES, NI, NJ, NK), 1.0, 6.0, ((1, 4), (2, 64)), jnp.float32)
    eigen_values = jnp.clip(jax.random.uniform(arg_keys[2], (CHAR_VARIABLES, NI, NJ, NK), jnp.float32, -1.5, 1.5) * shard_levels(arg_keys[2], (CHAR_VARIABLES, NI, NJ, NK), ((1, 4), (2, 64)), -0.4, 0.0), -1.5, 1.5)
    face_masks = touch_ends((jax.random.randint(arg_keys[3], (2, NJ, NK), 0, 2) < 1).astype(jnp.int32), jax.random.fold_in(arg_keys[3], 1), 0, 1)
    line_coeffs = draw_line_coeffs(jax.random.fold_in(arg_keys[6], 71), 0)
    cross_coeffs = draw_cross_coeffs(jax.random.fold_in(arg_keys[6], 71), 0)
    return {"adjoint": adjoint, "forcing": forcing, "eigen_values": eigen_values, "face_masks": face_masks, "line_coeffs": line_coeffs, "cross_coeffs": cross_coeffs}


def recurse(source, first, second, weight, start_one, start_two):
    def advance_sweep(carry, inputs):
        prev_one, prev_two = carry
        term, coef_one, coef_two, scale = inputs
        value = scale * term + coef_one * prev_one + coef_two * prev_two
        return (value, prev_one), value
    (final_one, final_two), values = lax.scan(advance_sweep, (start_one, start_two), (source, first, second, weight))
    return values, final_one, final_two


def line_solve(source, coeffs):
    blank = jnp.zeros(source.shape[1:], jnp.float32)
    lower, _, _ = recurse(source, coeffs[:, :, 0], coeffs[:, :, 1], coeffs[:, :, 2], blank, blank)
    flipped = coeffs[::-1]
    upper, _, _ = recurse(lower[::-1], flipped[:, :, 3], flipped[:, :, 4], flipped[:, :, 5], blank, blank)
    return upper[::-1]


def cross_solve(source, coeffs):
    blank = jnp.zeros(source.shape[1:], jnp.float32)
    forward, _, _ = recurse(source, coeffs[:, :, 0], jnp.zeros_like(coeffs[:, :, 0]), coeffs[:, :, 1], blank, blank)
    flipped = coeffs[::-1]
    backward, _, _ = recurse(forward[::-1], flipped[:, :, 2], jnp.zeros_like(flipped[:, :, 2]), flipped[:, :, 3], blank, blank)
    return backward[::-1]


def reference(adjoint, forcing, eigen_values, face_masks, line_coeffs, cross_coeffs):
    weighted = eigen_values * adjoint
    masks_float = face_masks.astype(jnp.float32)
    low_face = masks_float[0][None] * weighted[:, 0]
    high_face = masks_float[1][None] * weighted[:, -1]
    extended = jnp.concatenate([low_face[:, None], weighted, high_face[:, None]], axis=1)
    padded = jnp.pad(extended, ((0, 0), (0, 0), (1, 1), (1, 1)))
    ipart = padded[:, :, 1:-1, 1:-1]
    along_first_index = ipart[:, :-2] - ipart[:, 2:]
    jpart = padded[:, 1:-1, :, 1:-1]
    along_j = jpart[:, :, :-2] - jpart[:, :, 2:]
    kpart = padded[:, 1:-1, 1:-1, :]
    along_k = kpart[..., :-2] - kpart[..., 2:]
    source = forcing + 0.5 * (along_first_index + along_j + along_k)
    lines = jnp.moveaxis(source, 1, 0)
    line_factors = jnp.moveaxis(line_coeffs, 2, 0)[:, :, :, None, :]
    solved = jnp.moveaxis(line_solve(lines, line_factors), 0, 1)
    cross = jnp.moveaxis(solved, 2, 0)
    cross_factors = jnp.moveaxis(cross_coeffs, 2, 0)[:, :, :, None, :]
    return jnp.moveaxis(cross_solve(cross, cross_factors), 0, 2)
```

```python
import jax
import jax.numpy as jnp
from jax import lax
from jax.experimental import pallas as pl
from jax.experimental.pallas import tpu as pltpu
from jax.sharding import PartitionSpec as P

F32 = jnp.float32
NV, NI, NJ, NK = 5, 16, 8, 256
HALF = NK // 2


def rows_of(shape):
    return lax.broadcasted_iota(jnp.int32, shape, len(shape) - 2)


def lanes_of(shape):
    return lax.broadcasted_iota(jnp.int32, shape, len(shape) - 1)


def call(kernel, outs, *args, scratch=(), any_out=False, name=None):
    outs = [jax.ShapeDtypeStruct(s, F32) for s in outs]
    space = pl.ANY if any_out else pltpu.VMEM
    return pl.pallas_call(
        kernel,
        out_shape=outs,
        in_specs=[pl.BlockSpec(memory_space=pltpu.VMEM)] * len(args),
        out_specs=[pl.BlockSpec(memory_space=space)] * len(outs),
        scratch_shapes=list(scratch),
        compiler_params=pltpu.CompilerParams(vmem_limit_bytes=40 * 1024 * 1024),
        name=name,
    )(*args)


def faces_kernel(a_ref, e_ref, ia_ref, ib_ref, ja_ref, jb_ref, scr):
    even_line = lax.rem(lax.axis_index("line"), 2) == 0
    even_plane = lax.rem(lax.axis_index("plane"), 2) == 0

    def step(v, _):
        base = pl.multiple_of(v * NI * NJ, NI * NJ)
        first, last = pl.ds(base, NJ), pl.ds(base + (NI - 1) * NJ, NJ)
        low = a_ref[first, :] * e_ref[first, :]
        high = a_ref[last, :] * e_ref[last, :]
        ia_ref[v] = jnp.where(even_line, high, low)
        ib_ref[v] = jnp.where(even_line, low, high)
        block = pl.ds(base, NI * NJ)
        for part in range(2):
            lane = pl.ds(part * HALF, HALF)
            scr[...] = a_ref[block, lane] * e_ref[block, lane]
            low, high = scr[pl.ds(0, NI, stride=NJ), :], scr[pl.ds(NJ - 1, NI, stride=NJ), :]
            ja_ref[v, :, lane] = jnp.where(even_plane, high, low)
            jb_ref[v, :, lane] = jnp.where(even_plane, low, high)
        return 0

    lax.fori_loop(0, NV, step, 0)


def line_kernel(
    a_ref, e_ref, f_ref, ia_ref, ib_ref, ja_ref, jb_ref, m_ref, c_ref, s_ref, msg_ref, fore_ref
):
    p = lax.axis_index("line")
    even_line = lax.rem(p, 2) == 0
    even_plane = lax.rem(lax.axis_index("plane"), 2) == 0
    tile = (NJ, NK)
    row, lane = rows_of(tile), lanes_of(tile)
    low_mask = m_ref[0].astype(F32)
    high_mask = m_ref[1].astype(F32)

    def step(v, _):
        base = pl.multiple_of(v * NI * NJ, NI * NJ)
        at = [pl.ds(base + i * NJ, NJ) for i in range(NI)]
        w = [a_ref[at[i], :] * e_ref[at[i], :] for i in range(NI)]
        ia, ib = ia_ref[v], ib_ref[v]
        low = jnp.where(p == 0, low_mask * w[0], jnp.where(even_line, ib, ia))
        high = jnp.where(p == 3, high_mask * w[-1], jnp.where(even_line, ia, ib))
        ja, jb = ja_ref[v], jb_ref[v]
        j_low = jnp.where(even_plane, jb, ja)
        j_high = jnp.where(even_plane, ja, jb)
        lower, ends = [], []
        zero = jnp.zeros(tile, F32)
        one, two = zero, zero
        r_one, r_two = jnp.where(row == 0, 1.0, 0.0), jnp.where(row == 1, 1.0, 0.0)
        for i in range(NI):
            x = w[i]
            before = low if i == 0 else w[i - 1]
            after = high if i == NI - 1 else w[i + 1]
            j_before = jnp.where(row == 0, j_low[i : i + 1], pltpu.roll(x, 1, 0))
            j_after = jnp.where(row == NJ - 1, j_high[i : i + 1], pltpu.roll(x, NJ - 1, 0))
            k_before = jnp.where(lane == 0, 0.0, pltpu.roll(x, 1, 1))
            k_after = jnp.where(lane == NK - 1, 0.0, pltpu.roll(x, NK - 1, 1))
            s = f_ref[at[i], :] + 0.5 * (
                (before - after) + (j_before - j_after) + (k_before - k_after)
            )
            s_ref[at[i], :] = s
            first, second, scale = (c_ref[v, n, i : i + 1, :] for n in range(3))
            one, two = scale * s + first * one + second * two, one
            r_one, r_two = first * r_one + second * r_two, r_one
            lower.append((one, r_one))
        forth = (one, two, jnp.where(row < 2, r_one, pltpu.roll(r_two, 2, 0)))
        one, two = zero, zero
        r_one, r_two = jnp.where(row == 2, 1.0, 0.0), jnp.where(row == 3, 1.0, 0.0)
        for i in reversed(range(NI)):
            first, second, scale = (c_ref[v, n, i : i + 1, :] for n in range(3, 6))
            one, two = scale * lower[i][0] + first * one + second * two, one
            r_one, r_two = scale * lower[i][1] + first * r_one + second * r_two, r_one
        back = (one, two, jnp.where(row < 4, r_one, pltpu.roll(r_two, 4, 0)))
        for n in range(3):
            msg_ref[v, n * 8 : n * 8 + 8, :] = forth[n]
            msg_ref[v, 24 + n * 8 : 32 + n * 8, :] = back[n]
            fore_ref[v, n * 8 : n * 8 + 8, :] = jnp.where(p == 3, back[n], forth[n])
        return 0

    lax.fori_loop(0, NV, step, 0)


def scan_up(x, steps):
    for n, c in zip((1, 2, 4), steps):
        x = x + c * pltpu.roll(x, n, 0)
    return x


def scan_down(x, steps):
    for n, c in zip((1, 2, 4), steps):
        x = x + c * pltpu.roll(x, NJ - n, 0)
    return x


def pick(p, options):
    out = options[-1]
    for n in reversed(range(len(options) - 1)):
        out = jnp.where(p == n, options[n], out)
    return out


def cross_kernel(
    s_ref, c_ref, x_ref, own_ref, one_ref, two_ref, three_ref,
    g_ref, resp_ref, keep_ref, send_ref, f_scr, h_scr,
):
    p = lax.axis_index("line")
    even_plane = lax.rem(lax.axis_index("plane"), 2) == 0
    tile = (NJ, NK)
    row = rows_of(tile)

    def step(v, _):
        base = pl.multiple_of(v * NI * NJ, NI * NJ)

        def part(ref, n):
            return ref[v, n * 8 : n * 8 + 8, :]

        def ups(n):
            own, one, two, three = (part(r, n) for r in (own_ref, one_ref, two_ref, three_ref))
            return (
                pick(p, (own, one, two, three)),
                pick(p, (three, own, one, two)),
                pick(p, (two, three, own, one)),
            )

        def downs(n):
            one = part(one_ref, n)
            two, three = (part(r, n + 3) for r in (two_ref, three_ref))
            return (three, jnp.where(p == 0, two, three), pick(p, (one, two, three)))

        la, lb, lm = ups(0), ups(1), ups(2)
        ua, ub, um = downs(0), downs(1), downs(2)
        low = [(jnp.zeros(tile, F32), jnp.zeros(tile, F32)), (la[0], lb[0])]
        for n in (1, 2):
            x, y = low[n]
            m = lm[n]
            low.append((la[n] + m[0:1] * x + m[1:2] * y, lb[n] + m[2:3] * x + m[3:4] * y))
        zero = jnp.zeros(tile, F32)
        high = [(zero, zero)]
        for n in (3, 2, 1):
            x, y = low[n]
            z, w = high[-1]
            m = um[n - 1]
            a = ua[n - 1] + m[0:1] * x + m[1:2] * y
            b = ub[n - 1] + m[4:5] * x + m[5:6] * y
            if n < 3:
                a = a + m[2:3] * z + m[3:4] * w
                b = b + m[6:7] * z + m[7:8] * w
            high.append((a, b))
        one, two = (pick(p, [low[n][t] for n in range(4)]) for t in range(2))
        lower = []
        for i in range(NI):
            first, second, scale = (c_ref[v, n, i : i + 1, :] for n in range(3))
            s = s_ref[pl.ds(base + i * NJ, NJ), :]
            one, two = scale * s + first * one + second * two, one
            lower.append(one)
        one, two = (pick(p, [high[3 - n][t] for n in range(4)]) for t in range(2))

        fc, fd, bc, bd = (x_ref[v, n] for n in range(4))
        up1 = jnp.where(row == 0, 0.0, fc)
        up2 = up1 * pltpu.roll(up1, 1, 0)
        up = (up1, up2, up2 * pltpu.roll(up2, 2, 0))
        dn1 = jnp.where(row == NJ - 1, 0.0, bc)
        dn2 = dn1 * pltpu.roll(dn1, NJ - 1, 0)
        dn = (dn1, dn2, dn2 * pltpu.roll(dn2, NJ - 2, 0))
        f_resp = scan_up(jnp.where(row == 0, fc, 0.0), up)
        g_resp = scan_down(bd * f_resp, dn)
        b_resp = scan_down(jnp.where(row == NJ - 1, bc, 0.0), dn)
        resp_ref[v, 0] = g_resp
        resp_ref[v, 1] = b_resp

        for i in reversed(range(NI)):
            first, second, scale = (c_ref[v, n, i : i + 1, :] for n in range(3, 6))
            one, two = scale * lower[i] + first * one + second * two, one
            f = scan_up(fd * one, up)
            g = scan_down(bd * f, dn)
            for part in range(2):
                lane = slice(part * HALF, part * HALF + HALF)
                f_scr[part, i * NJ : i * NJ + NJ, :] = f[:, lane]
                h_scr[part, i * NJ : i * NJ + NJ, :] = g[:, lane]
            g_ref[pl.ds(base + i * NJ, NJ), :] = g
        co = jnp.where(
            row == 0,
            f_resp[NJ - 1 : NJ],
            jnp.where(row == 1, b_resp[0:1], jnp.where(row == 2, g_resp[0:1], 0.0)),
        )
        top, bottom = pl.ds(NJ - 1, NI, stride=NJ), pl.ds(0, NI, stride=NJ)
        for at, lo, hi in (
            (pl.ds(0, NI), f_scr[0, top, :], f_scr[1, top, :]),
            (pl.ds(NI, NI), h_scr[0, bottom, :], h_scr[1, bottom, :]),
            (pl.ds(2 * NI, 8), co[:, :HALF], co[:, HALF:]),
        ):
            keep_ref[v, at, :] = jnp.where(even_plane, lo, hi)
            send_ref[v, at, :] = jnp.where(even_plane, hi, lo)
        return 0

    lax.fori_loop(0, NV, step, 0)


def unpack(x):
    n = (x.shape[1] - 8) // 2
    c = x[:, 2 * n :, :]
    return x[:, :n], x[:, n : 2 * n], c[:, 0:1], c[:, 1:2], c[:, 2:3]


def ordered(low_is_own, own, other):
    return (
        [jnp.where(low_is_own, a, b) for a, b in zip(own, other)],
        [jnp.where(low_is_own, b, a) for a, b in zip(own, other)],
    )


def compose(low, high):
    lp, lb, lF, lB, lg = low
    hp, hb, hF, hB, hg = high
    return (
        hF * lp + hp,
        lb + lB * (hb + hg * lp),
        hF * lF,
        lB * hB,
        lg + lB * hg * lF,
    )


def inflow_high(low, f):
    return low[2] * f + low[0]


def inflow_low(low, high, f, u):
    return high[1] + high[4] * inflow_high(low, f) + high[3] * u


def pack_into(ref, agg):
    phi, beta, F, B, g = agg
    n = phi.shape[1]
    row = rows_of((NV, 8, HALF))
    ref[:, :n, :] = phi
    ref[:, n : 2 * n, :] = beta
    ref[:, 2 * n :, :] = jnp.where(
        row == 0, F, jnp.where(row == 1, B, jnp.where(row == 2, g, 0.0))
    )


def place():
    q = lax.axis_index("plane")
    return lax.rem(q, 2), lax.rem(q // 2, 8), q // 16


def bit_clear(z, n):
    return lax.rem(z // n, 2) == 0


def chip_kernel(keep_ref, got_ref, keep_out, send_out):
    core, z, _ = place()
    low, high = ordered(core == 0, unpack(keep_ref[...]), unpack(got_ref[...]))
    phi, beta, F, B, g = compose(low, high)
    even = bit_clear(z, 1)
    first = (phi[:, :8], beta[:, :8])
    second = (phi[:, 8:], beta[:, 8:])
    pack_into(keep_out, [jnp.where(even, a, b) for a, b in zip(first, second)] + [F, B, g])
    pack_into(send_out, [jnp.where(even, b, a) for a, b in zip(first, second)] + [F, B, g])


def pair_kernel(stride, own_ref, got_ref, out_ref):
    _, z, _ = place()
    low, high = ordered(bit_clear(z, stride), unpack(own_ref[...]), unpack(got_ref[...]))
    pack_into(out_ref, compose(low, high))


def ring_kernel(own_ref, got_ref, out_ref, fore_ref):
    _, z, y = place()
    low, high = ordered(bit_clear(z, 4), unpack(own_ref[...]), unpack(got_ref[...]))
    agg = compose(low, high)
    pack_into(out_ref, agg)
    fore_ref[:, :8, :] = jnp.where(y == 3, agg[1], agg[0])
    fore_ref[:, 8:, :] = out_ref[:, 16:, :]


def down_kernel(
    own_ref, one_ref, two_ref, three_ref,
    own4_ref, got4_ref, own2_ref, got2_ref, own1_ref, got1_ref,
    mine_ref, send_ref,
):
    _, z, y = place()
    own, two, three = (unpack(r[...]) for r in (own_ref, two_ref, three_ref))
    x, c = one_ref[:, :8, :], one_ref[:, 8:, :]
    one = (x, x, c[:, 0:1], c[:, 1:2], c[:, 2:3])

    def ups(n):
        o, a, b, c = own[n], one[n], two[n], three[n]
        return (pick(y, (o, a, b, c)), pick(y, (c, o, a, b)), pick(y, (b, c, o, a)))

    def downs(n):
        a, b, c = one[n], two[n], three[n]
        return (c, jnp.where(y == 0, b, c), pick(y, (a, b, c)))

    phi, F = ups(0), ups(2)
    beta, B, g = downs(1), downs(3), downs(4)
    fs = [jnp.zeros_like(phi[0]), phi[0]]
    fs.append(F[1] * fs[1] + phi[1])
    fs.append(F[2] * fs[2] + phi[2])
    us = [None, None, None, jnp.zeros_like(phi[0])]
    us[2] = beta[2] + g[2] * fs[3]
    us[1] = beta[1] + g[1] * fs[2] + B[1] * us[2]
    us[0] = beta[0] + g[0] * fs[1] + B[0] * us[1]
    f, u = pick(y, fs), pick(y, us)
    for stride, mine, got in ((4, own4_ref, got4_ref), (2, own2_ref, got2_ref)):
        is_low = bit_clear(z, stride)
        low, high = ordered(is_low, unpack(mine[...]), unpack(got[...]))
        f, u = (
            jnp.where(is_low, f, inflow_high(low, f)),
            jnp.where(is_low, inflow_low(low, high, f, u), u),
        )
    is_low = bit_clear(z, 1)
    low, high = ordered(is_low, unpack(own1_ref[...]), unpack(got1_ref[...]))
    f_high, u_low = inflow_high(low, f), inflow_low(low, high, f, u)
    mine_ref[:, :8, :] = jnp.where(is_low, f, f_high)
    mine_ref[:, 8:, :] = jnp.where(is_low, u_low, u)
    send_ref[:, :8, :] = jnp.where(is_low, f_high, f)
    send_ref[:, 8:, :] = jnp.where(is_low, u, u_low)


def split_kernel(mine_ref, got_ref, keep_ref, gotc_ref, own_out, send_out):
    core, z, _ = place()
    even = bit_clear(z, 1)
    first = jnp.where(even, mine_ref[...], got_ref[...])
    second = jnp.where(even, got_ref[...], mine_ref[...])
    f = jnp.concatenate([first[:, :8], second[:, :8]], axis=1)
    u = jnp.concatenate([first[:, 8:], second[:, 8:]], axis=1)
    is_low = core == 0
    low, high = ordered(is_low, unpack(keep_ref[...]), unpack(gotc_ref[...]))
    f_high, u_low = inflow_high(low, f), inflow_low(low, high, f, u)
    own_out[:, :NI, :] = jnp.where(is_low, f, f_high)
    own_out[:, NI:, :] = jnp.where(is_low, u_low, u)
    send_out[:, :NI, :] = jnp.where(is_low, f_high, f)
    send_out[:, NI:, :] = jnp.where(is_low, u, u_low)


def final_kernel(g_ref, resp_ref, own_ref, got_ref, out_ref, scr, fu_scr, sems):
    even = place()[0] == 0
    fu_scr[:, :, :HALF] = jnp.where(even, own_ref[...], got_ref[...])
    fu_scr[:, :, HALF:] = jnp.where(even, got_ref[...], own_ref[...])
    size = NI * NJ

    def copy(v):
        at = pl.ds(pl.multiple_of(v * size, size), size)
        return pltpu.make_async_copy(scr.at[at], out_ref.at[at], sems.at[v])

    for v in range(NV):
        a, b = resp_ref[v, 0], resp_ref[v, 1]
        for i in range(NI):
            at = pl.ds(v * size + i * NJ, NJ)
            f, u = fu_scr[v, i : i + 1, :], fu_scr[v, NI + i : NI + i + 1, :]
            scr[at, :] = g_ref[at, :] + a * f + b * u
        copy(v).start()
    for v in range(NV):
        copy(v).wait()


def swap(x, axis, size, flip):
    return lax.ppermute(x, axis, [(i, i ^ flip) for i in range(size)])


def shift(x, axis, size, by):
    return lax.ppermute(x, axis, [(i, (i + by) % size) for i in range(size)])


def body(adjoint, forcing, eigen_values, face_masks, line_coeffs, cross_coeffs):
    flat = (NV * NI * NJ, NK)
    a, f, e = (x.reshape(flat) for x in (adjoint, forcing, eigen_values))
    i_face, j_face = (NV, NJ, NK), (NV, NI, NK)
    ia, ib, ja, jb = call(
        faces_kernel, [i_face, i_face, j_face, j_face], a, e,
        scratch=[pltpu.VMEM((NI * NJ, HALF), F32)], name="faces",
    )
    jb = lax.ppermute(
        jb, "plane", [(i, i + 1 if i % 2 else i - 1) for i in range(1, 63)]
    )
    ia = swap(ia, "line", 4, 1)
    ib = lax.ppermute(ib, "line", [(1, 2), (2, 1)])
    ja = swap(ja, "plane", 64, 1)
    s, msg, fore = call(
        line_kernel, [flat, (NV, 48, NK), (NV, 24, NK)],
        a, e, f, ia, ib, ja, jb, face_masks, line_coeffs, name="line",
    )
    two = shift(msg, "line", 4, 2)
    one = shift(fore, "line", 4, 1)
    three = shift(msg, "line", 4, 3)
    g, resp, keep, send = call(
        cross_kernel, [flat, (NV, 2, NJ, NK), (NV, 40, HALF), (NV, 40, HALF)],
        s, line_coeffs, cross_coeffs, msg, one, two, three,
        scratch=[pltpu.VMEM((2, NI * NJ, HALF), F32)] * 2, name="cross",
    )
    got = swap(send, "plane", 64, 1)
    z_shape = (NV, 24, HALF)
    own1, send1 = call(chip_kernel, [z_shape, z_shape], keep, got, name="chip")
    got1 = swap(send1, "plane", 64, 2)
    own2 = call(lambda *r: pair_kernel(1, *r), [z_shape], own1, got1, name="pair1")[0]
    got2 = swap(own2, "plane", 64, 4)
    own4 = call(lambda *r: pair_kernel(2, *r), [z_shape], own2, got2, name="pair2")[0]
    got4 = swap(own4, "plane", 64, 8)
    ring, fore = call(ring_kernel, [z_shape, (NV, 16, HALF)], own4, got4, name="ring")
    two = shift(ring, "plane", 64, 32)
    one = shift(fore, "plane", 64, 16)
    three = shift(ring, "plane", 64, 48)
    back = (NV, 16, HALF)
    mine, send = call(
        down_kernel, [back, back],
        ring, one, two, three, own4, got4, own2, got2, own1, got1, name="down",
    )
    other = swap(send, "plane", 64, 2)
    fu = (NV, 2 * NI, HALF)
    own, send = call(split_kernel, [fu, fu], mine, other, keep, got, name="split")
    other = swap(send, "plane", 64, 1)
    out = call(
        final_kernel, [flat], g, resp, own, other, any_out=True, name="final",
        scratch=[
            pltpu.VMEM(flat, F32),
            pltpu.VMEM((NV, 2 * NI, NK), F32),
            pltpu.SemaphoreType.DMA((NV,)),
        ],
    )[0]
    return out.reshape(NV, NI, NJ, NK)


def solution(mesh):
    return jax.shard_map(
        body,
        mesh=mesh,
        in_specs=(
            P(None, "line", "plane", None),
            P(None, "line", "plane", None),
            P(None, "line", "plane", None),
            P(None, "plane", None),
            P(None, None, "line", None),
            P(None, None, "plane", None),
        ),
        out_specs=P(None, "line", "plane", None),
        check_vma=False,
    )
```

```python
import jax
import jax.numpy as jnp
from jax import lax
from jax.experimental import pallas as pl
from jax.experimental.pallas import tpu as pltpu
from jax.sharding import PartitionSpec as P

F32 = jnp.float32
NV, NI, NJ, NK = 5, 16, 8, 256
HALF = NK // 2
PLANE = NI * NJ
TILE = (NJ, NK)
MAPS = NV * 8


def rows_of(shape):
    return lax.broadcasted_iota(jnp.int32, shape, len(shape) - 2)


def lanes_of(shape):
    return lax.broadcasted_iota(jnp.int32, shape, len(shape) - 1)


def call(kernel, outs, *args, scratch=(), in_hbm=0, out_hbm=False, name=None, flops=1000):
    outs = [jax.ShapeDtypeStruct(s, F32) for s in outs]
    args = [
        pltpu.with_memory_space_constraint(x, pltpu.HBM) if n < in_hbm else x
        for n, x in enumerate(args)
    ]
    spaces = [pltpu.HBM] * in_hbm + [pltpu.VMEM] * (len(args) - in_hbm)
    return pl.pallas_call(
        kernel,
        out_shape=outs,
        in_specs=[pl.BlockSpec(memory_space=s) for s in spaces],
        out_specs=[pl.BlockSpec(memory_space=pltpu.HBM if out_hbm else pltpu.VMEM)] * len(outs),
        scratch_shapes=list(scratch),
        compiler_params=pltpu.CompilerParams(vmem_limit_bytes=40 * 1024 * 1024),
        cost_estimate=pl.CostEstimate(flops=flops, bytes_accessed=flops, transcendentals=0),
        name=name,
    )(*args)


def place():
    q = lax.axis_index("plane")
    return lax.rem(q, 2), lax.rem(q // 2, 8), q // 16


def pick(p, options):
    out = options[-1]
    for n in reversed(range(len(options) - 1)):
        out = jnp.where(p == n, options[n], out)
    return out


def faces_kernel(
    a_hbm, e_hbm, w_ref, ia_ref, ib_ref, ja_ref, jb_ref, a_scr, e_scr, scr, sems
):
    even_line = lax.rem(lax.axis_index("line"), 2) == 0
    even_plane = lax.rem(lax.axis_index("plane"), 2) == 0

    def fetch(v, n):
        src, dst = ((a_hbm, a_scr), (e_hbm, e_scr))[n]
        at = pl.ds(v * PLANE, PLANE)
        return pltpu.make_async_copy(src.at[at], dst.at[at], sems.at[v, n])

    for v in range(NV):
        for n in range(2):
            fetch(v, n).start()
    for v in range(NV):
        for n in range(2):
            fetch(v, n).wait()
        base = v * PLANE
        for part in range(2):
            lane = slice(part * HALF, part * HALF + HALF)
            w = a_scr[base : base + PLANE, lane] * e_scr[base : base + PLANE, lane]
            w_ref[base : base + PLANE, lane] = w
            scr[v, part] = w
            low, high = w[:NJ], w[PLANE - NJ :]
            ia_ref[v, :, lane] = jnp.where(even_line, high, low)
            ib_ref[v, :, lane] = jnp.where(even_line, low, high)
            low = scr[v, part, pl.ds(0, NI, stride=NJ), :]
            high = scr[v, part, pl.ds(NJ - 1, NI, stride=NJ), :]
            ja_ref[v, :, lane] = jnp.where(even_plane, high, low)
            jb_ref[v, :, lane] = jnp.where(even_plane, low, high)


def prep_kernel(
    f_hbm, c_hbm, x_hbm, m_hbm, w_ref,
    c_ref, line_resp_ref, maps_ref, cross_resp_ref, halo_resp_ref, co_ref, g_ref, t_ref, x_ref,
    f_ref, m_ref, sems,
):
    pairs = ((c_hbm, c_ref), (x_hbm, x_ref), (m_hbm, m_ref), (f_hbm, f_ref))
    copies = [pltpu.make_async_copy(a, b, sems.at[n]) for n, (a, b) in enumerate(pairs)]
    for copy in copies:
        copy.start()
    copies[0].wait()
    line_coeffs_of(c_ref, line_resp_ref, maps_ref)
    copies[1].wait()
    cross_coeffs_of(x_ref, cross_resp_ref, halo_resp_ref, co_ref)
    copies[2].wait()
    copies[3].wait()
    local_source(w_ref, f_ref, m_ref, x_ref, g_ref, t_ref)


def line_coeffs_of(c_ref, resp_ref, msg_ref):
    row = rows_of(TILE)
    unit = [jnp.where(row == n, 1.0, 0.0) for n in range(4)]
    one, two = [unit[0]] * NV, [unit[1]] * NV
    lower = [[None] * NI for _ in range(NV)]
    for i in range(NI):
        for v in range(NV):
            first, second = (c_ref[v, n, i : i + 1, :] for n in range(2))
            one[v], two[v] = first * one[v] + second * two[v], one[v]
            lower[v][i] = one[v]
    for v in range(NV):
        msg_ref[v * 12 : v * 12 + 2, :] = one[v][0:2]
        msg_ref[v * 12 + 2 : v * 12 + 4, :] = two[v][0:2]
    one, two = [unit[2]] * NV, [unit[3]] * NV
    for i in reversed(range(NI)):
        for v in range(NV):
            first, second, scale = (c_ref[v, n, i : i + 1, :] for n in range(3, 6))
            one[v], two[v] = scale * lower[v][i] + first * one[v] + second * two[v], one[v]
            at = v * PLANE + i * NJ
            for part in range(2):
                resp_ref[part, at : at + NJ, :] = one[v][:, part * HALF : part * HALF + HALF]
    for v in range(NV):
        msg_ref[v * 12 + 4 : v * 12 + 8, :] = one[v][0:4]
        msg_ref[v * 12 + 8 : v * 12 + 12, :] = two[v][0:4]
    msg_ref[60:, :] = jnp.zeros((4, NK), F32)


def up_steps(c):
    row = rows_of(TILE)
    one = jnp.where(row == 0, 0.0, c)
    two = one * pltpu.roll(one, 1, 0)
    return (one, two, two * pltpu.roll(two, 2, 0))


def down_steps(c):
    row = rows_of(TILE)
    one = jnp.where(row == NJ - 1, 0.0, c)
    two = one * pltpu.roll(one, NJ - 1, 0)
    return (one, two, two * pltpu.roll(two, NJ - 2, 0))


def scan_up(x, steps):
    for n, c in zip((1, 2, 4), steps):
        x = x + c * pltpu.roll(x, n, 0)
    return x


def scan_down(x, steps):
    for n, c in zip((1, 2, 4), steps):
        x = x + c * pltpu.roll(x, NJ - n, 0)
    return x


def cross_coeffs_of(x_ref, resp_ref, halo_ref, co_ref):
    row = rows_of(TILE)
    co_ref[15:, :] = jnp.zeros((1, NK), F32)
    for v in range(NV):
        fc, fd, bc, bd = (x_ref[v, n] for n in range(4))
        up, dn = up_steps(fc), down_steps(bc)
        f_resp = scan_up(jnp.where(row == 0, fc, 0.0), up)
        g_resp = scan_down(bd * f_resp, dn)
        b_resp = scan_down(jnp.where(row == NJ - 1, bc, 0.0), dn)
        resp_ref[v, 0] = g_resp
        resp_ref[v, 1] = b_resp
        for n, at, half in ((0, 0, 0.5), (1, NJ - 1, -0.5)):
            f = scan_up(jnp.where(row == at, half * fd, 0.0), up)
            g = scan_down(bd * f, dn)
            halo_ref[v, n] = g
            halo_ref[v, n + 2] = edge_rows(f, g)
        co_ref[v : v + 1, :] = f_resp[NJ - 1 : NJ]
        co_ref[NV + v : NV + v + 1, :] = b_resp[0:1]
        co_ref[2 * NV + v : 2 * NV + v + 1, :] = g_resp[0:1]


def edge_rows(f, g):
    row = rows_of(TILE)
    return jnp.where(row == 0, pltpu.roll(f, 1, 0), pltpu.roll(g, 1, 0))


def local_source(w_ref, f_ref, m_ref, x_ref, g_ref, t_ref):
    p = lax.axis_index("line")
    row, lane = rows_of(TILE), lanes_of(TILE)
    zero = jnp.zeros(TILE, F32)
    low_mask = jnp.where(p == 0, m_ref[0].astype(F32), zero)
    high_mask = jnp.where(p == 3, m_ref[1].astype(F32), zero)

    def step(v, _):
        base = pl.multiple_of(v * PLANE, PLANE)
        at = [pl.ds(base + i * NJ, NJ) for i in range(NI)]
        w = [w_ref[at[i], :] for i in range(NI)]
        fd, bd = x_ref[v, 1], x_ref[v, 3]
        up, dn = up_steps(x_ref[v, 0]), down_steps(x_ref[v, 2])
        for i in range(NI):
            x = w[i]
            before = low_mask * x if i == 0 else w[i - 1]
            after = high_mask * x if i == NI - 1 else w[i + 1]
            j_before = jnp.where(row == 0, 0.0, pltpu.roll(x, 1, 0))
            j_after = jnp.where(row == NJ - 1, 0.0, pltpu.roll(x, NJ - 1, 0))
            k_before = jnp.where(lane == 0, 0.0, pltpu.roll(x, 1, 1))
            k_after = jnp.where(lane == NK - 1, 0.0, pltpu.roll(x, NK - 1, 1))
            s = f_ref[at[i], :] + 0.5 * (
                (before - after) + (j_before - j_after) + (k_before - k_after)
            )
            f = scan_up(fd * s, up)
            g = scan_down(bd * f, dn)
            g_ref[at[i], :] = g
            t_ref[at[i], :] = edge_rows(f, g)
        return 0

    lax.fori_loop(0, NV, step, 0)


def source_kernel(
    g_in, t_in, ia_ref, ib_ref, ja_ref, jb_ref, c_ref, x_ref, halo_ref, maps_ref,
    low_ref, high_ref, gi_ref, edge_ref, msg_ref, t_scr,
):
    p, q = lax.axis_index("line"), lax.axis_index("plane")
    even_line, even_plane = lax.rem(p, 2) == 0, lax.rem(q, 2) == 0
    for v in range(NV):
        ia, ib = ia_ref[v], ib_ref[v]
        low = jnp.where(p == 0, 0.0, jnp.where(even_line, ib, ia))
        high = jnp.where(p == 3, 0.0, jnp.where(even_line, ia, ib))
        ja, jb = ja_ref[v], jb_ref[v]
        j_low = jnp.where(q == 0, 0.0, jnp.where(even_plane, jb, ja))
        j_high = jnp.where(q == 63, 0.0, jnp.where(even_plane, ja, jb))
        low_ref[v] = j_low
        high_ref[v] = j_high
        fd, bd = x_ref[v, 1], x_ref[v, 3]
        up, dn = up_steps(x_ref[v, 0]), down_steps(x_ref[v, 2])
        ends = []
        for n, face in enumerate((0.5 * low, -0.5 * high)):
            f = scan_up(fd * face, up)
            g = scan_down(bd * f, dn)
            gi_ref[v, n] = g
            ends.append(edge_rows(f, g))
        a, b = halo_ref[v, 2], halo_ref[v, 3]
        for i in range(NI):
            at = slice(v * PLANE + i * NJ, v * PLANE + i * NJ + NJ)
            t = t_in[at, :] + a * j_low[i : i + 1] + b * j_high[i : i + 1]
            if i == 0:
                t = t + ends[0]
            if i == NI - 1:
                t = t + ends[1]
            t_scr[at, :] = t
    local_sweeps(c_ref, t_scr, t_scr, edge_ref, msg_ref, small=True)
    msg_ref[MAPS:, :] = maps_ref[...]


def local_sweeps(c_ref, src_ref, tmp_ref, out_ref, msg_ref, small):
    row = rows_of(TILE)
    zero = jnp.zeros(TILE, F32)
    one, two = [zero] * NV, [zero] * NV
    for i in range(NI):
        for v in range(NV):
            first, second, scale = (c_ref[v, n, i : i + 1, :] for n in range(3))
            at = slice(v * PLANE + i * NJ, v * PLANE + i * NJ + NJ)
            one[v], two[v] = scale * src_ref[at, :] + first * one[v] + second * two[v], one[v]
            tmp_ref[at, :] = one[v]
    ends = list(zip(one, two))
    one, two = [zero] * NV, [zero] * NV
    for i in reversed(range(NI)):
        for v in range(NV):
            first, second, scale = (c_ref[v, n, i : i + 1, :] for n in range(3, 6))
            at = slice(v * PLANE + i * NJ, v * PLANE + i * NJ + NJ)
            one[v], two[v] = scale * tmp_ref[at, :] + first * one[v] + second * two[v], one[v]
            if small:
                for part in range(2):
                    out_ref[part, at, :] = one[v][:, part * HALF : part * HALF + HALF]
            else:
                out_ref[at, :] = one[v]
    for v in range(NV):
        if small:
            a, b, c, d = ends[v][0], ends[v][1], one[v], two[v]
            msg_ref[v * 8 : v * 8 + 8, :] = jnp.where(
                row < 2,
                a,
                jnp.where(
                    row < 4,
                    pltpu.roll(b, 2, 0),
                    jnp.where(row < 6, pltpu.roll(c, 4, 0), pltpu.roll(d, 6, 0)),
                ),
            )
        else:
            for n, x in enumerate((ends[v][0], ends[v][1], one[v], two[v])):
                msg_ref[v, n * NJ : n * NJ + NJ, :] = x


def planes_kernel(c_ref, g_ref, halo_ref, low_ref, high_ref, gi_ref, out_ref, msg_ref, g_scr):
    for v in range(NV):
        a, b = halo_ref[v, 0], halo_ref[v, 1]
        for i in range(NI):
            at = slice(v * PLANE + i * NJ, v * PLANE + i * NJ + NJ)
            g = g_ref[at, :] + a * low_ref[v, i : i + 1, :] + b * high_ref[v, i : i + 1, :]
            if i == 0:
                g = g + gi_ref[v, 0]
            if i == NI - 1:
                g = g + gi_ref[v, 1]
            g_scr[at, :] = g
    local_sweeps(c_ref, g_scr, out_ref, out_ref, msg_ref, small=False)


def maps_of(ref, v):
    return ref[MAPS + v * 12 : MAPS + v * 12 + 12, :]


def line_pair(p, own, got):
    is_low = lax.rem(p, 2) == 0
    return (
        [jnp.where(is_low, a, b) for a, b in zip(own, got)],
        [jnp.where(is_low, b, a) for a, b in zip(own, got)],
    )


def l_after(m, phi, l):
    return (
        m[0:1] * l[0] + m[1:2] * l[1] + phi[0],
        m[2:3] * l[0] + m[3:4] * l[1] + phi[1],
    )


def u_before(m, beta, l, u):
    return (
        m[4:5] * l[0] + m[5:6] * l[1] + m[6:7] * u[0] + m[7:8] * u[1] + beta[0],
        m[8:9] * l[0] + m[9:10] * l[1] + m[10:11] * u[0] + m[11:12] * u[1] + beta[1],
    )


def pair_states(p, low, high):
    lm, la, lb, lc, ld = low
    hm, ha, hb, hc, hd = high
    phi = l_after(hm, (ha, hb), (la, lb))
    zero = jnp.zeros_like(la)
    beta = u_before(lm, (lc, ld), (zero, zero), u_before(hm, (hc, hd), (la, lb), (zero, zero)))
    upper = p >= 2
    return [jnp.where(upper, a, b) for a, b in zip(beta, phi)]


def pair_gamma(low_m, high_m):
    columns = []
    for c in range(2):
        l = (low_m[c : c + 1], low_m[2 + c : 3 + c])
        a = high_m[4:5] * l[0] + high_m[5:6] * l[1]
        b = high_m[8:9] * l[0] + high_m[9:10] * l[1]
        columns.append(
            (
                low_m[4 + c : 5 + c] + low_m[6:7] * a + low_m[7:8] * b,
                low_m[8 + c : 9 + c] + low_m[10:11] * a + low_m[11:12] * b,
            )
        )
    (raa, rba), (rab, rbb) = columns
    return raa, rab, rba, rbb


def entering(p, low, high, mine, got, gamma):
    upper, is_low = p >= 2, lax.rem(p, 2) == 0
    zero = jnp.zeros_like(mine[0])
    l = [jnp.where(upper, x, zero) for x in got]
    raa, rab, rba, rbb = gamma
    u = (
        got[0] + raa * mine[0] + rab * mine[1],
        got[1] + rba * mine[0] + rbb * mine[1],
    )
    u = [jnp.where(upper, zero, x) for x in u]
    l_high = l_after(low[0], low[1:3], l)
    u_low = u_before(high[0], high[3:5], l_high, u)
    return [jnp.where(is_low, a, b) for a, b in zip(l, l_high)] + [
        jnp.where(is_low, a, b) for a, b in zip(u_low, u)
    ]


def edges_kernel(
    edge_ref, resp_ref, co_ref, own_ref, got1_ref, got2_ref, got3_ref,
    keep_ref, send_ref, gamma_ref,
):
    p = lax.axis_index("line")
    even = place()[0] == 0
    refs = (own_ref, got1_ref, got2_ref, got3_ref)

    def put(at, x, y):
        keep_ref[at, :] = jnp.where(even, x, y)
        send_ref[at, :] = jnp.where(even, y, x)

    for v in range(NV):
        rows, maps = [], []
        for r in range(4):
            rows.append(pick(p, [refs[r ^ own][v * 8 : v * 8 + 8, :] for own in range(4)]))
            maps.append(pick(p, [maps_of(refs[r ^ own], v) for own in range(4)]))
        part = [[x[n * 2 : n * 2 + 2] for n in range(4)] for x in rows]
        zero = jnp.zeros((2, NK), F32)
        low = [(zero, zero), (part[0][0], part[0][1])]
        for r in (1, 2):
            low.append(l_after(maps[r], part[r][:2], low[r]))
        high = [None, None, None, (zero, zero)]
        for r in (3, 2, 1):
            high[r - 1] = u_before(maps[r], part[r][2:], low[r], high[r])
        states = [pick(p, [x[t] for x in low]) for t in range(2)]
        states += [pick(p, [x[t] for x in high]) for t in range(2)]
        for t in range(2):
            parts = []
            for half in range(2):
                lane = slice(half * HALF, half * HALF + HALF)
                x = edge_ref[half, pl.ds(v * PLANE + t, NI, stride=NJ), :]
                for n in range(4):
                    r = resp_ref[half, pl.ds(v * PLANE + n, NI, stride=NJ), :]
                    x = x + r * states[n][t : t + 1, lane]
                parts.append(x)
            put(slice(v * 32 + t * 16, v * 32 + t * 16 + 16), *parts)
        for n, x in enumerate(pair_gamma(maps[2], maps[3])):
            gamma_ref[v * 4 + n : v * 4 + n + 1, :] = x
    put(slice(160, 176), co_ref[:, :HALF], co_ref[:, HALF:])
    gamma_ref[20:24, :] = jnp.zeros((4, NK), F32)


def last_gamma(ref, v):
    return [ref[v * 4 + n : v * 4 + n + 1, :] for n in range(4)]


def big_parts(ref, maps_ref, v):
    return [maps_of(maps_ref, v)] + [ref[v, n * NJ : n * NJ + NJ, :] for n in range(4)]


def plane_pair_kernel(own_ref, got_ref, own_maps, got_maps, out_ref):
    p = lax.axis_index("line")
    for v in range(NV):
        low, high = line_pair(p, big_parts(own_ref, own_maps, v), big_parts(got_ref, got_maps, v))
        a, b = pair_states(p, low, high)
        out_ref[v, :NJ, :] = a
        out_ref[v, NJ:, :] = b


def solved_kernel(
    local_ref, resp_ref, own_ref, got_ref, own_maps, got_maps, mine2_ref, got2_ref, last_ref, out_ref
):
    p = lax.axis_index("line")
    for v in range(NV):
        low, high = line_pair(p, big_parts(own_ref, own_maps, v), big_parts(got_ref, got_maps, v))
        mine = (mine2_ref[v, :NJ, :], mine2_ref[v, NJ:, :])
        got = (got2_ref[v, :NJ, :], got2_ref[v, NJ:, :])
        states = entering(p, low, high, mine, got, last_gamma(last_ref, v))
        for i in range(NI):
            at = v * PLANE + i * NJ
            for part in range(2):
                lane = slice(part * HALF, part * HALF + HALF)
                x = local_ref[at : at + NJ, lane]
                for n in range(4):
                    x = x + resp_ref[part, at + n : at + n + 1, :] * states[n][:, lane]
                out_ref[at : at + NJ, lane] = x


def load(ref):
    phi = [ref[v * 32 : v * 32 + NI, :] for v in range(NV)]
    beta = [ref[v * 32 + NI : v * 32 + 2 * NI, :] for v in range(NV)]
    return (phi, beta, ref[160:165, :], ref[165:170, :], ref[170:175, :])


def store(ref, agg):
    phi, beta, F, B, g = agg
    for v in range(NV):
        ref[v * 32 : v * 32 + NI, :] = phi[v]
        ref[v * 32 + NI : v * 32 + 2 * NI, :] = beta[v]
    ref[160:165, :] = F
    ref[165:170, :] = B
    ref[170:175, :] = g
    ref[175:176, :] = jnp.zeros((1, HALF), F32)


def choose(low_is_own, own, other):
    return jax.tree.map(lambda a, b: jnp.where(low_is_own, a, b), own, other)


def ordered(low_is_own, own, other):
    return choose(low_is_own, own, other), choose(low_is_own, other, own)


def compose(low, high):
    lp, lb, lF, lB, lg = low
    hp, hb, hF, hB, hg = high
    at = [slice(v, v + 1) for v in range(NV)]
    return (
        [hF[at[v]] * lp[v] + hp[v] for v in range(NV)],
        [lb[v] + lB[at[v]] * (hb[v] + hg[at[v]] * lp[v]) for v in range(NV)],
        hF * lF,
        lB * hB,
        lg + lB * hg * lF,
    )


def f_after(agg, f):
    return [agg[2][v : v + 1] * f[v] + agg[0][v] for v in range(NV)]


def g_before(agg, f, u):
    return [agg[1][v] + agg[4][v : v + 1] * f[v] + agg[3][v : v + 1] * u[v] for v in range(NV)]


def bit_clear(z, n):
    return lax.rem(z // n, 2) == 0


def chip_kernel(keep_ref, got_ref, out_ref):
    store(out_ref, compose(*ordered(place()[0] == 0, load(keep_ref), load(got_ref))))


def members(refs):
    m = lax.rem(place()[1], 4)
    parts = [load(r) for r in refs]
    return [
        jax.tree.map(lambda *x: pick(m, x), *(parts[r ^ own] for own in range(4)))
        for r in range(4)
    ]


def quad_kernel(*refs):
    a, b, c, d = members(refs[:4])
    store(refs[4], compose(compose(a, b), compose(c, d)))


def ring_kernel(own_ref, got_ref, out_ref):
    store(out_ref, compose(*ordered(bit_clear(place()[1], 4), load(own_ref), load(got_ref))))


def top_kernel(own_ref, got_ref, out_ref):
    y = place()[2]
    agg = compose(*ordered(bit_clear(y, 1), load(own_ref), load(got_ref)))
    for v in range(NV):
        out_ref[v * NI : v * NI + NI, :] = jnp.where(y >= 2, agg[1][v], agg[0][v])
    out_ref[80:85, :] = agg[4]
    out_ref[85:88, :] = jnp.zeros((3, HALF), F32)


def step_down(is_low, low, high, f, u):
    f_high = f_after(low, f)
    u_low = g_before(high, f_high, u)
    return (f, u_low), (f_high, u)


def put_states(ref, states):
    for v in range(NV):
        ref[v * 32 : v * 32 + NI, :] = states[0][v]
        ref[v * 32 + NI : v * 32 + 2 * NI, :] = states[1][v]


def down_kernel(
    mine_ref, got_ref, own8_ref, got8_ref, own4_ref, got4_ref,
    q0_ref, q1_ref, q2_ref, q3_ref, own1_ref, got1_ref, keep_ref, send_ref,
):
    core, z, y = place()
    upper = y >= 2
    zero = jnp.zeros((NI, HALF), F32)
    at = [slice(v * NI, v * NI + NI) for v in range(NV)]
    f = [jnp.where(upper, got_ref[x, :], zero) for x in at]
    u = [
        jnp.where(upper, zero, got_ref[x, :] + got_ref[80 + v : 81 + v, :] * mine_ref[x, :])
        for v, x in enumerate(at)
    ]
    for is_low, mine, got in (
        (bit_clear(y, 1), own8_ref, got8_ref),
        (bit_clear(z, 4), own4_ref, got4_ref),
    ):
        low, high = ordered(is_low, load(mine), load(got))
        f, u = choose(is_low, *step_down(is_low, low, high, f, u))
    parts = members((q0_ref, q1_ref, q2_ref, q3_ref))
    fs, us = [f], [None, None, None, u]
    for r in range(3):
        fs.append(f_after(parts[r], fs[r]))
    for r in (3, 2, 1):
        us[r - 1] = g_before(parts[r], fs[r], us[r])
    m = lax.rem(z, 4)
    f = [pick(m, [x[v] for x in fs]) for v in range(NV)]
    u = [pick(m, [x[v] for x in us]) for v in range(NV)]
    is_low = core == 0
    low, high = ordered(is_low, load(own1_ref), load(got1_ref))
    low, high = step_down(is_low, low, high, f, u)
    put_states(keep_ref, choose(is_low, low, high))
    put_states(send_ref, choose(is_low, high, low))


def final_kernel(g_ref, resp_ref, mine_ref, other_ref, out_ref, scr, fu_scr, sems):
    even = place()[0] == 0

    def copy(v):
        at = pl.ds(v * PLANE, PLANE)
        return pltpu.make_async_copy(scr.at[at], out_ref.at[at], sems.at[v])

    for v in range(NV):
        x, y = mine_ref[v * 32 : v * 32 + 32, :], other_ref[v * 32 : v * 32 + 32, :]
        fu_scr[v, :, :HALF] = jnp.where(even, x, y)
        fu_scr[v, :, HALF:] = jnp.where(even, y, x)
        a, b = resp_ref[v, 0], resp_ref[v, 1]
        for i in range(NI):
            at = slice(v * PLANE + i * NJ, v * PLANE + i * NJ + NJ)
            f, u = fu_scr[v, i : i + 1, :], fu_scr[v, NI + i : NI + i + 1, :]
            scr[at, :] = g_ref[at, :] + a * f + b * u
        copy(v).start()
    for v in range(NV):
        copy(v).wait()


def swap(x, axis, size, flip):
    return lax.ppermute(x, axis, [(i, i ^ flip) for i in range(size)])


def across(x):
    pairs = []
    for q in range(64):
        z = q // 2 % 8
        other = (6 - z if z % 2 == 0 else 8 - z) % 8
        pairs.append((q, q + 2 * (other - z)))
    return lax.ppermute(x, "plane", pairs)


def body(adjoint, forcing, eigen_values, face_masks, line_coeffs, cross_coeffs):
    flat = (NV * PLANE, NK)
    a, f, e = (x.reshape(flat) for x in (adjoint, forcing, eigen_values))
    i_face, j_face = (NV, NJ, NK), (NV, NI, NK)
    w, ia, ib, ja, jb = call(
        faces_kernel, [flat, i_face, i_face, j_face, j_face], a, e, in_hbm=2, name="faces",
        scratch=[
            pltpu.VMEM(flat, F32),
            pltpu.VMEM(flat, F32),
            pltpu.VMEM((NV, 2, PLANE, HALF), F32),
            pltpu.SemaphoreType.DMA((NV, 2)),
        ],
    )
    ia = swap(ia, "line", 4, 1)
    ib = swap(ib, "line", 4, 3)
    ja = swap(ja, "plane", 64, 1)
    jb = lax.ppermute(jb, "plane", [(i, (i + 1 if i % 2 else i - 1) % 64) for i in range(64)])

    halves = (2, NV * PLANE, HALF)
    c, line_resp, maps, cross_resp, halo_resp, co, g, t, x = call(
        prep_kernel,
        [
            line_coeffs.shape, halves, (64, NK), (NV, 2, NJ, NK), (NV, 4, NJ, NK), (16, NK),
            flat, flat, cross_coeffs.shape,
        ],
        f, line_coeffs, cross_coeffs, face_masks, w, in_hbm=4, name="prep", flops=10**7,
        scratch=[
            pltpu.VMEM(flat, F32),
            pltpu.VMEM(face_masks.shape, face_masks.dtype),
            pltpu.SemaphoreType.DMA((4,)),
        ],
    )
    j_low, j_high, gi, edge, small = call(
        source_kernel, [j_face, j_face, (NV, 2, NJ, NK), halves, (MAPS + 64, NK)],
        g, t, ia, ib, ja, jb, c, x, halo_resp, maps,
        scratch=[pltpu.VMEM(flat, F32)], name="source",
    )
    smalls = [small] + [swap(small, "line", 4, d) for d in (1, 2, 3)]

    local, big = call(
        planes_kernel, [flat, (NV, 32, NK)], c, g, halo_resp, j_low, j_high, gi,
        scratch=[pltpu.VMEM(flat, F32)], name="planes", flops=10**7,
    )
    got_big = swap(big, "line", 4, 1)
    last_big = call(
        plane_pair_kernel, [(NV, 16, NK)], big, got_big, small, smalls[1], name="plane_pair"
    )[0]
    got_last_big = swap(last_big, "line", 4, 3)

    msg = (176, HALF)
    keep, send, gamma = call(
        edges_kernel, [msg, msg, (24, NK)], edge, line_resp, co, *smalls, name="edges"
    )
    solved = call(
        solved_kernel, [flat],
        local, line_resp, big, got_big, small, smalls[1], last_big, got_last_big, gamma,
        name="solved", flops=10**7,
    )[0]
    got = swap(send, "plane", 64, 1)
    own1 = call(chip_kernel, [msg], keep, got, name="chip")[0]
    quad = [own1] + [swap(own1, "plane", 64, d) for d in (2, 4, 6)]
    own4 = call(quad_kernel, [msg], *quad, name="quad")[0]
    got4 = across(own4)
    own8 = call(ring_kernel, [msg], own4, got4, name="ring")[0]
    got8 = swap(own8, "plane", 64, 16)
    top = call(top_kernel, [(88, HALF)], own8, got8, name="top")[0]
    got_top = swap(top, "plane", 64, 48)
    mine, send = call(
        down_kernel, [(160, HALF)] * 2,
        top, got_top, own8, got8, own4, got4, *quad, keep, got, name="down",
    )
    other = swap(send, "plane", 64, 1)
    out = call(
        final_kernel, [flat], solved, cross_resp, mine, other, out_hbm=True, name="final",
        scratch=[
            pltpu.VMEM(flat, F32),
            pltpu.VMEM((NV, 2 * NI, NK), F32),
            pltpu.SemaphoreType.DMA((NV,)),
        ],
    )[0]
    return out.reshape(NV, NI, NJ, NK)


def solution(mesh):
    return jax.shard_map(
        body,
        mesh=mesh,
        in_specs=(
            P(None, "line", "plane", None),
            P(None, "line", "plane", None),
            P(None, "line", "plane", None),
            P(None, "plane", None),
            P(None, None, "line", None),
            P(None, None, "plane", None),
        ),
        out_specs=P(None, "line", "plane", None),
        check_vma=False,
    )
```

```python
import jax
import jax.numpy as jnp
from jax import lax
from jax.experimental import pallas as pl
from jax.experimental.pallas import tpu as pltpu
from jax.sharding import PartitionSpec as P

F32 = jnp.float32
NV, NI, NJ, NK = 5, 16, 8, 256
HALF = NK // 2
PLANE = NI * NJ
TILE = (NJ, NK)
MAPS = NV * 16


def rows_of(shape):
    return lax.broadcasted_iota(jnp.int32, shape, len(shape) - 2)


def lanes_of(shape):
    return lax.broadcasted_iota(jnp.int32, shape, len(shape) - 1)


def call(kernel, outs, *args, scratch=(), in_hbm=0, out_hbm=False, name=None, flops=1000):
    outs = [jax.ShapeDtypeStruct(s, F32) for s in outs]
    args = [
        pltpu.with_memory_space_constraint(x, pltpu.HBM) if n < in_hbm else x
        for n, x in enumerate(args)
    ]
    spaces = [pltpu.HBM] * in_hbm + [pltpu.VMEM] * (len(args) - in_hbm)
    return pl.pallas_call(
        kernel,
        out_shape=outs,
        in_specs=[pl.BlockSpec(memory_space=s) for s in spaces],
        out_specs=[pl.BlockSpec(memory_space=pltpu.HBM if out_hbm else pltpu.VMEM)] * len(outs),
        scratch_shapes=list(scratch),
        compiler_params=pltpu.CompilerParams(vmem_limit_bytes=40 * 1024 * 1024),
        cost_estimate=pl.CostEstimate(flops=flops, bytes_accessed=flops, transcendentals=0),
        name=name,
    )(*args)


def place():
    q = lax.axis_index("plane")
    return lax.rem(q, 2), lax.rem(q // 2, 8), q // 16


def pick(p, options):
    out = options[-1]
    for n in reversed(range(len(options) - 1)):
        out = jnp.where(p == n, options[n], out)
    return out


def faces_kernel(
    a_hbm, e_hbm, w_ref, ia_ref, ib_ref, ja_ref, jb_ref, a_scr, e_scr, scr, sems
):
    even_line = lax.rem(lax.axis_index("line"), 2) == 0
    even_plane = lax.rem(lax.axis_index("plane"), 2) == 0

    def fetch(v, n):
        src, dst = ((a_hbm, a_scr), (e_hbm, e_scr))[n]
        at = pl.ds(v * PLANE, PLANE)
        return pltpu.make_async_copy(src.at[at], dst.at[at], sems.at[v, n])

    for v in range(NV):
        for n in range(2):
            fetch(v, n).start()
    for v in range(NV):
        for n in range(2):
            fetch(v, n).wait()
        base = v * PLANE
        for part in range(2):
            lane = slice(part * HALF, part * HALF + HALF)
            w = a_scr[base : base + PLANE, lane] * e_scr[base : base + PLANE, lane]
            w_ref[base : base + PLANE, lane] = w
            scr[v, part] = w
            low, high = w[:NJ], w[PLANE - NJ :]
            ia_ref[v, :, lane] = jnp.where(even_line, high, low)
            ib_ref[v, :, lane] = jnp.where(even_line, low, high)
            low = scr[v, part, pl.ds(0, NI, stride=NJ), :]
            high = scr[v, part, pl.ds(NJ - 1, NI, stride=NJ), :]
            ja_ref[v, :, lane] = jnp.where(even_plane, high, low)
            jb_ref[v, :, lane] = jnp.where(even_plane, low, high)


def prep_kernel(
    x_hbm, m_hbm, w_ref, f_ref, c_ref,
    half_ref, line_resp_ref, maps_ref, cross_resp_ref, halo_resp_ref, co_ref, g_ref, t_ref, x_ref,
    m_ref, sems,
):
    copies = [
        pltpu.make_async_copy(x_hbm, x_ref, sems.at[0]),
        pltpu.make_async_copy(m_hbm, m_ref, sems.at[1]),
    ]
    for copy in copies:
        copy.start()
    even = place()[0] == 0
    for v in range(NV):
        for n in range(6):
            c = c_ref[v, n]
            half_ref[v, n] = jnp.where(even, c[:, :HALF], c[:, HALF:])
    line_coeffs_of(c_ref, line_resp_ref, maps_ref)
    for copy in copies:
        copy.wait()
    cross_coeffs_of(x_ref, cross_resp_ref, halo_resp_ref, co_ref)
    local_source(w_ref, f_ref, m_ref, x_ref, g_ref, t_ref)


def line_coeffs_of(c_ref, resp_ref, msg_ref):
    row = rows_of(TILE)
    unit = [jnp.where(row == n, 1.0, 0.0) for n in range(4)]
    one, two = [unit[0]] * NV, [unit[1]] * NV
    lower = [[None] * NI for _ in range(NV)]
    for i in range(NI):
        for v in range(NV):
            first, second = (c_ref[v, n, i : i + 1, :] for n in range(2))
            one[v], two[v] = first * one[v] + second * two[v], one[v]
            lower[v][i] = one[v]
    for v in range(NV):
        msg_ref[v * 12 : v * 12 + 2, :] = one[v][0:2]
        msg_ref[v * 12 + 2 : v * 12 + 4, :] = two[v][0:2]
    one, two = [unit[2]] * NV, [unit[3]] * NV
    for i in reversed(range(NI)):
        for v in range(NV):
            first, second, scale = (c_ref[v, n, i : i + 1, :] for n in range(3, 6))
            one[v], two[v] = scale * lower[v][i] + first * one[v] + second * two[v], one[v]
            at = v * PLANE + i * NJ
            for part in range(2):
                resp_ref[part, at : at + NJ, :] = one[v][:, part * HALF : part * HALF + HALF]
    for v in range(NV):
        msg_ref[v * 12 + 4 : v * 12 + 8, :] = one[v][0:4]
        msg_ref[v * 12 + 8 : v * 12 + 12, :] = two[v][0:4]
    msg_ref[60:, :] = jnp.zeros((4, NK), F32)


def up_steps(c):
    row = rows_of(TILE)
    one = jnp.where(row == 0, 0.0, c)
    two = one * pltpu.roll(one, 1, 0)
    return (one, two, two * pltpu.roll(two, 2, 0))


def down_steps(c):
    row = rows_of(TILE)
    one = jnp.where(row == NJ - 1, 0.0, c)
    two = one * pltpu.roll(one, NJ - 1, 0)
    return (one, two, two * pltpu.roll(two, NJ - 2, 0))


def scan_up(x, steps):
    for n, c in zip((1, 2, 4), steps):
        x = x + c * pltpu.roll(x, n, 0)
    return x


def scan_down(x, steps):
    for n, c in zip((1, 2, 4), steps):
        x = x + c * pltpu.roll(x, NJ - n, 0)
    return x


def cross_coeffs_of(x_ref, resp_ref, halo_ref, co_ref):
    row = rows_of(TILE)
    co_ref[15:, :] = jnp.zeros((1, NK), F32)
    for v in range(NV):
        fc, fd, bc, bd = (x_ref[v, n] for n in range(4))
        up, dn = up_steps(fc), down_steps(bc)
        f_resp = scan_up(jnp.where(row == 0, fc, 0.0), up)
        g_resp = scan_down(bd * f_resp, dn)
        b_resp = scan_down(jnp.where(row == NJ - 1, bc, 0.0), dn)
        resp_ref[v, 0] = g_resp
        resp_ref[v, 1] = b_resp
        for n, at, half in ((0, 0, 0.5), (1, NJ - 1, -0.5)):
            f = scan_up(jnp.where(row == at, half * fd, 0.0), up)
            g = scan_down(bd * f, dn)
            halo_ref[v, n] = g
            halo_ref[v, n + 2] = edge_rows(f, g)
        co_ref[v : v + 1, :] = f_resp[NJ - 1 : NJ]
        co_ref[NV + v : NV + v + 1, :] = b_resp[0:1]
        co_ref[2 * NV + v : 2 * NV + v + 1, :] = g_resp[0:1]


def edge_rows(f, g):
    row = rows_of(TILE)
    return jnp.where(row == 0, pltpu.roll(f, 1, 0), pltpu.roll(g, 1, 0))


def local_source(w_ref, f_ref, m_ref, x_ref, g_ref, t_ref):
    p = lax.axis_index("line")
    row, lane = rows_of(TILE), lanes_of(TILE)
    zero = jnp.zeros(TILE, F32)
    low_mask = jnp.where(p == 0, m_ref[0].astype(F32), zero)
    high_mask = jnp.where(p == 3, m_ref[1].astype(F32), zero)

    def step(v, _):
        base = pl.multiple_of(v * PLANE, PLANE)
        at = [pl.ds(base + i * NJ, NJ) for i in range(NI)]
        w = [w_ref[at[i], :] for i in range(NI)]
        fd, bd = x_ref[v, 1], x_ref[v, 3]
        up, dn = up_steps(x_ref[v, 0]), down_steps(x_ref[v, 2])
        for i in range(NI):
            x = w[i]
            before = low_mask * x if i == 0 else w[i - 1]
            after = high_mask * x if i == NI - 1 else w[i + 1]
            j_before = jnp.where(row == 0, 0.0, pltpu.roll(x, 1, 0))
            j_after = jnp.where(row == NJ - 1, 0.0, pltpu.roll(x, NJ - 1, 0))
            k_before = jnp.where(lane == 0, 0.0, pltpu.roll(x, 1, 1))
            k_after = jnp.where(lane == NK - 1, 0.0, pltpu.roll(x, NK - 1, 1))
            s = f_ref[at[i], :] + 0.5 * (
                (before - after) + (j_before - j_after) + (k_before - k_after)
            )
            f = scan_up(fd * s, up)
            g = scan_down(bd * f, dn)
            g_ref[at[i], :] = g
            t_ref[at[i], :] = edge_rows(f, g)
        return 0

    lax.fori_loop(0, NV, step, 0)


def source_kernel(
    t_in, ia_ref, ib_ref, ja_ref, jb_ref, x_ref, halo_ref, co_ref,
    low_ref, high_ref, gi_ref, keep_ref, send_ref, t_scr,
):
    p, q = lax.axis_index("line"), lax.axis_index("plane")
    even_line, even_plane = lax.rem(p, 2) == 0, lax.rem(q, 2) == 0
    for v in range(NV):
        ia, ib = ia_ref[v], ib_ref[v]
        low = jnp.where(p == 0, 0.0, jnp.where(even_line, ib, ia))
        high = jnp.where(p == 3, 0.0, jnp.where(even_line, ia, ib))
        ja, jb = ja_ref[v], jb_ref[v]
        j_low = jnp.where(q == 0, 0.0, jnp.where(even_plane, jb, ja))
        j_high = jnp.where(q == 63, 0.0, jnp.where(even_plane, ja, jb))
        low_ref[v] = j_low
        high_ref[v] = j_high
        fd, bd = x_ref[v, 1], x_ref[v, 3]
        up, dn = up_steps(x_ref[v, 0]), down_steps(x_ref[v, 2])
        ends = []
        for n, face in enumerate((0.5 * low, -0.5 * high)):
            f = scan_up(fd * face, up)
            g = scan_down(bd * f, dn)
            gi_ref[v, n] = g
            ends.append(edge_rows(f, g))
        a, b = halo_ref[v, 2], halo_ref[v, 3]
        for i in range(NI):
            at = slice(v * PLANE + i * NJ, v * PLANE + i * NJ + NJ)
            t = t_in[at, :] + a * j_low[i : i + 1] + b * j_high[i : i + 1]
            if i == 0:
                t = t + ends[0]
            if i == NI - 1:
                t = t + ends[1]
            for half in range(2):
                t_scr[half, at, :] = t[:, half * HALF : half * HALF + HALF]
        for n in range(2):
            a, b = (t_scr[half, pl.ds(v * PLANE + n, NI, stride=NJ), :] for half in range(2))
            at = slice(v * 32 + n * NI, v * 32 + n * NI + NI)
            keep_ref[at, :] = jnp.where(even_plane, a, b)
            send_ref[at, :] = jnp.where(even_plane, b, a)
    a, b = co_ref[:, :HALF], co_ref[:, HALF:]
    keep_ref[160:, :] = jnp.where(even_plane, a, b)
    send_ref[160:, :] = jnp.where(even_plane, b, a)


def layers_kernel(keep_ref, got_ref, c_ref, maps_ref, out_ref, msg_ref, t_scr):
    even = place()[0] == 0
    tile = (NJ, HALF)
    row = rows_of(tile)
    low, high = ordered(even, [keep_ref[...]], [got_ref[...]])
    low, high = low[0], high[0]
    for v in range(NV):
        for i in range(NI):
            a, b = v * 32 + i, v * 32 + NI + i
            t_scr[v * PLANE + i * NJ : v * PLANE + i * NJ + NJ, :] = jnp.where(
                row == 0,
                low[a : a + 1],
                jnp.where(row == 1, low[b : b + 1], jnp.where(row == 2, high[a : a + 1], high[b : b + 1])),
            )
    ends = local_sweeps(c_ref, t_scr, out_ref, out_ref)
    for v in range(NV):
        for n in range(2):
            a, b = ends[v][2 * n : 2 * n + 2]
            at = v * 16 + n * 8
            msg_ref[at : at + 8, :] = jnp.where(row < 4, a, pltpu.roll(b, 4, 0))
    msg_ref[MAPS:, :] = jnp.where(even, maps_ref[:, :HALF], maps_ref[:, HALF:])


def local_sweeps(c_ref, src_ref, tmp_ref, out_ref):
    zero = jnp.zeros((NJ, src_ref.shape[-1]), F32)
    one, two = [zero] * NV, [zero] * NV
    for i in range(NI):
        for v in range(NV):
            first, second, scale = (c_ref[v, n, i : i + 1, :] for n in range(3))
            at = slice(v * PLANE + i * NJ, v * PLANE + i * NJ + NJ)
            one[v], two[v] = scale * src_ref[at, :] + first * one[v] + second * two[v], one[v]
            tmp_ref[at, :] = one[v]
    ends = list(zip(one, two))
    one, two = [zero] * NV, [zero] * NV
    for i in reversed(range(NI)):
        for v in range(NV):
            first, second, scale = (c_ref[v, n, i : i + 1, :] for n in range(3, 6))
            at = slice(v * PLANE + i * NJ, v * PLANE + i * NJ + NJ)
            one[v], two[v] = scale * tmp_ref[at, :] + first * one[v] + second * two[v], one[v]
            out_ref[at, :] = one[v]
    return [ends[v] + (one[v], two[v]) for v in range(NV)]


def planes_kernel(c_ref, g_ref, halo_ref, low_ref, high_ref, gi_ref, out_ref, msg_ref, g_scr):
    for v in range(NV):
        a, b = halo_ref[v, 0], halo_ref[v, 1]
        for i in range(NI):
            at = slice(v * PLANE + i * NJ, v * PLANE + i * NJ + NJ)
            g = g_ref[at, :] + a * low_ref[v, i : i + 1, :] + b * high_ref[v, i : i + 1, :]
            if i == 0:
                g = g + gi_ref[v, 0]
            if i == NI - 1:
                g = g + gi_ref[v, 1]
            g_scr[at, :] = g
    ends = local_sweeps(c_ref, g_scr, out_ref, out_ref)
    for v in range(NV):
        for n, x in enumerate(ends[v]):
            msg_ref[v, n * NJ : n * NJ + NJ, :] = x


def maps_of(ref, v, at=MAPS):
    return ref[at + v * 12 : at + v * 12 + 12, :]


def line_pair(p, own, got):
    is_low = lax.rem(p, 2) == 0
    return (
        [jnp.where(is_low, a, b) for a, b in zip(own, got)],
        [jnp.where(is_low, b, a) for a, b in zip(own, got)],
    )


def l_after(m, phi, l):
    return (
        m[0:1] * l[0] + m[1:2] * l[1] + phi[0],
        m[2:3] * l[0] + m[3:4] * l[1] + phi[1],
    )


def u_before(m, beta, l, u):
    return (
        m[4:5] * l[0] + m[5:6] * l[1] + m[6:7] * u[0] + m[7:8] * u[1] + beta[0],
        m[8:9] * l[0] + m[9:10] * l[1] + m[10:11] * u[0] + m[11:12] * u[1] + beta[1],
    )


def pair_states(p, low, high):
    lm, la, lb, lc, ld = low
    hm, ha, hb, hc, hd = high
    phi = l_after(hm, (ha, hb), (la, lb))
    zero = jnp.zeros_like(la)
    beta = u_before(lm, (lc, ld), (zero, zero), u_before(hm, (hc, hd), (la, lb), (zero, zero)))
    upper = p >= 2
    return [jnp.where(upper, a, b) for a, b in zip(beta, phi)]


def pair_gamma(low_m, high_m):
    columns = []
    for c in range(2):
        l = (low_m[c : c + 1], low_m[2 + c : 3 + c])
        a = high_m[4:5] * l[0] + high_m[5:6] * l[1]
        b = high_m[8:9] * l[0] + high_m[9:10] * l[1]
        columns.append(
            (
                low_m[4 + c : 5 + c] + low_m[6:7] * a + low_m[7:8] * b,
                low_m[8 + c : 9 + c] + low_m[10:11] * a + low_m[11:12] * b,
            )
        )
    (raa, rba), (rab, rbb) = columns
    return raa, rab, rba, rbb


def entering(p, low, high, mine, got, gamma):
    upper, is_low = p >= 2, lax.rem(p, 2) == 0
    zero = jnp.zeros_like(mine[0])
    l = [jnp.where(upper, x, zero) for x in got]
    raa, rab, rba, rbb = gamma
    u = (
        got[0] + raa * mine[0] + rab * mine[1],
        got[1] + rba * mine[0] + rbb * mine[1],
    )
    u = [jnp.where(upper, zero, x) for x in u]
    l_high = l_after(low[0], low[1:3], l)
    u_low = u_before(high[0], high[3:5], l_high, u)
    return [jnp.where(is_low, a, b) for a, b in zip(l, l_high)] + [
        jnp.where(is_low, a, b) for a, b in zip(u_low, u)
    ]


def edges_kernel(
    layers_ref, resp_ref, keep_ref, gotc_ref, own_ref, got1_ref, got2_ref, got3_ref,
    low_ref, high_ref, chip_ref, maps_ref,
):
    p, core = lax.axis_index("line"), place()[0]
    refs = (own_ref, got1_ref, got2_ref, got3_ref)
    for v in range(NV):
        rows, maps = [], []
        for r in range(4):
            at = slice(v * 16, v * 16 + 16)
            rows.append(pick(p, [refs[r ^ own][at, :] for own in range(4)]))
            maps.append(pick(p, [maps_of(refs[r ^ own], v) for own in range(4)]))
        part = [[x[n * 4 : n * 4 + 4] for n in range(4)] for x in rows]
        zero = jnp.zeros((4, HALF), F32)
        low = [(zero, zero), (part[0][0], part[0][1])]
        for r in (1, 2):
            low.append(l_after(maps[r], part[r][:2], low[r]))
        high = [None, None, None, (zero, zero)]
        for r in (3, 2, 1):
            high[r - 1] = u_before(maps[r], part[r][2:], low[r], high[r])
        states = [pick(p, [x[t] for x in low]) for t in range(2)]
        states += [pick(p, [x[t] for x in high]) for t in range(2)]
        answers = [resp_ref[core, pl.ds(v * PLANE + n, NI, stride=NJ), :] for n in range(4)]
        for t in range(4):
            x = layers_ref[pl.ds(v * PLANE + t, NI, stride=NJ), :]
            for n in range(4):
                x = x + answers[n] * states[n][t : t + 1]
            at = v * 32 + (t % 2) * NI
            (low_ref, high_ref)[t // 2][at : at + NI, :] = x
        maps_ref[v * 12 : v * 12 + 12, :] = maps_of(got1_ref, v)
        for n, x in enumerate(pair_gamma(maps[2], maps[3])):
            maps_ref[60 + v * 4 + n : 61 + v * 4 + n, :] = x
    own, other = keep_ref[160:, :], gotc_ref[160:, :]
    low_ref[160:, :] = jnp.where(core == 0, own, other)
    high_ref[160:, :] = jnp.where(core == 0, other, own)
    store(chip_ref, compose(load(low_ref), load(high_ref)))


def last_gamma(ref, v):
    return [ref[60 + v * 4 + n : 61 + v * 4 + n, :] for n in range(4)]


def big_parts(ref, maps_ref, v):
    return [maps_of(maps_ref, v, 0)] + [ref[v, n * NJ : n * NJ + NJ, :] for n in range(4)]


def plane_pair_kernel(own_ref, got_ref, own_maps, half_ref, other_ref, out_ref, got_maps):
    p = lax.axis_index("line")
    even = place()[0] == 0
    a, b = half_ref[...], other_ref[...]
    got_maps[:, :HALF] = jnp.where(even, a, b)
    got_maps[:, HALF:] = jnp.where(even, b, a)
    for v in range(NV):
        low, high = line_pair(p, big_parts(own_ref, own_maps, v), big_parts(got_ref, got_maps, v))
        a, b = pair_states(p, low, high)
        out_ref[v, :NJ, :] = a
        out_ref[v, NJ:, :] = b


def solved_kernel(
    local_ref, resp_ref, own_ref, got_ref, own_maps, got_maps, mine2_ref, got2_ref, out_ref
):
    p = lax.axis_index("line")
    for v in range(NV):
        low, high = line_pair(p, big_parts(own_ref, own_maps, v), big_parts(got_ref, got_maps, v))
        mine = (mine2_ref[v, :NJ, :], mine2_ref[v, NJ:, :])
        got = (got2_ref[v, :NJ, :], got2_ref[v, NJ:, :])
        states = entering(p, low, high, mine, got, last_gamma(got_maps, v))
        for i in range(NI):
            at = v * PLANE + i * NJ
            for part in range(2):
                lane = slice(part * HALF, part * HALF + HALF)
                x = local_ref[at : at + NJ, lane]
                for n in range(4):
                    x = x + resp_ref[part, at + n : at + n + 1, :] * states[n][:, lane]
                out_ref[at : at + NJ, lane] = x


def load(ref):
    phi = [ref[v * 32 : v * 32 + NI, :] for v in range(NV)]
    beta = [ref[v * 32 + NI : v * 32 + 2 * NI, :] for v in range(NV)]
    return (phi, beta, ref[160:165, :], ref[165:170, :], ref[170:175, :])


def store(ref, agg):
    phi, beta, F, B, g = agg
    for v in range(NV):
        ref[v * 32 : v * 32 + NI, :] = phi[v]
        ref[v * 32 + NI : v * 32 + 2 * NI, :] = beta[v]
    ref[160:165, :] = F
    ref[165:170, :] = B
    ref[170:175, :] = g
    ref[175:176, :] = jnp.zeros((1, HALF), F32)


def choose(low_is_own, own, other):
    return jax.tree.map(lambda a, b: jnp.where(low_is_own, a, b), own, other)


def ordered(low_is_own, own, other):
    return choose(low_is_own, own, other), choose(low_is_own, other, own)


def compose(low, high):
    lp, lb, lF, lB, lg = low
    hp, hb, hF, hB, hg = high
    at = [slice(v, v + 1) for v in range(NV)]
    return (
        [hF[at[v]] * lp[v] + hp[v] for v in range(NV)],
        [lb[v] + lB[at[v]] * (hb[v] + hg[at[v]] * lp[v]) for v in range(NV)],
        hF * lF,
        lB * hB,
        lg + lB * hg * lF,
    )


def f_after(agg, f):
    return [agg[2][v : v + 1] * f[v] + agg[0][v] for v in range(NV)]


def g_before(agg, f, u):
    return [agg[1][v] + agg[4][v : v + 1] * f[v] + agg[3][v : v + 1] * u[v] for v in range(NV)]


def bit_clear(z, n):
    return lax.rem(z // n, 2) == 0


def members(refs):
    m = lax.rem(place()[1], 4)
    parts = [load(r) for r in refs]
    return [
        jax.tree.map(lambda *x: pick(m, x), *(parts[r ^ own] for own in range(4)))
        for r in range(4)
    ]


def quad_kernel(*refs):
    a, b, c, d = members(refs[:4])
    store(refs[-1], compose(compose(a, b), compose(c, d)))


def ring_kernel(own_ref, got_ref, after_ref, out_ref):
    store(out_ref, compose(*ordered(bit_clear(place()[1], 4), load(own_ref), load(got_ref))))


def top_kernel(own_ref, got_ref, out_ref):
    y = place()[2]
    agg = compose(*ordered(bit_clear(y, 1), load(own_ref), load(got_ref)))
    for v in range(NV):
        out_ref[v * NI : v * NI + NI, :] = jnp.where(y >= 2, agg[1][v], agg[0][v])
    out_ref[80:85, :] = agg[4]
    out_ref[85:88, :] = jnp.zeros((3, HALF), F32)


def step_down(is_low, low, high, f, u):
    f_high = f_after(low, f)
    u_low = g_before(high, f_high, u)
    return (f, u_low), (f_high, u)


def put_states(ref, states):
    for v in range(NV):
        ref[v * 32 : v * 32 + NI, :] = states[0][v]
        ref[v * 32 + NI : v * 32 + 2 * NI, :] = states[1][v]


def down_kernel(
    mine_ref, got_ref, own8_ref, got8_ref, own4_ref, got4_ref,
    q0_ref, q1_ref, q2_ref, q3_ref, low_ref, high_ref, after_ref, keep_ref, send_ref,
):
    core, z, y = place()
    upper = y >= 2
    zero = jnp.zeros((NI, HALF), F32)
    at = [slice(v * NI, v * NI + NI) for v in range(NV)]
    f = [jnp.where(upper, got_ref[x, :], zero) for x in at]
    u = [
        jnp.where(upper, zero, got_ref[x, :] + got_ref[80 + v : 81 + v, :] * mine_ref[x, :])
        for v, x in enumerate(at)
    ]
    for is_low, mine, got in (
        (bit_clear(y, 1), own8_ref, got8_ref),
        (bit_clear(z, 4), own4_ref, got4_ref),
    ):
        low, high = ordered(is_low, load(mine), load(got))
        f, u = choose(is_low, *step_down(is_low, low, high, f, u))
    parts = members((q0_ref, q1_ref, q2_ref, q3_ref))
    fs, us = [f], [None, None, None, u]
    for r in range(3):
        fs.append(f_after(parts[r], fs[r]))
    for r in (3, 2, 1):
        us[r - 1] = g_before(parts[r], fs[r], us[r])
    m = lax.rem(z, 4)
    f = [pick(m, [x[v] for x in fs]) for v in range(NV)]
    u = [pick(m, [x[v] for x in us]) for v in range(NV)]
    is_low = core == 0
    low, high = step_down(is_low, load(low_ref), load(high_ref), f, u)
    put_states(keep_ref, choose(is_low, low, high))
    put_states(send_ref, choose(is_low, high, low))


def final_kernel(g_ref, resp_ref, mine_ref, other_ref, out_ref, scr, fu_scr, sems):
    even = place()[0] == 0

    def copy(v):
        at = pl.ds(v * PLANE, PLANE)
        return pltpu.make_async_copy(scr.at[at], out_ref.at[at], sems.at[v])

    for v in range(NV):
        x, y = mine_ref[v * 32 : v * 32 + 32, :], other_ref[v * 32 : v * 32 + 32, :]
        fu_scr[v, :, :HALF] = jnp.where(even, x, y)
        fu_scr[v, :, HALF:] = jnp.where(even, y, x)
        a, b = resp_ref[v, 0], resp_ref[v, 1]
        for i in range(NI):
            at = slice(v * PLANE + i * NJ, v * PLANE + i * NJ + NJ)
            f, u = fu_scr[v, i : i + 1, :], fu_scr[v, NI + i : NI + i + 1, :]
            scr[at, :] = g_ref[at, :] + a * f + b * u
        copy(v).start()
    for v in range(NV):
        copy(v).wait()


def swap(x, axis, size, flip):
    return lax.ppermute(x, axis, [(i, i ^ flip) for i in range(size)])


def across(x):
    pairs = []
    for q in range(64):
        z = q // 2 % 8
        other = (6 - z if z % 2 == 0 else 8 - z) % 8
        pairs.append((q, q + 2 * (other - z)))
    return lax.ppermute(x, "plane", pairs)


def body(adjoint, forcing, eigen_values, face_masks, line_coeffs, cross_coeffs):
    flat = (NV * PLANE, NK)
    a, f, e = (x.reshape(flat) for x in (adjoint, forcing, eigen_values))
    i_face, j_face = (NV, NJ, NK), (NV, NI, NK)
    w, ia, ib, ja, jb = call(
        faces_kernel, [flat, i_face, i_face, j_face, j_face], a, e, in_hbm=2, name="faces",
        scratch=[
            pltpu.VMEM(flat, F32),
            pltpu.VMEM(flat, F32),
            pltpu.VMEM((NV, 2, PLANE, HALF), F32),
            pltpu.SemaphoreType.DMA((NV, 2)),
        ],
    )
    ia = swap(ia, "line", 4, 1)
    ib = swap(ib, "line", 4, 3)
    ja = swap(ja, "plane", 64, 1)
    jb = lax.ppermute(jb, "plane", [(i, (i + 1 if i % 2 else i - 1) % 64) for i in range(64)])

    halves = (2, NV * PLANE, HALF)
    half, line_resp, maps, cross_resp, halo_resp, co, g, t, x = call(
        prep_kernel,
        [
            line_coeffs.shape[:3] + (HALF,), halves, (64, NK), (NV, 2, NJ, NK), (NV, 4, NJ, NK),
            (16, NK), flat, flat, cross_coeffs.shape,
        ],
        cross_coeffs, face_masks, w, f, line_coeffs, in_hbm=2, name="prep", flops=10**7,
        scratch=[
            pltpu.VMEM(face_masks.shape, face_masks.dtype),
            pltpu.SemaphoreType.DMA((2,)),
        ],
    )
    msg = (176, HALF)
    j_low, j_high, gi, keep, send = call(
        source_kernel, [j_face, j_face, (NV, 2, NJ, NK), msg, msg],
        t, ia, ib, ja, jb, x, halo_resp, co, scratch=[pltpu.VMEM(halves, F32)], name="source",
    )
    got = swap(send, "plane", 64, 1)
    half_flat = (NV * PLANE, HALF)
    layers, small = call(
        layers_kernel, [half_flat, (MAPS + 64, HALF)], keep, got, half, maps,
        scratch=[pltpu.VMEM(half_flat, F32)], name="layers",
    )
    smalls = [small] + [swap(small, "line", 4, d) for d in (1, 2, 3)]
    low, high, chip, pair_maps = call(
        edges_kernel, [msg, msg, msg, (80, HALF)],
        layers, line_resp, keep, got, *smalls, name="edges",
    )
    quad = [chip] + [swap(chip, "plane", 64, d) for d in (2, 4, 6)]

    local, big = call(
        planes_kernel, [flat, (NV, 32, NK)], line_coeffs, g, halo_resp, j_low, j_high, gi,
        scratch=[pltpu.VMEM(flat, F32)], name="planes", flops=10**7,
    )
    got_big = swap(big, "line", 4, 1)
    last_big, line_maps = call(
        plane_pair_kernel, [(NV, 16, NK), (80, NK)],
        big, got_big, maps, pair_maps, swap(pair_maps, "plane", 64, 1), name="plane_pair",
    )
    got_last_big = swap(last_big, "line", 4, 3)
    solved = call(
        solved_kernel, [flat],
        local, line_resp, big, got_big, maps, line_maps, last_big, got_last_big,
        name="solved", flops=10**7,
    )[0]

    own4 = call(quad_kernel, [msg], *quad, big, name="quad")[0]
    got4 = across(own4)
    own8 = call(ring_kernel, [msg], own4, got4, last_big, name="ring")[0]
    got8 = swap(own8, "plane", 64, 16)
    top = call(top_kernel, [(88, HALF)], own8, got8, name="top")[0]
    got_top = swap(top, "plane", 64, 48)
    mine, send = call(
        down_kernel, [(160, HALF)] * 2,
        top, got_top, own8, got8, own4, got4, *quad, low, high, solved, name="down",
    )
    other = swap(send, "plane", 64, 1)
    out = call(
        final_kernel, [flat], solved, cross_resp, mine, other, out_hbm=True, name="final",
        scratch=[
            pltpu.VMEM(flat, F32),
            pltpu.VMEM((NV, 2 * NI, NK), F32),
            pltpu.SemaphoreType.DMA((NV,)),
        ],
    )[0]
    return out.reshape(NV, NI, NJ, NK)


def solution(mesh):
    return jax.shard_map(
        body,
        mesh=mesh,
        in_specs=(
            P(None, "line", "plane", None),
            P(None, "line", "plane", None),
            P(None, "line", "plane", None),
            P(None, "plane", None),
            P(None, None, "line", None),
            P(None, None, "plane", None),
        ),
        out_specs=P(None, "line", "plane", None),
        check_vma=False,
    )
```

```python
import jax
import jax.numpy as jnp
from jax import lax
from jax.experimental import pallas as pl
from jax.experimental.pallas import tpu as pltpu
from jax.sharding import PartitionSpec as P

F32 = jnp.float32
NV, NI, NJ, NK = 5, 16, 8, 256
HALF = NK // 2
PLANE = NI * NJ
TILE = (NJ, NK)
MAPS = NV * 16


def rows_of(shape):
    return lax.broadcasted_iota(jnp.int32, shape, len(shape) - 2)


def lanes_of(shape):
    return lax.broadcasted_iota(jnp.int32, shape, len(shape) - 1)


def call(kernel, outs, *args, scratch=(), in_hbm=0, out_hbm=False, name=None, flops=1000):
    outs = [jax.ShapeDtypeStruct(s, F32) for s in outs]
    args = [
        pltpu.with_memory_space_constraint(x, pltpu.HBM) if n < in_hbm else x
        for n, x in enumerate(args)
    ]
    spaces = [pltpu.HBM] * in_hbm + [pltpu.VMEM] * (len(args) - in_hbm)
    return pl.pallas_call(
        kernel,
        out_shape=outs,
        in_specs=[pl.BlockSpec(memory_space=s) for s in spaces],
        out_specs=[pl.BlockSpec(memory_space=pltpu.HBM if out_hbm else pltpu.VMEM)] * len(outs),
        scratch_shapes=list(scratch),
        compiler_params=pltpu.CompilerParams(vmem_limit_bytes=40 * 1024 * 1024),
        cost_estimate=pl.CostEstimate(flops=flops, bytes_accessed=flops, transcendentals=0),
        name=name,
    )(*args)


def place():
    q = lax.axis_index("plane")
    return lax.rem(q, 2), lax.rem(q // 2, 8), q // 16


def pick(p, options):
    out = options[-1]
    for n in reversed(range(len(options) - 1)):
        out = jnp.where(p == n, options[n], out)
    return out


def faces_kernel(
    a_hbm, e_hbm, w_ref, ia_ref, ib_ref, ja_ref, jb_ref, a_scr, e_scr, scr, sems
):
    even_line = lax.rem(lax.axis_index("line"), 2) == 0
    even_plane = lax.rem(lax.axis_index("plane"), 2) == 0

    def fetch(v, n):
        src, dst = ((a_hbm, a_scr), (e_hbm, e_scr))[n]
        at = pl.ds(v * PLANE, PLANE)
        return pltpu.make_async_copy(src.at[at], dst.at[at], sems.at[v, n])

    for v in range(NV):
        for n in range(2):
            fetch(v, n).start()
    for v in range(NV):
        for n in range(2):
            fetch(v, n).wait()
        base = v * PLANE
        for part in range(2):
            lane = slice(part * HALF, part * HALF + HALF)
            w = a_scr[base : base + PLANE, lane] * e_scr[base : base + PLANE, lane]
            w_ref[base : base + PLANE, lane] = w
            scr[v, part] = w
            low, high = w[:NJ], w[PLANE - NJ :]
            ia_ref[v, :, lane] = jnp.where(even_line, high, low)
            ib_ref[v, :, lane] = jnp.where(even_line, low, high)
            low = scr[v, part, pl.ds(0, NI, stride=NJ), :]
            high = scr[v, part, pl.ds(NJ - 1, NI, stride=NJ), :]
            ja_ref[v, :, lane] = jnp.where(even_plane, high, low)
            jb_ref[v, :, lane] = jnp.where(even_plane, low, high)


def prep_kernel(
    x_hbm, m_hbm, w_ref, f_ref, c_ref,
    half_ref, line_resp_ref, maps_ref, cross_resp_ref, halo_resp_ref, co_ref, g_ref, t_ref, x_ref,
    m_ref, sems,
):
    copies = [
        pltpu.make_async_copy(x_hbm, x_ref, sems.at[0]),
        pltpu.make_async_copy(m_hbm, m_ref, sems.at[1]),
    ]
    for copy in copies:
        copy.start()
    even = place()[0] == 0
    for v in range(NV):
        for n in range(6):
            c = c_ref[v, n]
            half_ref[v, n] = jnp.where(even, c[:, :HALF], c[:, HALF:])
    line_coeffs_of(c_ref, line_resp_ref, maps_ref)
    for copy in copies:
        copy.wait()
    cross_coeffs_of(x_ref, cross_resp_ref, halo_resp_ref, co_ref)
    local_source(w_ref, f_ref, m_ref, x_ref, g_ref, t_ref)


def line_coeffs_of(c_ref, resp_ref, msg_ref):
    row = rows_of(TILE)
    unit = [jnp.where(row == n, 1.0, 0.0) for n in range(4)]
    one, two = [unit[0]] * NV, [unit[1]] * NV
    lower = [[None] * NI for _ in range(NV)]
    for i in range(NI):
        for v in range(NV):
            first, second = (c_ref[v, n, i : i + 1, :] for n in range(2))
            one[v], two[v] = first * one[v] + second * two[v], one[v]
            lower[v][i] = one[v]
    for v in range(NV):
        msg_ref[v * 12 : v * 12 + 2, :] = one[v][0:2]
        msg_ref[v * 12 + 2 : v * 12 + 4, :] = two[v][0:2]
    one, two = [unit[2]] * NV, [unit[3]] * NV
    for i in reversed(range(NI)):
        for v in range(NV):
            first, second, scale = (c_ref[v, n, i : i + 1, :] for n in range(3, 6))
            one[v], two[v] = scale * lower[v][i] + first * one[v] + second * two[v], one[v]
            at = v * PLANE + i * NJ
            for part in range(2):
                resp_ref[part, at : at + NJ, :] = one[v][:, part * HALF : part * HALF + HALF]
    for v in range(NV):
        msg_ref[v * 12 + 4 : v * 12 + 8, :] = one[v][0:4]
        msg_ref[v * 12 + 8 : v * 12 + 12, :] = two[v][0:4]
    msg_ref[60:, :] = jnp.zeros((4, NK), F32)


def up_steps(c):
    row = rows_of(TILE)
    one = jnp.where(row == 0, 0.0, c)
    two = one * pltpu.roll(one, 1, 0)
    return (one, two, two * pltpu.roll(two, 2, 0))


def down_steps(c):
    row = rows_of(TILE)
    one = jnp.where(row == NJ - 1, 0.0, c)
    two = one * pltpu.roll(one, NJ - 1, 0)
    return (one, two, two * pltpu.roll(two, NJ - 2, 0))


def scan_up(x, steps):
    for n, c in zip((1, 2, 4), steps):
        x = x + c * pltpu.roll(x, n, 0)
    return x


def scan_down(x, steps):
    for n, c in zip((1, 2, 4), steps):
        x = x + c * pltpu.roll(x, NJ - n, 0)
    return x


def cross_coeffs_of(x_ref, resp_ref, halo_ref, co_ref):
    row = rows_of(TILE)
    co_ref[15:, :] = jnp.zeros((1, NK), F32)
    for v in range(NV):
        fc, fd, bc, bd = (x_ref[v, n] for n in range(4))
        up, dn = up_steps(fc), down_steps(bc)
        f_resp = scan_up(jnp.where(row == 0, fc, 0.0), up)
        g_resp = scan_down(bd * f_resp, dn)
        b_resp = scan_down(jnp.where(row == NJ - 1, bc, 0.0), dn)
        resp_ref[v, 0] = g_resp
        resp_ref[v, 1] = b_resp
        for n, at, half in ((0, 0, 0.5), (1, NJ - 1, -0.5)):
            f = scan_up(jnp.where(row == at, half * fd, 0.0), up)
            g = scan_down(bd * f, dn)
            halo_ref[v, n] = g
            halo_ref[v, n + 2] = edge_rows(f, g)
        co_ref[v : v + 1, :] = f_resp[NJ - 1 : NJ]
        co_ref[NV + v : NV + v + 1, :] = b_resp[0:1]
        co_ref[2 * NV + v : 2 * NV + v + 1, :] = g_resp[0:1]


def edge_rows(f, g):
    row = rows_of(TILE)
    return jnp.where(row == 0, pltpu.roll(f, 1, 0), pltpu.roll(g, 1, 0))


def local_source(w_ref, f_ref, m_ref, x_ref, g_ref, t_ref):
    p = lax.axis_index("line")
    row, lane = rows_of(TILE), lanes_of(TILE)
    zero = jnp.zeros(TILE, F32)
    low_mask = jnp.where(p == 0, m_ref[0].astype(F32), zero)
    high_mask = jnp.where(p == 3, m_ref[1].astype(F32), zero)

    def step(v, _):
        base = pl.multiple_of(v * PLANE, PLANE)
        at = [pl.ds(base + i * NJ, NJ) for i in range(NI)]
        w = [w_ref[at[i], :] for i in range(NI)]
        fd, bd = x_ref[v, 1], x_ref[v, 3]
        up, dn = up_steps(x_ref[v, 0]), down_steps(x_ref[v, 2])
        for i in range(NI):
            x = w[i]
            before = low_mask * x if i == 0 else w[i - 1]
            after = high_mask * x if i == NI - 1 else w[i + 1]
            j_before = jnp.where(row == 0, 0.0, pltpu.roll(x, 1, 0))
            j_after = jnp.where(row == NJ - 1, 0.0, pltpu.roll(x, NJ - 1, 0))
            k_before = jnp.where(lane == 0, 0.0, pltpu.roll(x, 1, 1))
            k_after = jnp.where(lane == NK - 1, 0.0, pltpu.roll(x, NK - 1, 1))
            s = f_ref[at[i], :] + 0.5 * (
                (before - after) + (j_before - j_after) + (k_before - k_after)
            )
            f = scan_up(fd * s, up)
            g = scan_down(bd * f, dn)
            g_ref[at[i], :] = g
            t_ref[at[i], :] = edge_rows(f, g)
        return 0

    lax.fori_loop(0, NV, step, 0)


def source_kernel(
    t_in, ia_ref, ib_ref, ja_ref, jb_ref, x_ref, halo_ref, co_ref,
    low_ref, high_ref, gi_ref, keep_ref, send_ref, t_scr,
):
    p, q = lax.axis_index("line"), lax.axis_index("plane")
    even_line, even_plane = lax.rem(p, 2) == 0, lax.rem(q, 2) == 0
    for v in range(NV):
        ia, ib = ia_ref[v], ib_ref[v]
        low = jnp.where(p == 0, 0.0, jnp.where(even_line, ib, ia))
        high = jnp.where(p == 3, 0.0, jnp.where(even_line, ia, ib))
        ja, jb = ja_ref[v], jb_ref[v]
        j_low = jnp.where(q == 0, 0.0, jnp.where(even_plane, jb, ja))
        j_high = jnp.where(q == 63, 0.0, jnp.where(even_plane, ja, jb))
        low_ref[v] = j_low
        high_ref[v] = j_high
        fd, bd = x_ref[v, 1], x_ref[v, 3]
        up, dn = up_steps(x_ref[v, 0]), down_steps(x_ref[v, 2])
        ends = []
        for n, face in enumerate((0.5 * low, -0.5 * high)):
            f = scan_up(fd * face, up)
            g = scan_down(bd * f, dn)
            gi_ref[v, n] = g
            ends.append(edge_rows(f, g))
        a, b = halo_ref[v, 2], halo_ref[v, 3]
        for i in range(NI):
            at = slice(v * PLANE + i * NJ, v * PLANE + i * NJ + NJ)
            t = t_in[at, :] + a * j_low[i : i + 1] + b * j_high[i : i + 1]
            if i == 0:
                t = t + ends[0]
            if i == NI - 1:
                t = t + ends[1]
            for half in range(2):
                t_scr[half, at, :] = t[:, half * HALF : half * HALF + HALF]
        for n in range(2):
            a, b = (t_scr[half, pl.ds(v * PLANE + n, NI, stride=NJ), :] for half in range(2))
            at = slice(v * 32 + n * NI, v * 32 + n * NI + NI)
            keep_ref[at, :] = jnp.where(even_plane, a, b)
            send_ref[at, :] = jnp.where(even_plane, b, a)
    a, b = co_ref[:, :HALF], co_ref[:, HALF:]
    keep_ref[160:, :] = jnp.where(even_plane, a, b)
    send_ref[160:, :] = jnp.where(even_plane, b, a)


def layers_kernel(keep_ref, got_ref, c_ref, maps_ref, out_ref, msg_ref, t_scr):
    even = place()[0] == 0
    tile = (NJ, HALF)
    row = rows_of(tile)
    low, high = ordered(even, [keep_ref[...]], [got_ref[...]])
    low, high = low[0], high[0]
    for v in range(NV):
        for i in range(NI):
            a, b = v * 32 + i, v * 32 + NI + i
            t_scr[v * PLANE + i * NJ : v * PLANE + i * NJ + NJ, :] = jnp.where(
                row == 0,
                low[a : a + 1],
                jnp.where(row == 1, low[b : b + 1], jnp.where(row == 2, high[a : a + 1], high[b : b + 1])),
            )
    ends = local_sweeps(c_ref, t_scr, out_ref, out_ref)
    for v in range(NV):
        for n in range(2):
            a, b = ends[v][2 * n : 2 * n + 2]
            at = v * 16 + n * 8
            msg_ref[at : at + 8, :] = jnp.where(row < 4, a, pltpu.roll(b, 4, 0))
    msg_ref[MAPS:, :] = jnp.where(even, maps_ref[:, :HALF], maps_ref[:, HALF:])


def local_sweeps(c_ref, src_ref, tmp_ref, out_ref):
    zero = jnp.zeros((NJ, src_ref.shape[-1]), F32)
    one, two = [zero] * NV, [zero] * NV
    for i in range(NI):
        for v in range(NV):
            first, second, scale = (c_ref[v, n, i : i + 1, :] for n in range(3))
            at = slice(v * PLANE + i * NJ, v * PLANE + i * NJ + NJ)
            one[v], two[v] = scale * src_ref[at, :] + first * one[v] + second * two[v], one[v]
            tmp_ref[at, :] = one[v]
    ends = list(zip(one, two))
    one, two = [zero] * NV, [zero] * NV
    for i in reversed(range(NI)):
        for v in range(NV):
            first, second, scale = (c_ref[v, n, i : i + 1, :] for n in range(3, 6))
            at = slice(v * PLANE + i * NJ, v * PLANE + i * NJ + NJ)
            one[v], two[v] = scale * tmp_ref[at, :] + first * one[v] + second * two[v], one[v]
            out_ref[at, :] = one[v]
    return [ends[v] + (one[v], two[v]) for v in range(NV)]


def planes_kernel(
    c_ref, g_ref, halo_ref, low_ref, high_ref, gi_ref, maps_ref, out_ref, msg_ref, g_scr
):
    for v in range(NV):
        a, b = halo_ref[v, 0], halo_ref[v, 1]
        for i in range(NI):
            at = slice(v * PLANE + i * NJ, v * PLANE + i * NJ + NJ)
            g = g_ref[at, :] + a * low_ref[v, i : i + 1, :] + b * high_ref[v, i : i + 1, :]
            if i == 0:
                g = g + gi_ref[v, 0]
            if i == NI - 1:
                g = g + gi_ref[v, 1]
            g_scr[at, :] = g
    ends = local_sweeps(c_ref, g_scr, out_ref, out_ref)
    for v in range(NV):
        for n, x in enumerate(ends[v]):
            msg_ref[v * 32 + n * NJ : v * 32 + n * NJ + NJ, :] = x
    msg_ref[BIG:, :] = maps_ref[...]


def maps_of(ref, v, at=MAPS):
    return ref[at + v * 12 : at + v * 12 + 12, :]


def line_pair(p, own, got):
    is_low = lax.rem(p, 2) == 0
    return (
        [jnp.where(is_low, a, b) for a, b in zip(own, got)],
        [jnp.where(is_low, b, a) for a, b in zip(own, got)],
    )


def l_after(m, phi, l):
    return (
        m[0:1] * l[0] + m[1:2] * l[1] + phi[0],
        m[2:3] * l[0] + m[3:4] * l[1] + phi[1],
    )


def u_before(m, beta, l, u):
    return (
        m[4:5] * l[0] + m[5:6] * l[1] + m[6:7] * u[0] + m[7:8] * u[1] + beta[0],
        m[8:9] * l[0] + m[9:10] * l[1] + m[10:11] * u[0] + m[11:12] * u[1] + beta[1],
    )


def pair_states(p, low, high):
    lm, la, lb, lc, ld = low
    hm, ha, hb, hc, hd = high
    phi = l_after(hm, (ha, hb), (la, lb))
    zero = jnp.zeros_like(la)
    beta = u_before(lm, (lc, ld), (zero, zero), u_before(hm, (hc, hd), (la, lb), (zero, zero)))
    upper = p >= 2
    return [jnp.where(upper, a, b) for a, b in zip(beta, phi)]


def pair_gamma(low_m, high_m):
    columns = []
    for c in range(2):
        l = (low_m[c : c + 1], low_m[2 + c : 3 + c])
        a = high_m[4:5] * l[0] + high_m[5:6] * l[1]
        b = high_m[8:9] * l[0] + high_m[9:10] * l[1]
        columns.append(
            (
                low_m[4 + c : 5 + c] + low_m[6:7] * a + low_m[7:8] * b,
                low_m[8 + c : 9 + c] + low_m[10:11] * a + low_m[11:12] * b,
            )
        )
    (raa, rba), (rab, rbb) = columns
    return raa, rab, rba, rbb


def entering(p, low, high, mine, got, gamma):
    upper, is_low = p >= 2, lax.rem(p, 2) == 0
    zero = jnp.zeros_like(mine[0])
    l = [jnp.where(upper, x, zero) for x in got]
    raa, rab, rba, rbb = gamma
    u = (
        got[0] + raa * mine[0] + rab * mine[1],
        got[1] + rba * mine[0] + rbb * mine[1],
    )
    u = [jnp.where(upper, zero, x) for x in u]
    l_high = l_after(low[0], low[1:3], l)
    u_low = u_before(high[0], high[3:5], l_high, u)
    return [jnp.where(is_low, a, b) for a, b in zip(l, l_high)] + [
        jnp.where(is_low, a, b) for a, b in zip(u_low, u)
    ]


def edges_kernel(
    layers_ref, resp_ref, keep_ref, gotc_ref, own_ref, got1_ref, got2_ref, got3_ref,
    low_ref, high_ref, chip_ref,
):
    p, core = lax.axis_index("line"), place()[0]
    refs = (own_ref, got1_ref, got2_ref, got3_ref)
    for v in range(NV):
        rows, maps = [], []
        for r in range(4):
            at = slice(v * 16, v * 16 + 16)
            rows.append(pick(p, [refs[r ^ own][at, :] for own in range(4)]))
            maps.append(pick(p, [maps_of(refs[r ^ own], v) for own in range(4)]))
        part = [[x[n * 4 : n * 4 + 4] for n in range(4)] for x in rows]
        zero = jnp.zeros((4, HALF), F32)
        low = [(zero, zero), (part[0][0], part[0][1])]
        for r in (1, 2):
            low.append(l_after(maps[r], part[r][:2], low[r]))
        high = [None, None, None, (zero, zero)]
        for r in (3, 2, 1):
            high[r - 1] = u_before(maps[r], part[r][2:], low[r], high[r])
        states = [pick(p, [x[t] for x in low]) for t in range(2)]
        states += [pick(p, [x[t] for x in high]) for t in range(2)]
        answers = [resp_ref[core, pl.ds(v * PLANE + n, NI, stride=NJ), :] for n in range(4)]
        for t in range(4):
            x = layers_ref[pl.ds(v * PLANE + t, NI, stride=NJ), :]
            for n in range(4):
                x = x + answers[n] * states[n][t : t + 1]
            at = v * 32 + (t % 2) * NI
            (low_ref, high_ref)[t // 2][at : at + NI, :] = x
    own, other = keep_ref[160:, :], gotc_ref[160:, :]
    low_ref[160:, :] = jnp.where(core == 0, own, other)
    high_ref[160:, :] = jnp.where(core == 0, other, own)
    store(chip_ref, compose(load(low_ref), load(high_ref)))


BIG = NV * 32
LAST = NV * 16


def big_parts(ref, v):
    at = v * 32
    return [maps_of(ref, v, BIG)] + [ref[at + n * NJ : at + n * NJ + NJ, :] for n in range(4)]


def last_parts(ref, v):
    at = v * 16
    return ref[at : at + NJ, :], ref[at + NJ : at + 2 * NJ, :]


def last_gamma(ref, v):
    return [ref[LAST + v * 4 + n : LAST + v * 4 + n + 1, :] for n in range(4)]


def plane_pair_kernel(own_ref, got_ref, out_ref):
    p = lax.axis_index("line")
    for v in range(NV):
        low, high = line_pair(p, big_parts(own_ref, v), big_parts(got_ref, v))
        a, b = pair_states(p, low, high)
        out_ref[v * 16 : v * 16 + NJ, :] = a
        out_ref[v * 16 + NJ : v * 16 + 2 * NJ, :] = b
        for n, x in enumerate(pair_gamma(low[0], high[0])):
            out_ref[LAST + v * 4 + n : LAST + v * 4 + n + 1, :] = x
    out_ref[LAST + 20 :, :] = jnp.zeros((4, NK), F32)


def solved_kernel(local_ref, resp_ref, own_ref, got_ref, mine2_ref, got2_ref, out_ref):
    p = lax.axis_index("line")
    for v in range(NV):
        low, high = line_pair(p, big_parts(own_ref, v), big_parts(got_ref, v))
        mine, got = last_parts(mine2_ref, v), last_parts(got2_ref, v)
        states = entering(p, low, high, mine, got, last_gamma(got2_ref, v))
        for i in range(NI):
            at = v * PLANE + i * NJ
            for part in range(2):
                lane = slice(part * HALF, part * HALF + HALF)
                x = local_ref[at : at + NJ, lane]
                for n in range(4):
                    x = x + resp_ref[part, at + n : at + n + 1, :] * states[n][:, lane]
                out_ref[at : at + NJ, lane] = x


def load(ref):
    phi = [ref[v * 32 : v * 32 + NI, :] for v in range(NV)]
    beta = [ref[v * 32 + NI : v * 32 + 2 * NI, :] for v in range(NV)]
    return (phi, beta, ref[160:165, :], ref[165:170, :], ref[170:175, :])


def store(ref, agg):
    phi, beta, F, B, g = agg
    for v in range(NV):
        ref[v * 32 : v * 32 + NI, :] = phi[v]
        ref[v * 32 + NI : v * 32 + 2 * NI, :] = beta[v]
    ref[160:165, :] = F
    ref[165:170, :] = B
    ref[170:175, :] = g
    ref[175:176, :] = jnp.zeros((1, HALF), F32)


def choose(low_is_own, own, other):
    return jax.tree.map(lambda a, b: jnp.where(low_is_own, a, b), own, other)


def ordered(low_is_own, own, other):
    return choose(low_is_own, own, other), choose(low_is_own, other, own)


def compose(low, high):
    lp, lb, lF, lB, lg = low
    hp, hb, hF, hB, hg = high
    at = [slice(v, v + 1) for v in range(NV)]
    return (
        [hF[at[v]] * lp[v] + hp[v] for v in range(NV)],
        [lb[v] + lB[at[v]] * (hb[v] + hg[at[v]] * lp[v]) for v in range(NV)],
        hF * lF,
        lB * hB,
        lg + lB * hg * lF,
    )


def f_after(agg, f):
    return [agg[2][v : v + 1] * f[v] + agg[0][v] for v in range(NV)]


def g_before(agg, f, u):
    return [agg[1][v] + agg[4][v : v + 1] * f[v] + agg[3][v : v + 1] * u[v] for v in range(NV)]


def bit_clear(z, n):
    return lax.rem(z // n, 2) == 0


def members(refs):
    m = lax.rem(place()[1], 4)
    parts = [load(r) for r in refs]
    return [
        jax.tree.map(lambda *x: pick(m, x), *(parts[r ^ own] for own in range(4)))
        for r in range(4)
    ]


def quad_kernel(*refs):
    a, b, c, d = members(refs[:4])
    store(refs[-1], compose(compose(a, b), compose(c, d)))


def ring_kernel(own_ref, got_ref, after_ref, out_ref, fore_ref):
    agg = compose(*ordered(bit_clear(place()[1], 4), load(own_ref), load(got_ref)))
    store(out_ref, agg)
    last = place()[2] == 3
    for v in range(NV):
        fore_ref[v * NI : v * NI + NI, :] = jnp.where(last, agg[1][v], agg[0][v])
    fore_ref[80:, :] = out_ref[160:, :]


def step_down(low, high, f, u):
    f_high = f_after(low, f)
    u_low = g_before(high, f_high, u)
    return (f, u_low), (f_high, u)


def put_states(ref, states):
    for v in range(NV):
        ref[v * 32 : v * 32 + NI, :] = states[0][v]
        ref[v * 32 + NI : v * 32 + 2 * NI, :] = states[1][v]


def down_kernel(
    own_ref, one_ref, two_ref, three_ref, own4_ref, got4_ref,
    q0_ref, q1_ref, q2_ref, q3_ref, low_ref, high_ref, after_ref, keep_ref, send_ref,
):
    core, z, y = place()
    own, two, three = (load(r) for r in (own_ref, two_ref, three_ref))
    x = [one_ref[v * NI : v * NI + NI, :] for v in range(NV)]
    one = (x, x, one_ref[80:85, :], one_ref[85:90, :], one_ref[90:95, :])

    def sort(*groups):
        return jax.tree.map(lambda *x: pick(y, x), *groups)

    ups = (own, one, two, three), (three, own, one, two), (two, three, own, one)
    ups = [sort(*group) for group in ups]
    downs = [three, choose(y == 0, two, three), sort(one, two, three)]
    zero = [jnp.zeros((NI, HALF), F32)] * NV
    fs = [zero, ups[0][0]]
    fs.append(f_after(ups[1], fs[1]))
    fs.append(f_after(ups[2], fs[2]))
    us = [None, None, None, zero]
    for n in (3, 2, 1):
        us[n - 1] = g_before(downs[n - 1], fs[n], us[n])
    f, u = sort(*fs), sort(*us)
    is_low = bit_clear(z, 4)
    low, high = ordered(is_low, load(own4_ref), load(got4_ref))
    f, u = choose(is_low, *step_down(low, high, f, u))
    parts = members((q0_ref, q1_ref, q2_ref, q3_ref))
    fs, us = [f], [None, None, None, u]
    for r in range(3):
        fs.append(f_after(parts[r], fs[r]))
    for r in (3, 2, 1):
        us[r - 1] = g_before(parts[r], fs[r], us[r])
    m = lax.rem(z, 4)
    f = [pick(m, [x[v] for x in fs]) for v in range(NV)]
    u = [pick(m, [x[v] for x in us]) for v in range(NV)]
    is_low = core == 0
    low, high = step_down(load(low_ref), load(high_ref), f, u)
    put_states(keep_ref, choose(is_low, low, high))
    put_states(send_ref, choose(is_low, high, low))


def final_kernel(g_ref, resp_ref, mine_ref, other_ref, out_ref, scr, fu_scr, sems):
    even = place()[0] == 0

    def copy(v):
        at = pl.ds(v * PLANE, PLANE)
        return pltpu.make_async_copy(scr.at[at], out_ref.at[at], sems.at[v])

    for v in range(NV):
        x, y = mine_ref[v * 32 : v * 32 + 32, :], other_ref[v * 32 : v * 32 + 32, :]
        fu_scr[v, :, :HALF] = jnp.where(even, x, y)
        fu_scr[v, :, HALF:] = jnp.where(even, y, x)
        a, b = resp_ref[v, 0], resp_ref[v, 1]
        for i in range(NI):
            at = slice(v * PLANE + i * NJ, v * PLANE + i * NJ + NJ)
            f, u = fu_scr[v, i : i + 1, :], fu_scr[v, NI + i : NI + i + 1, :]
            scr[at, :] = g_ref[at, :] + a * f + b * u
        copy(v).start()
    for v in range(NV):
        copy(v).wait()


def swap(x, axis, size, flip):
    return lax.ppermute(x, axis, [(i, i ^ flip) for i in range(size)])


def shift(x, axis, size, by):
    return lax.ppermute(x, axis, [(i, (i + by) % size) for i in range(size)])


def across(x):
    pairs = []
    for q in range(64):
        z = q // 2 % 8
        other = (6 - z if z % 2 == 0 else 8 - z) % 8
        pairs.append((q, q + 2 * (other - z)))
    return lax.ppermute(x, "plane", pairs)


def body(adjoint, forcing, eigen_values, face_masks, line_coeffs, cross_coeffs):
    flat = (NV * PLANE, NK)
    a, f, e = (x.reshape(flat) for x in (adjoint, forcing, eigen_values))
    i_face, j_face = (NV, NJ, NK), (NV, NI, NK)
    w, ia, ib, ja, jb = call(
        faces_kernel, [flat, i_face, i_face, j_face, j_face], a, e, in_hbm=2, name="faces",
        scratch=[
            pltpu.VMEM(flat, F32),
            pltpu.VMEM(flat, F32),
            pltpu.VMEM((NV, 2, PLANE, HALF), F32),
            pltpu.SemaphoreType.DMA((NV, 2)),
        ],
    )
    ia = swap(ia, "line", 4, 1)
    ib = swap(ib, "line", 4, 3)
    ja = swap(ja, "plane", 64, 1)
    jb = lax.ppermute(jb, "plane", [(i, (i + 1 if i % 2 else i - 1) % 64) for i in range(64)])

    halves = (2, NV * PLANE, HALF)
    half, line_resp, maps, cross_resp, halo_resp, co, g, t, x = call(
        prep_kernel,
        [
            line_coeffs.shape[:3] + (HALF,), halves, (64, NK), (NV, 2, NJ, NK), (NV, 4, NJ, NK),
            (16, NK), flat, flat, cross_coeffs.shape,
        ],
        cross_coeffs, face_masks, w, f, line_coeffs, in_hbm=2, name="prep", flops=10**7,
        scratch=[
            pltpu.VMEM(face_masks.shape, face_masks.dtype),
            pltpu.SemaphoreType.DMA((2,)),
        ],
    )
    msg = (176, HALF)
    j_low, j_high, gi, keep, send = call(
        source_kernel, [j_face, j_face, (NV, 2, NJ, NK), msg, msg],
        t, ia, ib, ja, jb, x, halo_resp, co, scratch=[pltpu.VMEM(halves, F32)], name="source",
    )
    got = swap(send, "plane", 64, 1)
    half_flat = (NV * PLANE, HALF)
    layers, small = call(
        layers_kernel, [half_flat, (MAPS + 64, HALF)], keep, got, half, maps,
        scratch=[pltpu.VMEM(half_flat, F32)], name="layers",
    )
    smalls = [small] + [swap(small, "line", 4, d) for d in (1, 2, 3)]
    low, high, chip = call(
        edges_kernel, [msg, msg, msg],
        layers, line_resp, keep, got, *smalls, name="edges",
    )
    quad = [chip] + [swap(chip, "plane", 64, d) for d in (2, 4, 6)]

    local, big = call(
        planes_kernel, [flat, (BIG + 64, NK)],
        line_coeffs, g, halo_resp, j_low, j_high, gi, maps,
        scratch=[pltpu.VMEM(flat, F32)], name="planes", flops=10**7,
    )
    got_big = swap(big, "line", 4, 1)
    last_big = call(plane_pair_kernel, [(LAST + 24, NK)], big, got_big, name="plane_pair")[0]
    got_last_big = swap(last_big, "line", 4, 3)
    solved = call(
        solved_kernel, [flat], local, line_resp, big, got_big, last_big, got_last_big,
        name="solved", flops=10**7,
    )[0]

    own4 = call(quad_kernel, [msg], *quad, big, name="quad")[0]
    got4 = across(own4)
    ring, fore = call(ring_kernel, [msg, (96, HALF)], own4, got4, last_big, name="ring")
    y1, y2, y3 = (
        shift(fore, "plane", 64, 16), shift(ring, "plane", 64, 32), shift(ring, "plane", 64, 48)
    )
    mine, send = call(
        down_kernel, [(160, HALF)] * 2,
        ring, y1, y2, y3, own4, got4, *quad, low, high, solved, name="down",
    )
    other = swap(send, "plane", 64, 1)
    out = call(
        final_kernel, [flat], solved, cross_resp, mine, other, out_hbm=True, name="final",
        scratch=[
            pltpu.VMEM(flat, F32),
            pltpu.VMEM((NV, 2 * NI, NK), F32),
            pltpu.SemaphoreType.DMA((NV,)),
        ],
    )[0]
    return out.reshape(NV, NI, NJ, NK)


def solution(mesh):
    return jax.shard_map(
        body,
        mesh=mesh,
        in_specs=(
            P(None, "line", "plane", None),
            P(None, "line", "plane", None),
            P(None, "line", "plane", None),
            P(None, "plane", None),
            P(None, None, "line", None),
            P(None, None, "plane", None),
        ),
        out_specs=P(None, "line", "plane", None),
        check_vma=False,
    )
```

```python
import jax
import jax.numpy as jnp
from jax import lax
from jax.experimental import pallas as pl
from jax.experimental.pallas import tpu as pltpu
from jax.sharding import PartitionSpec as P

F32 = jnp.float32
NV, NI, NJ, NK = 5, 16, 8, 256
HALF = NK // 2
PLANE = NI * NJ
TILE = (NJ, NK)
MAPS = NV * 16


def rows_of(shape):
    return lax.broadcasted_iota(jnp.int32, shape, len(shape) - 2)


def lanes_of(shape):
    return lax.broadcasted_iota(jnp.int32, shape, len(shape) - 1)


def call(kernel, outs, *args, scratch=(), in_hbm=0, out_hbm=False, name=None, flops=1000):
    outs = [jax.ShapeDtypeStruct(s, F32) for s in outs]
    args = [
        pltpu.with_memory_space_constraint(x, pltpu.HBM) if n < in_hbm else x
        for n, x in enumerate(args)
    ]
    spaces = [pltpu.HBM] * in_hbm + [pltpu.VMEM] * (len(args) - in_hbm)
    return pl.pallas_call(
        kernel,
        out_shape=outs,
        in_specs=[pl.BlockSpec(memory_space=s) for s in spaces],
        out_specs=[pl.BlockSpec(memory_space=pltpu.HBM if out_hbm else pltpu.VMEM)] * len(outs),
        scratch_shapes=list(scratch),
        compiler_params=pltpu.CompilerParams(vmem_limit_bytes=40 * 1024 * 1024),
        cost_estimate=pl.CostEstimate(flops=flops, bytes_accessed=flops, transcendentals=0),
        name=name,
    )(*args)


def place():
    q = lax.axis_index("plane")
    return lax.rem(q, 2), lax.rem(q // 2, 8), q // 16


def pick(p, options):
    out = options[-1]
    for n in reversed(range(len(options) - 1)):
        out = jnp.where(p == n, options[n], out)
    return out


def faces_kernel(
    a_hbm, e_hbm, w_ref, ia_ref, ib_ref, ja_ref, jb_ref, a_scr, e_scr, scr, sems
):
    even_line = lax.rem(lax.axis_index("line"), 2) == 0
    even_plane = lax.rem(lax.axis_index("plane"), 2) == 0

    def fetch(v, n):
        src, dst = ((a_hbm, a_scr), (e_hbm, e_scr))[n]
        at = pl.ds(v * PLANE, PLANE)
        return pltpu.make_async_copy(src.at[at], dst.at[at], sems.at[v, n])

    for v in range(NV):
        for n in range(2):
            fetch(v, n).start()
    for v in range(NV):
        for n in range(2):
            fetch(v, n).wait()
        base = v * PLANE
        for part in range(2):
            lane = slice(part * HALF, part * HALF + HALF)
            w = a_scr[base : base + PLANE, lane] * e_scr[base : base + PLANE, lane]
            w_ref[base : base + PLANE, lane] = w
            scr[v, part] = w
            low, high = w[:NJ], w[PLANE - NJ :]
            ia_ref[v, :, lane] = jnp.where(even_line, high, low)
            ib_ref[v, :, lane] = jnp.where(even_line, low, high)
            low = scr[v, part, pl.ds(0, NI, stride=NJ), :]
            high = scr[v, part, pl.ds(NJ - 1, NI, stride=NJ), :]
            ja_ref[v, :, lane] = jnp.where(even_plane, high, low)
            jb_ref[v, :, lane] = jnp.where(even_plane, low, high)


def prep_kernel(
    x_hbm, m_hbm, w_ref, f_ref, c_ref,
    half_ref, line_resp_ref, maps_ref, cross_resp_ref, halo_resp_ref, weight_ref, co_ref, s_ref, t_ref, x_ref,
    m_ref, sems,
):
    copies = [
        pltpu.make_async_copy(x_hbm, x_ref, sems.at[0]),
        pltpu.make_async_copy(m_hbm, m_ref, sems.at[1]),
    ]
    for copy in copies:
        copy.start()
    even = place()[0] == 0
    for v in range(NV):
        for n in range(6):
            c = c_ref[v, n]
            half_ref[v, n] = jnp.where(even, c[:, :HALF], c[:, HALF:])
    line_coeffs_of(c_ref, line_resp_ref, maps_ref)
    for copy in copies:
        copy.wait()
    cross_coeffs_of(x_ref, cross_resp_ref, halo_resp_ref, weight_ref, co_ref)
    local_source(w_ref, f_ref, m_ref, weight_ref, s_ref, t_ref)


def line_coeffs_of(c_ref, resp_ref, msg_ref):
    row = rows_of(TILE)
    unit = [jnp.where(row == n, 1.0, 0.0) for n in range(4)]
    one, two = [unit[0]] * NV, [unit[1]] * NV
    lower = [[None] * NI for _ in range(NV)]
    for i in range(NI):
        for v in range(NV):
            first, second = (c_ref[v, n, i : i + 1, :] for n in range(2))
            one[v], two[v] = first * one[v] + second * two[v], one[v]
            lower[v][i] = one[v]
    for v in range(NV):
        msg_ref[v * 12 : v * 12 + 2, :] = one[v][0:2]
        msg_ref[v * 12 + 2 : v * 12 + 4, :] = two[v][0:2]
    one, two = [unit[2]] * NV, [unit[3]] * NV
    for i in reversed(range(NI)):
        for v in range(NV):
            first, second, scale = (c_ref[v, n, i : i + 1, :] for n in range(3, 6))
            one[v], two[v] = scale * lower[v][i] + first * one[v] + second * two[v], one[v]
            at = v * PLANE + i * NJ
            for part in range(2):
                resp_ref[part, at : at + NJ, :] = one[v][:, part * HALF : part * HALF + HALF]
    for v in range(NV):
        msg_ref[v * 12 + 4 : v * 12 + 8, :] = one[v][0:4]
        msg_ref[v * 12 + 8 : v * 12 + 12, :] = two[v][0:4]
    msg_ref[60:, :] = jnp.zeros((4, NK), F32)


def up_steps(c):
    row = rows_of(TILE)
    one = jnp.where(row == 0, 0.0, c)
    two = one * pltpu.roll(one, 1, 0)
    return (one, two, two * pltpu.roll(two, 2, 0))


def down_steps(c):
    row = rows_of(TILE)
    one = jnp.where(row == NJ - 1, 0.0, c)
    two = one * pltpu.roll(one, NJ - 1, 0)
    return (one, two, two * pltpu.roll(two, NJ - 2, 0))


def scan_up(x, steps):
    for n, c in zip((1, 2, 4), steps):
        x = x + c * pltpu.roll(x, n, 0)
    return x


def scan_down(x, steps):
    for n, c in zip((1, 2, 4), steps):
        x = x + c * pltpu.roll(x, NJ - n, 0)
    return x


def cross_coeffs_of(x_ref, resp_ref, halo_ref, weight_ref, co_ref):
    row = rows_of(TILE)
    co_ref[15:, :] = jnp.zeros((1, NK), F32)
    for v in range(NV):
        fc, fd, bc, bd = (x_ref[v, n] for n in range(4))
        up, dn = up_steps(fc), down_steps(bc)
        f_resp = scan_up(jnp.where(row == 0, fc, 0.0), up)
        g_resp = scan_down(bd * f_resp, dn)
        b_resp = scan_down(jnp.where(row == NJ - 1, bc, 0.0), dn)
        resp_ref[v, 0] = g_resp
        resp_ref[v, 1] = b_resp
        following = down_steps(pltpu.roll(fc, NJ - 1, 0))
        before = up_steps(pltpu.roll(bc, 1, 0))
        phi = fd * scan_down(jnp.where(row == NJ - 1, 1.0, 0.0), following)
        beta = fd * scan_down(bd * scan_up(jnp.where(row == 0, 1.0, 0.0), before), following)
        weight_ref[v, 0] = phi
        weight_ref[v, 1] = beta
        for n, at, half in ((0, 0, 0.5), (1, NJ - 1, -0.5)):
            halo_ref[v, n] = half * jnp.where(row < 4, phi[at : at + 1], beta[at : at + 1])
        co_ref[v : v + 1, :] = f_resp[NJ - 1 : NJ]
        co_ref[NV + v : NV + v + 1, :] = b_resp[0:1]
        co_ref[2 * NV + v : 2 * NV + v + 1, :] = g_resp[0:1]


def edge_rows(weight_ref, v, s):
    a, b = weight_ref[v, 0] * s, weight_ref[v, 1] * s
    x = jnp.where(rows_of(TILE) < 4, a + pltpu.roll(a, 4, 0), b + pltpu.roll(b, 4, 0))
    x = x + pltpu.roll(x, NJ - 1, 0)
    return x + pltpu.roll(x, NJ - 2, 0)


def local_source(w_ref, f_ref, m_ref, weight_ref, s_ref, t_ref):
    p = lax.axis_index("line")
    row, lane = rows_of(TILE), lanes_of(TILE)
    zero = jnp.zeros(TILE, F32)
    low_mask = jnp.where(p == 0, m_ref[0].astype(F32), zero)
    high_mask = jnp.where(p == 3, m_ref[1].astype(F32), zero)

    def step(v, _):
        base = pl.multiple_of(v * PLANE, PLANE)
        at = [pl.ds(base + i * NJ, NJ) for i in range(NI)]
        w = [w_ref[at[i], :] for i in range(NI)]
        for i in range(NI):
            x = w[i]
            before = low_mask * x if i == 0 else w[i - 1]
            after = high_mask * x if i == NI - 1 else w[i + 1]
            j_before = jnp.where(row == 0, 0.0, pltpu.roll(x, 1, 0))
            j_after = jnp.where(row == NJ - 1, 0.0, pltpu.roll(x, NJ - 1, 0))
            k_before = jnp.where(lane == 0, 0.0, pltpu.roll(x, 1, 1))
            k_after = jnp.where(lane == NK - 1, 0.0, pltpu.roll(x, NK - 1, 1))
            s = f_ref[at[i], :] + 0.5 * (
                (before - after) + (j_before - j_after) + (k_before - k_after)
            )
            s_ref[at[i], :] = s
            t_ref[at[i], :] = edge_rows(weight_ref, v, s)
        return 0

    lax.fori_loop(0, NV, step, 0)


def source_kernel(
    t_in, ia_ref, ib_ref, ja_ref, jb_ref, halo_ref, weight_ref, co_ref,
    low_ref, high_ref, face_ref, keep_ref, send_ref, t_scr,
):
    p, q = lax.axis_index("line"), lax.axis_index("plane")
    even_line, even_plane = lax.rem(p, 2) == 0, lax.rem(q, 2) == 0
    for v in range(NV):
        ia, ib = ia_ref[v], ib_ref[v]
        low = jnp.where(p == 0, 0.0, jnp.where(even_line, ib, ia))
        high = jnp.where(p == 3, 0.0, jnp.where(even_line, ia, ib))
        ja, jb = ja_ref[v], jb_ref[v]
        j_low = jnp.where(q == 0, 0.0, jnp.where(even_plane, jb, ja))
        j_high = jnp.where(q == 63, 0.0, jnp.where(even_plane, ja, jb))
        low_ref[v] = j_low
        high_ref[v] = j_high
        ends = []
        for n, face in enumerate((0.5 * low, -0.5 * high)):
            face_ref[v, n] = face
            ends.append(edge_rows(weight_ref, v, face))
        a, b = halo_ref[v, 0], halo_ref[v, 1]
        for i in range(NI):
            at = slice(v * PLANE + i * NJ, v * PLANE + i * NJ + NJ)
            t = t_in[at, :] + a * j_low[i : i + 1] + b * j_high[i : i + 1]
            if i == 0:
                t = t + ends[0]
            if i == NI - 1:
                t = t + ends[1]
            for half in range(2):
                t_scr[half, at, :] = t[:, half * HALF : half * HALF + HALF]
        for n in range(2):
            a, b = (t_scr[half, pl.ds(v * PLANE + 4 * n, NI, stride=NJ), :] for half in range(2))
            at = slice(v * 32 + n * NI, v * 32 + n * NI + NI)
            keep_ref[at, :] = jnp.where(even_plane, a, b)
            send_ref[at, :] = jnp.where(even_plane, b, a)
    a, b = co_ref[:, :HALF], co_ref[:, HALF:]
    keep_ref[160:, :] = jnp.where(even_plane, a, b)
    send_ref[160:, :] = jnp.where(even_plane, b, a)


def layers_kernel(keep_ref, got_ref, c_ref, maps_ref, out_ref, msg_ref, t_scr):
    even = place()[0] == 0
    tile = (NJ, HALF)
    row = rows_of(tile)
    low, high = ordered(even, [keep_ref[...]], [got_ref[...]])
    low, high = low[0], high[0]
    for v in range(NV):
        for i in range(NI):
            a, b = v * 32 + i, v * 32 + NI + i
            t_scr[v * PLANE + i * NJ : v * PLANE + i * NJ + NJ, :] = jnp.where(
                row == 0,
                low[a : a + 1],
                jnp.where(row == 1, low[b : b + 1], jnp.where(row == 2, high[a : a + 1], high[b : b + 1])),
            )
    ends = local_sweeps(c_ref, t_scr, out_ref, out_ref)
    for v in range(NV):
        for n in range(2):
            a, b = ends[v][2 * n : 2 * n + 2]
            at = v * 16 + n * 8
            msg_ref[at : at + 8, :] = jnp.where(row < 4, a, pltpu.roll(b, 4, 0))
    msg_ref[MAPS:, :] = jnp.where(even, maps_ref[:, :HALF], maps_ref[:, HALF:])


def local_sweeps(c_ref, src_ref, tmp_ref, out_ref):
    zero = jnp.zeros((NJ, src_ref.shape[-1]), F32)
    one, two = [zero] * NV, [zero] * NV
    for i in range(NI):
        for v in range(NV):
            first, second, scale = (c_ref[v, n, i : i + 1, :] for n in range(3))
            at = slice(v * PLANE + i * NJ, v * PLANE + i * NJ + NJ)
            one[v], two[v] = scale * src_ref[at, :] + first * one[v] + second * two[v], one[v]
            tmp_ref[at, :] = one[v]
    ends = list(zip(one, two))
    one, two = [zero] * NV, [zero] * NV
    for i in reversed(range(NI)):
        for v in range(NV):
            first, second, scale = (c_ref[v, n, i : i + 1, :] for n in range(3, 6))
            at = slice(v * PLANE + i * NJ, v * PLANE + i * NJ + NJ)
            one[v], two[v] = scale * tmp_ref[at, :] + first * one[v] + second * two[v], one[v]
            out_ref[at, :] = one[v]
    return [ends[v] + (one[v], two[v]) for v in range(NV)]


def planes_kernel(
    c_ref, x_ref, s_ref, low_ref, high_ref, face_ref, maps_ref, out_ref, msg_ref, g_scr
):
    row = rows_of(TILE)
    for v in range(NV):
        fd, bd = x_ref[v, 1], x_ref[v, 3]
        up, dn = up_steps(x_ref[v, 0]), down_steps(x_ref[v, 2])
        for i in range(NI):
            at = slice(v * PLANE + i * NJ, v * PLANE + i * NJ + NJ)
            low, high = low_ref[v, i : i + 1, :], high_ref[v, i : i + 1, :]
            s = s_ref[at, :] + jnp.where(
                row == 0, 0.5 * low, jnp.where(row == NJ - 1, -0.5 * high, 0.0)
            )
            if i in (0, NI - 1):
                s = s + face_ref[v, 0 if i == 0 else 1]
            g_scr[at, :] = scan_down(bd * scan_up(fd * s, up), dn)
    ends = local_sweeps(c_ref, g_scr, out_ref, out_ref)
    for v in range(NV):
        for n, x in enumerate(ends[v]):
            msg_ref[v * 32 + n * NJ : v * 32 + n * NJ + NJ, :] = x
    msg_ref[BIG:, :] = maps_ref[...]


def maps_of(ref, v, at=MAPS):
    return ref[at + v * 12 : at + v * 12 + 12, :]


def line_pair(p, own, got):
    is_low = lax.rem(p, 2) == 0
    return (
        [jnp.where(is_low, a, b) for a, b in zip(own, got)],
        [jnp.where(is_low, b, a) for a, b in zip(own, got)],
    )


def l_after(m, phi, l):
    return (
        m[0:1] * l[0] + m[1:2] * l[1] + phi[0],
        m[2:3] * l[0] + m[3:4] * l[1] + phi[1],
    )


def u_before(m, beta, l, u):
    return (
        m[4:5] * l[0] + m[5:6] * l[1] + m[6:7] * u[0] + m[7:8] * u[1] + beta[0],
        m[8:9] * l[0] + m[9:10] * l[1] + m[10:11] * u[0] + m[11:12] * u[1] + beta[1],
    )


def pair_states(p, low, high):
    lm, la, lb, lc, ld = low
    hm, ha, hb, hc, hd = high
    phi = l_after(hm, (ha, hb), (la, lb))
    zero = jnp.zeros_like(la)
    beta = u_before(lm, (lc, ld), (zero, zero), u_before(hm, (hc, hd), (la, lb), (zero, zero)))
    upper = p >= 2
    return [jnp.where(upper, a, b) for a, b in zip(beta, phi)]


def pair_gamma(low_m, high_m):
    columns = []
    for c in range(2):
        l = (low_m[c : c + 1], low_m[2 + c : 3 + c])
        a = high_m[4:5] * l[0] + high_m[5:6] * l[1]
        b = high_m[8:9] * l[0] + high_m[9:10] * l[1]
        columns.append(
            (
                low_m[4 + c : 5 + c] + low_m[6:7] * a + low_m[7:8] * b,
                low_m[8 + c : 9 + c] + low_m[10:11] * a + low_m[11:12] * b,
            )
        )
    (raa, rba), (rab, rbb) = columns
    return raa, rab, rba, rbb


def entering(p, low, high, mine, got, gamma):
    upper, is_low = p >= 2, lax.rem(p, 2) == 0
    zero = jnp.zeros_like(mine[0])
    l = [jnp.where(upper, x, zero) for x in got]
    raa, rab, rba, rbb = gamma
    u = (
        got[0] + raa * mine[0] + rab * mine[1],
        got[1] + rba * mine[0] + rbb * mine[1],
    )
    u = [jnp.where(upper, zero, x) for x in u]
    l_high = l_after(low[0], low[1:3], l)
    u_low = u_before(high[0], high[3:5], l_high, u)
    return [jnp.where(is_low, a, b) for a, b in zip(l, l_high)] + [
        jnp.where(is_low, a, b) for a, b in zip(u_low, u)
    ]


def edges_kernel(
    layers_ref, resp_ref, keep_ref, gotc_ref, own_ref, got1_ref, got2_ref, got3_ref,
    low_ref, high_ref, chip_ref,
):
    p, core = lax.axis_index("line"), place()[0]
    refs = (own_ref, got1_ref, got2_ref, got3_ref)
    for v in range(NV):
        rows, maps = [], []
        for r in range(4):
            at = slice(v * 16, v * 16 + 16)
            rows.append(pick(p, [refs[r ^ own][at, :] for own in range(4)]))
            maps.append(pick(p, [maps_of(refs[r ^ own], v) for own in range(4)]))
        part = [[x[n * 4 : n * 4 + 4] for n in range(4)] for x in rows]
        zero = jnp.zeros((4, HALF), F32)
        low = [(zero, zero), (part[0][0], part[0][1])]
        for r in (1, 2):
            low.append(l_after(maps[r], part[r][:2], low[r]))
        high = [None, None, None, (zero, zero)]
        for r in (3, 2, 1):
            high[r - 1] = u_before(maps[r], part[r][2:], low[r], high[r])
        states = [pick(p, [x[t] for x in low]) for t in range(2)]
        states += [pick(p, [x[t] for x in high]) for t in range(2)]
        answers = [resp_ref[core, pl.ds(v * PLANE + n, NI, stride=NJ), :] for n in range(4)]
        for t in range(4):
            x = layers_ref[pl.ds(v * PLANE + t, NI, stride=NJ), :]
            for n in range(4):
                x = x + answers[n] * states[n][t : t + 1]
            at = v * 32 + (t % 2) * NI
            (low_ref, high_ref)[t // 2][at : at + NI, :] = x
    own, other = keep_ref[160:, :], gotc_ref[160:, :]
    low_ref[160:, :] = jnp.where(core == 0, own, other)
    high_ref[160:, :] = jnp.where(core == 0, other, own)
    store(chip_ref, compose(load(low_ref), load(high_ref)))


BIG = NV * 32
LAST = NV * 16


def big_parts(ref, v):
    at = v * 32
    return [maps_of(ref, v, BIG)] + [ref[at + n * NJ : at + n * NJ + NJ, :] for n in range(4)]


def last_parts(ref, v):
    at = v * 16
    return ref[at : at + NJ, :], ref[at + NJ : at + 2 * NJ, :]


def last_gamma(ref, v):
    return [ref[LAST + v * 4 + n : LAST + v * 4 + n + 1, :] for n in range(4)]


def plane_pair_kernel(own_ref, got_ref, out_ref):
    p = lax.axis_index("line")
    for v in range(NV):
        low, high = line_pair(p, big_parts(own_ref, v), big_parts(got_ref, v))
        a, b = pair_states(p, low, high)
        out_ref[v * 16 : v * 16 + NJ, :] = a
        out_ref[v * 16 + NJ : v * 16 + 2 * NJ, :] = b
        for n, x in enumerate(pair_gamma(low[0], high[0])):
            out_ref[LAST + v * 4 + n : LAST + v * 4 + n + 1, :] = x
    out_ref[LAST + 20 :, :] = jnp.zeros((4, NK), F32)


def solved_kernel(local_ref, resp_ref, own_ref, got_ref, mine2_ref, got2_ref, out_ref):
    p = lax.axis_index("line")
    for v in range(NV):
        low, high = line_pair(p, big_parts(own_ref, v), big_parts(got_ref, v))
        mine, got = last_parts(mine2_ref, v), last_parts(got2_ref, v)
        states = entering(p, low, high, mine, got, last_gamma(got2_ref, v))
        for i in range(NI):
            at = v * PLANE + i * NJ
            for part in range(2):
                lane = slice(part * HALF, part * HALF + HALF)
                x = local_ref[at : at + NJ, lane]
                for n in range(4):
                    x = x + resp_ref[part, at + n : at + n + 1, :] * states[n][:, lane]
                out_ref[at : at + NJ, lane] = x


def load(ref):
    phi = [ref[v * 32 : v * 32 + NI, :] for v in range(NV)]
    beta = [ref[v * 32 + NI : v * 32 + 2 * NI, :] for v in range(NV)]
    return (phi, beta, ref[160:165, :], ref[165:170, :], ref[170:175, :])


def store(ref, agg):
    phi, beta, F, B, g = agg
    for v in range(NV):
        ref[v * 32 : v * 32 + NI, :] = phi[v]
        ref[v * 32 + NI : v * 32 + 2 * NI, :] = beta[v]
    ref[160:165, :] = F
    ref[165:170, :] = B
    ref[170:175, :] = g
    ref[175:176, :] = jnp.zeros((1, HALF), F32)


def choose(low_is_own, own, other):
    return jax.tree.map(lambda a, b: jnp.where(low_is_own, a, b), own, other)


def ordered(low_is_own, own, other):
    return choose(low_is_own, own, other), choose(low_is_own, other, own)


def compose(low, high):
    lp, lb, lF, lB, lg = low
    hp, hb, hF, hB, hg = high
    at = [slice(v, v + 1) for v in range(NV)]
    return (
        [hF[at[v]] * lp[v] + hp[v] for v in range(NV)],
        [lb[v] + lB[at[v]] * (hb[v] + hg[at[v]] * lp[v]) for v in range(NV)],
        hF * lF,
        lB * hB,
        lg + lB * hg * lF,
    )


def f_after(agg, f):
    return [agg[2][v : v + 1] * f[v] + agg[0][v] for v in range(NV)]


def g_before(agg, f, u):
    return [agg[1][v] + agg[4][v : v + 1] * f[v] + agg[3][v : v + 1] * u[v] for v in range(NV)]


def bit_clear(z, n):
    return lax.rem(z // n, 2) == 0


def members(refs):
    m = lax.rem(place()[1], 4)
    parts = [load(r) for r in refs]
    return [
        jax.tree.map(lambda *x: pick(m, x), *(parts[r ^ own] for own in range(4)))
        for r in range(4)
    ]


def quad_kernel(*refs):
    a, b, c, d = members(refs[:4])
    store(refs[-1], compose(compose(a, b), compose(c, d)))


def ring_kernel(own_ref, got_ref, after_ref, out_ref, fore_ref):
    agg = compose(*ordered(bit_clear(place()[1], 4), load(own_ref), load(got_ref)))
    store(out_ref, agg)
    last = place()[2] == 3
    for v in range(NV):
        fore_ref[v * NI : v * NI + NI, :] = jnp.where(last, agg[1][v], agg[0][v])
    fore_ref[80:, :] = out_ref[160:, :]


def step_down(low, high, f, u):
    f_high = f_after(low, f)
    u_low = g_before(high, f_high, u)
    return (f, u_low), (f_high, u)


def put_states(ref, states):
    for v in range(NV):
        ref[v * 32 : v * 32 + NI, :] = states[0][v]
        ref[v * 32 + NI : v * 32 + 2 * NI, :] = states[1][v]


def down_kernel(
    own_ref, one_ref, three_ref, two_ref, own4_ref, got4_ref,
    q0_ref, q1_ref, q2_ref, q3_ref, low_ref, high_ref, after_ref, keep_ref, send_ref,
):
    core, z, y = place()
    own, two, three = (load(r) for r in (own_ref, two_ref, three_ref))
    x = [one_ref[v * NI : v * NI + NI, :] for v in range(NV)]
    one = (x, x, one_ref[80:85, :], one_ref[85:90, :], one_ref[90:95, :])

    def sort(*groups):
        return jax.tree.map(lambda *x: pick(y, x), *groups)

    ups = (own, one, two, three), (three, own, one, two), (two, three, own, one)
    ups = [sort(*group) for group in ups]
    downs = [three, choose(y == 0, two, three), sort(one, two, three)]
    zero = [jnp.zeros((NI, HALF), F32)] * NV
    fs = [zero, ups[0][0]]
    fs.append(f_after(ups[1], fs[1]))
    fs.append(f_after(ups[2], fs[2]))
    us = [None, None, None, zero]
    for n in (3, 2, 1):
        us[n - 1] = g_before(downs[n - 1], fs[n], us[n])
    f, u = sort(*fs), sort(*us)
    is_low = bit_clear(z, 4)
    low, high = ordered(is_low, load(own4_ref), load(got4_ref))
    f, u = choose(is_low, *step_down(low, high, f, u))
    parts = members((q0_ref, q1_ref, q2_ref, q3_ref))
    fs, us = [f], [None, None, None, u]
    for r in range(3):
        fs.append(f_after(parts[r], fs[r]))
    for r in (3, 2, 1):
        us[r - 1] = g_before(parts[r], fs[r], us[r])
    m = lax.rem(z, 4)
    f = [pick(m, [x[v] for x in fs]) for v in range(NV)]
    u = [pick(m, [x[v] for x in us]) for v in range(NV)]
    is_low = core == 0
    low, high = step_down(load(low_ref), load(high_ref), f, u)
    put_states(keep_ref, choose(is_low, low, high))
    put_states(send_ref, choose(is_low, high, low))


def final_kernel(g_ref, resp_ref, mine_ref, other_ref, out_ref, scr, fu_scr, sems):
    even = place()[0] == 0

    def copy(v):
        at = pl.ds(v * PLANE, PLANE)
        return pltpu.make_async_copy(scr.at[at], out_ref.at[at], sems.at[v])

    for v in range(NV):
        x, y = mine_ref[v * 32 : v * 32 + 32, :], other_ref[v * 32 : v * 32 + 32, :]
        fu_scr[v, :, :HALF] = jnp.where(even, x, y)
        fu_scr[v, :, HALF:] = jnp.where(even, y, x)
        a, b = resp_ref[v, 0], resp_ref[v, 1]
        for i in range(NI):
            at = slice(v * PLANE + i * NJ, v * PLANE + i * NJ + NJ)
            f, u = fu_scr[v, i : i + 1, :], fu_scr[v, NI + i : NI + i + 1, :]
            scr[at, :] = g_ref[at, :] + a * f + b * u
        copy(v).start()
    for v in range(NV):
        copy(v).wait()


def swap(x, axis, size, flip):
    return lax.ppermute(x, axis, [(i, i ^ flip) for i in range(size)])


def everyone(x, partner):
    places = [(p, q) for p in range(4) for q in range(64)]
    pairs = [(p * 64 + q, partner(p, q)) for p, q in places]
    return lax.ppermute(x, ("line", "plane"), [(n, p * 64 + q) for n, (p, q) in pairs])


def shift(x, axis, size, by):
    return lax.ppermute(x, axis, [(i, (i + by) % size) for i in range(size)])


def across(x):
    pairs = []
    for q in range(64):
        z = q // 2 % 8
        other = (6 - z if z % 2 == 0 else 8 - z) % 8
        pairs.append((q, q + 2 * (other - z)))
    return lax.ppermute(x, "plane", pairs)


def body(adjoint, forcing, eigen_values, face_masks, line_coeffs, cross_coeffs):
    flat = (NV * PLANE, NK)
    a, f, e = (x.reshape(flat) for x in (adjoint, forcing, eigen_values))
    i_face, j_face = (NV, NJ, NK), (NV, NI, NK)
    w, ia, ib, ja, jb = call(
        faces_kernel, [flat, i_face, i_face, j_face, j_face], a, e, in_hbm=2, name="faces",
        scratch=[
            pltpu.VMEM(flat, F32),
            pltpu.VMEM(flat, F32),
            pltpu.VMEM((NV, 2, PLANE, HALF), F32),
            pltpu.SemaphoreType.DMA((NV, 2)),
        ],
    )
    ia = swap(ia, "line", 4, 1)
    ib = everyone(ib, lambda p, q: (3 - p, q) if p in (1, 2) else (p, q ^ 1))
    ja = swap(ja, "plane", 64, 1)
    jb = everyone(jb, lambda p, q: (p ^ 1, q) if q in (0, 63) else (p, q + 1 if q % 2 else q - 1))

    halves = (2, NV * PLANE, HALF)
    half, line_resp, maps, cross_resp, halo_resp, weights, co, s, t, x = call(
        prep_kernel,
        [
            line_coeffs.shape[:3] + (HALF,), halves, (64, NK), (NV, 2, NJ, NK), (NV, 2, NJ, NK),
            (NV, 2, NJ, NK), (16, NK), flat, flat, cross_coeffs.shape,
        ],
        cross_coeffs, face_masks, w, f, line_coeffs, in_hbm=2, name="prep", flops=10**7,
        scratch=[
            pltpu.VMEM(face_masks.shape, face_masks.dtype),
            pltpu.SemaphoreType.DMA((2,)),
        ],
    )
    msg = (176, HALF)
    j_low, j_high, faces, keep, send = call(
        source_kernel, [j_face, j_face, (NV, 2, NJ, NK), msg, msg],
        t, ia, ib, ja, jb, halo_resp, weights, co, scratch=[pltpu.VMEM(halves, F32)], name="source",
    )
    got = swap(send, "plane", 64, 1)
    half_flat = (NV * PLANE, HALF)
    layers, small = call(
        layers_kernel, [half_flat, (MAPS + 64, HALF)], keep, got, half, maps,
        scratch=[pltpu.VMEM(half_flat, F32)], name="layers",
    )
    smalls = [small] + [swap(small, "line", 4, d) for d in (1, 2, 3)]
    low, high, chip = call(
        edges_kernel, [msg, msg, msg],
        layers, line_resp, keep, got, *smalls, name="edges",
    )
    quad = [chip] + [swap(chip, "plane", 64, d) for d in (2, 4, 6)]

    local, big = call(
        planes_kernel, [flat, (BIG + 64, NK)],
        line_coeffs, x, s, j_low, j_high, faces, maps,
        scratch=[pltpu.VMEM(flat, F32)], name="planes", flops=10**7,
    )
    got_big = swap(big, "line", 4, 1)
    last_big = call(plane_pair_kernel, [(LAST + 24, NK)], big, got_big, name="plane_pair")[0]
    got_last_big = swap(last_big, "line", 4, 3)
    solved = call(
        solved_kernel, [flat], local, line_resp, big, got_big, last_big, got_last_big,
        name="solved", flops=10**7,
    )[0]

    own4 = call(quad_kernel, [msg], *quad, big, name="quad")[0]
    got4 = across(own4)
    ring, fore = call(ring_kernel, [msg, (96, HALF)], own4, got4, last_big, name="ring")
    y1, y2, y3 = (
        shift(fore, "plane", 64, 16), shift(ring, "plane", 64, 32), shift(ring, "plane", 64, 48)
    )
    mine, send = call(
        down_kernel, [(160, HALF)] * 2,
        ring, y1, y3, y2, own4, got4, *quad, low, high, solved, name="down",
    )
    other = swap(send, "plane", 64, 1)
    out = call(
        final_kernel, [flat], solved, cross_resp, mine, other, out_hbm=True, name="final",
        scratch=[
            pltpu.VMEM(flat, F32),
            pltpu.VMEM((NV, 2 * NI, NK), F32),
            pltpu.SemaphoreType.DMA((NV,)),
        ],
    )[0]
    return out.reshape(NV, NI, NJ, NK)


def solution(mesh):
    return jax.shard_map(
        body,
        mesh=mesh,
        in_specs=(
            P(None, "line", "plane", None),
            P(None, "line", "plane", None),
            P(None, "line", "plane", None),
            P(None, "plane", None),
            P(None, None, "line", None),
            P(None, None, "plane", None),
        ),
        out_specs=P(None, "line", "plane", None),
        check_vma=False,
    )
```

```python
import jax
import jax.numpy as jnp
from jax import lax
from jax.experimental import pallas as pl
from jax.experimental.pallas import tpu as pltpu
from jax.sharding import PartitionSpec as P

F32 = jnp.float32
NV, NI, NJ, NK = 5, 16, 8, 256
HALF = NK // 2
PLANE = NI * NJ
TILE = (NJ, NK)
MAPS = NV * 16


def rows_of(shape):
    return lax.broadcasted_iota(jnp.int32, shape, len(shape) - 2)


def lanes_of(shape):
    return lax.broadcasted_iota(jnp.int32, shape, len(shape) - 1)


def call(kernel, outs, *args, scratch=(), in_hbm=0, out_hbm=False, name=None, flops=1000):
    outs = [s if isinstance(s, jax.ShapeDtypeStruct) else jax.ShapeDtypeStruct(s, F32) for s in outs]
    args = [
        pltpu.with_memory_space_constraint(x, pltpu.HBM) if n < in_hbm else x
        for n, x in enumerate(args)
    ]
    spaces = [pltpu.HBM] * in_hbm + [pltpu.VMEM] * (len(args) - in_hbm)
    return pl.pallas_call(
        kernel,
        out_shape=outs,
        in_specs=[pl.BlockSpec(memory_space=s) for s in spaces],
        out_specs=[pl.BlockSpec(memory_space=pltpu.HBM if out_hbm else pltpu.VMEM)] * len(outs),
        scratch_shapes=list(scratch),
        compiler_params=pltpu.CompilerParams(vmem_limit_bytes=40 * 1024 * 1024),
        cost_estimate=pl.CostEstimate(flops=flops, bytes_accessed=flops, transcendentals=0),
        name=name,
    )(*args)


def place():
    q = lax.axis_index("plane")
    return lax.rem(q, 2), lax.rem(q // 2, 8), q // 16


def pick(p, options):
    out = options[-1]
    for n in reversed(range(len(options) - 1)):
        out = jnp.where(p == n, options[n], out)
    return out


def faces_kernel(
    a_hbm, e_hbm, x_hbm, m_hbm,
    w_ref, ia_ref, ib_ref, ja_ref, jb_ref, x_ref, m_ref, a_scr, e_scr, scr, sems, more_sems,
):
    even_line = lax.rem(lax.axis_index("line"), 2) == 0
    even_plane = lax.rem(lax.axis_index("plane"), 2) == 0

    def fetch(v, n):
        src, dst = ((a_hbm, a_scr), (e_hbm, e_scr))[n]
        at = pl.ds(v * PLANE, PLANE)
        return pltpu.make_async_copy(src.at[at], dst.at[at], sems.at[v, n])

    for v in range(NV):
        for n in range(2):
            fetch(v, n).start()
    more = [
        pltpu.make_async_copy(x_hbm, x_ref, more_sems.at[0]),
        pltpu.make_async_copy(m_hbm, m_ref, more_sems.at[1]),
    ]
    for copy in more:
        copy.start()
    for v in range(NV):
        for n in range(2):
            fetch(v, n).wait()
        base = v * PLANE
        for part in range(2):
            lane = slice(part * HALF, part * HALF + HALF)
            w = a_scr[base : base + PLANE, lane] * e_scr[base : base + PLANE, lane]
            w_ref[base : base + PLANE, lane] = w
            scr[v, part] = w
            low, high = w[:NJ], w[PLANE - NJ :]
            ia_ref[v, :, lane] = jnp.where(even_line, high, low)
            ib_ref[v, :, lane] = jnp.where(even_line, low, high)
            low = scr[v, part, pl.ds(0, NI, stride=NJ), :]
            high = scr[v, part, pl.ds(NJ - 1, NI, stride=NJ), :]
            ja_ref[v, :, lane] = jnp.where(even_plane, high, low)
            jb_ref[v, :, lane] = jnp.where(even_plane, low, high)
    for copy in more:
        copy.wait()


def prep_kernel(
    x_ref, m_ref, w_ref, f_ref, c_ref,
    half_ref, line_resp_ref, maps_ref, cross_resp_ref, halo_resp_ref, weight_ref, co_ref, s_ref, t_ref,
):
    even = place()[0] == 0
    for v in range(NV):
        for n in range(6):
            c = c_ref[v, n]
            half_ref[v, n] = jnp.where(even, c[:, :HALF], c[:, HALF:])
    line_coeffs_of(c_ref, line_resp_ref, maps_ref)
    cross_coeffs_of(x_ref, cross_resp_ref, halo_resp_ref, weight_ref, co_ref)
    local_source(w_ref, f_ref, m_ref, weight_ref, s_ref, t_ref)


def line_coeffs_of(c_ref, resp_ref, msg_ref):
    row = rows_of(TILE)
    unit = [jnp.where(row == n, 1.0, 0.0) for n in range(4)]
    one, two = [unit[0]] * NV, [unit[1]] * NV
    lower = [[None] * NI for _ in range(NV)]
    for i in range(NI):
        for v in range(NV):
            first, second = (c_ref[v, n, i : i + 1, :] for n in range(2))
            one[v], two[v] = first * one[v] + second * two[v], one[v]
            lower[v][i] = one[v]
    for v in range(NV):
        msg_ref[v * 12 : v * 12 + 2, :] = one[v][0:2]
        msg_ref[v * 12 + 2 : v * 12 + 4, :] = two[v][0:2]
    one, two = [unit[2]] * NV, [unit[3]] * NV
    for i in reversed(range(NI)):
        for v in range(NV):
            first, second, scale = (c_ref[v, n, i : i + 1, :] for n in range(3, 6))
            one[v], two[v] = scale * lower[v][i] + first * one[v] + second * two[v], one[v]
            at = v * PLANE + i * NJ
            for part in range(2):
                resp_ref[part, at : at + NJ, :] = one[v][:, part * HALF : part * HALF + HALF]
    for v in range(NV):
        msg_ref[v * 12 + 4 : v * 12 + 8, :] = one[v][0:4]
        msg_ref[v * 12 + 8 : v * 12 + 12, :] = two[v][0:4]
    msg_ref[60:, :] = jnp.zeros((4, NK), F32)


def up_steps(c):
    row = rows_of(TILE)
    one = jnp.where(row == 0, 0.0, c)
    two = one * pltpu.roll(one, 1, 0)
    return (one, two, two * pltpu.roll(two, 2, 0))


def down_steps(c):
    row = rows_of(TILE)
    one = jnp.where(row == NJ - 1, 0.0, c)
    two = one * pltpu.roll(one, NJ - 1, 0)
    return (one, two, two * pltpu.roll(two, NJ - 2, 0))


def scan_up(x, steps):
    for n, c in zip((1, 2, 4), steps):
        x = x + c * pltpu.roll(x, n, 0)
    return x


def scan_down(x, steps):
    for n, c in zip((1, 2, 4), steps):
        x = x + c * pltpu.roll(x, NJ - n, 0)
    return x


def cross_coeffs_of(x_ref, resp_ref, halo_ref, weight_ref, co_ref):
    row = rows_of(TILE)
    co_ref[15:, :] = jnp.zeros((1, NK), F32)
    for v in range(NV):
        fc, fd, bc, bd = (x_ref[v, n] for n in range(4))
        up, dn = up_steps(fc), down_steps(bc)
        f_resp = scan_up(jnp.where(row == 0, fc, 0.0), up)
        g_resp = scan_down(bd * f_resp, dn)
        b_resp = scan_down(jnp.where(row == NJ - 1, bc, 0.0), dn)
        resp_ref[v, 0] = g_resp
        resp_ref[v, 1] = b_resp
        following = down_steps(pltpu.roll(fc, NJ - 1, 0))
        before = up_steps(pltpu.roll(bc, 1, 0))
        phi = fd * scan_down(jnp.where(row == NJ - 1, 1.0, 0.0), following)
        beta = fd * scan_down(bd * scan_up(jnp.where(row == 0, 1.0, 0.0), before), following)
        weight_ref[v, 0] = phi
        weight_ref[v, 1] = beta
        for n, at, half in ((0, 0, 0.5), (1, NJ - 1, -0.5)):
            halo_ref[v, n] = half * jnp.where(row < 4, phi[at : at + 1], beta[at : at + 1])
        co_ref[v : v + 1, :] = f_resp[NJ - 1 : NJ]
        co_ref[NV + v : NV + v + 1, :] = b_resp[0:1]
        co_ref[2 * NV + v : 2 * NV + v + 1, :] = g_resp[0:1]


def edge_rows(weight_ref, v, s):
    a, b = weight_ref[v, 0] * s, weight_ref[v, 1] * s
    x = jnp.where(rows_of(TILE) < 4, a + pltpu.roll(a, 4, 0), b + pltpu.roll(b, 4, 0))
    x = x + pltpu.roll(x, NJ - 1, 0)
    return x + pltpu.roll(x, NJ - 2, 0)


def local_source(w_ref, f_ref, m_ref, weight_ref, s_ref, t_ref):
    p = lax.axis_index("line")
    row, lane = rows_of(TILE), lanes_of(TILE)
    zero = jnp.zeros(TILE, F32)
    low_mask = jnp.where(p == 0, m_ref[0].astype(F32), zero)
    high_mask = jnp.where(p == 3, m_ref[1].astype(F32), zero)

    def step(v, _):
        base = pl.multiple_of(v * PLANE, PLANE)
        at = [pl.ds(base + i * NJ, NJ) for i in range(NI)]
        w = [w_ref[at[i], :] for i in range(NI)]
        for i in range(NI):
            x = w[i]
            before = low_mask * x if i == 0 else w[i - 1]
            after = high_mask * x if i == NI - 1 else w[i + 1]
            j_before = jnp.where(row == 0, 0.0, pltpu.roll(x, 1, 0))
            j_after = jnp.where(row == NJ - 1, 0.0, pltpu.roll(x, NJ - 1, 0))
            k_before = jnp.where(lane == 0, 0.0, pltpu.roll(x, 1, 1))
            k_after = jnp.where(lane == NK - 1, 0.0, pltpu.roll(x, NK - 1, 1))
            s = f_ref[at[i], :] + 0.5 * (
                (before - after) + (j_before - j_after) + (k_before - k_after)
            )
            s_ref[at[i], :] = s
            t_ref[at[i], :] = edge_rows(weight_ref, v, s)
        return 0

    lax.fori_loop(0, NV, step, 0)


def source_kernel(
    t_in, ia_ref, ib_ref, ja_ref, jb_ref, halo_ref, weight_ref, co_ref,
    low_ref, high_ref, face_ref, keep_ref, send_ref, t_scr,
):
    p, q = lax.axis_index("line"), lax.axis_index("plane")
    even_line, even_plane = lax.rem(p, 2) == 0, lax.rem(q, 2) == 0
    for v in range(NV):
        ia, ib = ia_ref[v], ib_ref[v]
        low = jnp.where(p == 0, 0.0, jnp.where(even_line, ib, ia))
        high = jnp.where(p == 3, 0.0, jnp.where(even_line, ia, ib))
        ja, jb = ja_ref[v], jb_ref[v]
        j_low = jnp.where(q == 0, 0.0, jnp.where(even_plane, jb, ja))
        j_high = jnp.where(q == 63, 0.0, jnp.where(even_plane, ja, jb))
        low_ref[v] = j_low
        high_ref[v] = j_high
        ends = []
        for n, face in enumerate((0.5 * low, -0.5 * high)):
            face_ref[v, n] = face
            ends.append(edge_rows(weight_ref, v, face))
        a, b = halo_ref[v, 0], halo_ref[v, 1]
        for i in range(NI):
            at = slice(v * PLANE + i * NJ, v * PLANE + i * NJ + NJ)
            t = t_in[at, :] + a * j_low[i : i + 1] + b * j_high[i : i + 1]
            if i == 0:
                t = t + ends[0]
            if i == NI - 1:
                t = t + ends[1]
            for half in range(2):
                t_scr[half, at, :] = t[:, half * HALF : half * HALF + HALF]
        for n in range(2):
            a, b = (t_scr[half, pl.ds(v * PLANE + 4 * n, NI, stride=NJ), :] for half in range(2))
            at = slice(v * 32 + n * NI, v * 32 + n * NI + NI)
            keep_ref[at, :] = jnp.where(even_plane, a, b)
            send_ref[at, :] = jnp.where(even_plane, b, a)
    a, b = co_ref[:, :HALF], co_ref[:, HALF:]
    keep_ref[160:, :] = jnp.where(even_plane, a, b)
    send_ref[160:, :] = jnp.where(even_plane, b, a)


def layers_kernel(keep_ref, got_ref, c_ref, maps_ref, out_ref, msg_ref, t_scr):
    even = place()[0] == 0
    tile = (NJ, HALF)
    row = rows_of(tile)
    low, high = ordered(even, [keep_ref[...]], [got_ref[...]])
    low, high = low[0], high[0]
    for v in range(NV):
        for i in range(NI):
            a, b = v * 32 + i, v * 32 + NI + i
            t_scr[v * PLANE + i * NJ : v * PLANE + i * NJ + NJ, :] = jnp.where(
                row == 0,
                low[a : a + 1],
                jnp.where(row == 1, low[b : b + 1], jnp.where(row == 2, high[a : a + 1], high[b : b + 1])),
            )
    ends = local_sweeps(c_ref, t_scr, out_ref, out_ref)
    for v in range(NV):
        for n in range(2):
            a, b = ends[v][2 * n : 2 * n + 2]
            at = v * 16 + n * 8
            msg_ref[at : at + 8, :] = jnp.where(row < 4, a, pltpu.roll(b, 4, 0))
    msg_ref[MAPS:, :] = jnp.where(even, maps_ref[:, :HALF], maps_ref[:, HALF:])


def local_sweeps(c_ref, src_ref, tmp_ref, out_ref):
    zero = jnp.zeros((NJ, src_ref.shape[-1]), F32)
    one, two = [zero] * NV, [zero] * NV
    for i in range(NI):
        for v in range(NV):
            first, second, scale = (c_ref[v, n, i : i + 1, :] for n in range(3))
            at = slice(v * PLANE + i * NJ, v * PLANE + i * NJ + NJ)
            one[v], two[v] = scale * src_ref[at, :] + first * one[v] + second * two[v], one[v]
            tmp_ref[at, :] = one[v]
    ends = list(zip(one, two))
    one, two = [zero] * NV, [zero] * NV
    for i in reversed(range(NI)):
        for v in range(NV):
            first, second, scale = (c_ref[v, n, i : i + 1, :] for n in range(3, 6))
            at = slice(v * PLANE + i * NJ, v * PLANE + i * NJ + NJ)
            one[v], two[v] = scale * tmp_ref[at, :] + first * one[v] + second * two[v], one[v]
            out_ref[at, :] = one[v]
    return [ends[v] + (one[v], two[v]) for v in range(NV)]


def planes_kernel(
    c_ref, x_ref, s_ref, low_ref, high_ref, face_ref, maps_ref, out_ref, msg_ref, g_scr
):
    row = rows_of(TILE)
    for v in range(NV):
        fd, bd = x_ref[v, 1], x_ref[v, 3]
        up, dn = up_steps(x_ref[v, 0]), down_steps(x_ref[v, 2])
        for i in range(NI):
            at = slice(v * PLANE + i * NJ, v * PLANE + i * NJ + NJ)
            low, high = low_ref[v, i : i + 1, :], high_ref[v, i : i + 1, :]
            s = s_ref[at, :] + jnp.where(
                row == 0, 0.5 * low, jnp.where(row == NJ - 1, -0.5 * high, 0.0)
            )
            if i in (0, NI - 1):
                s = s + face_ref[v, 0 if i == 0 else 1]
            g_scr[at, :] = scan_down(bd * scan_up(fd * s, up), dn)
    ends = local_sweeps(c_ref, g_scr, out_ref, out_ref)
    for v in range(NV):
        for n, x in enumerate(ends[v]):
            msg_ref[v * 32 + n * NJ : v * 32 + n * NJ + NJ, :] = x
    msg_ref[BIG:, :] = maps_ref[...]


def maps_of(ref, v, at=MAPS):
    return ref[at + v * 12 : at + v * 12 + 12, :]


def line_pair(p, own, got):
    is_low = lax.rem(p, 2) == 0
    return (
        [jnp.where(is_low, a, b) for a, b in zip(own, got)],
        [jnp.where(is_low, b, a) for a, b in zip(own, got)],
    )


def l_after(m, phi, l):
    return (
        m[0:1] * l[0] + m[1:2] * l[1] + phi[0],
        m[2:3] * l[0] + m[3:4] * l[1] + phi[1],
    )


def u_before(m, beta, l, u):
    return (
        m[4:5] * l[0] + m[5:6] * l[1] + m[6:7] * u[0] + m[7:8] * u[1] + beta[0],
        m[8:9] * l[0] + m[9:10] * l[1] + m[10:11] * u[0] + m[11:12] * u[1] + beta[1],
    )


def pair_states(p, low, high):
    lm, la, lb, lc, ld = low
    hm, ha, hb, hc, hd = high
    phi = l_after(hm, (ha, hb), (la, lb))
    zero = jnp.zeros_like(la)
    beta = u_before(lm, (lc, ld), (zero, zero), u_before(hm, (hc, hd), (la, lb), (zero, zero)))
    upper = p >= 2
    return [jnp.where(upper, a, b) for a, b in zip(beta, phi)]


def pair_gamma(low_m, high_m):
    columns = []
    for c in range(2):
        l = (low_m[c : c + 1], low_m[2 + c : 3 + c])
        a = high_m[4:5] * l[0] + high_m[5:6] * l[1]
        b = high_m[8:9] * l[0] + high_m[9:10] * l[1]
        columns.append(
            (
                low_m[4 + c : 5 + c] + low_m[6:7] * a + low_m[7:8] * b,
                low_m[8 + c : 9 + c] + low_m[10:11] * a + low_m[11:12] * b,
            )
        )
    (raa, rba), (rab, rbb) = columns
    return raa, rab, rba, rbb


def entering(p, low, high, mine, got, gamma):
    upper, is_low = p >= 2, lax.rem(p, 2) == 0
    zero = jnp.zeros_like(mine[0])
    l = [jnp.where(upper, x, zero) for x in got]
    raa, rab, rba, rbb = gamma
    u = (
        got[0] + raa * mine[0] + rab * mine[1],
        got[1] + rba * mine[0] + rbb * mine[1],
    )
    u = [jnp.where(upper, zero, x) for x in u]
    l_high = l_after(low[0], low[1:3], l)
    u_low = u_before(high[0], high[3:5], l_high, u)
    return [jnp.where(is_low, a, b) for a, b in zip(l, l_high)] + [
        jnp.where(is_low, a, b) for a, b in zip(u_low, u)
    ]


def edges_kernel(
    layers_ref, resp_ref, keep_ref, gotc_ref, own_ref, got1_ref, got2_ref, got3_ref,
    low_ref, high_ref, chip_ref,
):
    p, core = lax.axis_index("line"), place()[0]
    refs = (own_ref, got1_ref, got2_ref, got3_ref)
    for v in range(NV):
        rows, maps = [], []
        for r in range(4):
            at = slice(v * 16, v * 16 + 16)
            rows.append(pick(p, [refs[r ^ own][at, :] for own in range(4)]))
            maps.append(pick(p, [maps_of(refs[r ^ own], v) for own in range(4)]))
        part = [[x[n * 4 : n * 4 + 4] for n in range(4)] for x in rows]
        zero = jnp.zeros((4, HALF), F32)
        low = [(zero, zero), (part[0][0], part[0][1])]
        for r in (1, 2):
            low.append(l_after(maps[r], part[r][:2], low[r]))
        high = [None, None, None, (zero, zero)]
        for r in (3, 2, 1):
            high[r - 1] = u_before(maps[r], part[r][2:], low[r], high[r])
        states = [pick(p, [x[t] for x in low]) for t in range(2)]
        states += [pick(p, [x[t] for x in high]) for t in range(2)]
        answers = [resp_ref[core, pl.ds(v * PLANE + n, NI, stride=NJ), :] for n in range(4)]
        for t in range(4):
            x = layers_ref[pl.ds(v * PLANE + t, NI, stride=NJ), :]
            for n in range(4):
                x = x + answers[n] * states[n][t : t + 1]
            at = v * 32 + (t % 2) * NI
            (low_ref, high_ref)[t // 2][at : at + NI, :] = x
    own, other = keep_ref[160:, :], gotc_ref[160:, :]
    low_ref[160:, :] = jnp.where(core == 0, own, other)
    high_ref[160:, :] = jnp.where(core == 0, other, own)
    store(chip_ref, compose(load(low_ref), load(high_ref)))


BIG = NV * 32
LAST = NV * 16


def big_parts(ref, v):
    at = v * 32
    return [maps_of(ref, v, BIG)] + [ref[at + n * NJ : at + n * NJ + NJ, :] for n in range(4)]


def last_parts(ref, v):
    at = v * 16
    return ref[at : at + NJ, :], ref[at + NJ : at + 2 * NJ, :]


def last_gamma(ref, v):
    return [ref[LAST + v * 4 + n : LAST + v * 4 + n + 1, :] for n in range(4)]


def plane_pair_kernel(own_ref, got_ref, out_ref):
    p = lax.axis_index("line")
    for v in range(NV):
        low, high = line_pair(p, big_parts(own_ref, v), big_parts(got_ref, v))
        a, b = pair_states(p, low, high)
        out_ref[v * 16 : v * 16 + NJ, :] = a
        out_ref[v * 16 + NJ : v * 16 + 2 * NJ, :] = b
        for n, x in enumerate(pair_gamma(low[0], high[0])):
            out_ref[LAST + v * 4 + n : LAST + v * 4 + n + 1, :] = x
    out_ref[LAST + 20 :, :] = jnp.zeros((4, NK), F32)


def solved_kernel(local_ref, resp_ref, own_ref, got_ref, mine2_ref, got2_ref, out_ref):
    p = lax.axis_index("line")
    for v in range(NV):
        low, high = line_pair(p, big_parts(own_ref, v), big_parts(got_ref, v))
        mine, got = last_parts(mine2_ref, v), last_parts(got2_ref, v)
        states = entering(p, low, high, mine, got, last_gamma(got2_ref, v))
        for i in range(NI):
            at = v * PLANE + i * NJ
            for part in range(2):
                lane = slice(part * HALF, part * HALF + HALF)
                x = local_ref[at : at + NJ, lane]
                for n in range(4):
                    x = x + resp_ref[part, at + n : at + n + 1, :] * states[n][:, lane]
                out_ref[at : at + NJ, lane] = x


def load(ref):
    phi = [ref[v * 32 : v * 32 + NI, :] for v in range(NV)]
    beta = [ref[v * 32 + NI : v * 32 + 2 * NI, :] for v in range(NV)]
    return (phi, beta, ref[160:165, :], ref[165:170, :], ref[170:175, :])


def store(ref, agg):
    phi, beta, F, B, g = agg
    for v in range(NV):
        ref[v * 32 : v * 32 + NI, :] = phi[v]
        ref[v * 32 + NI : v * 32 + 2 * NI, :] = beta[v]
    ref[160:165, :] = F
    ref[165:170, :] = B
    ref[170:175, :] = g
    ref[175:176, :] = jnp.zeros((1, HALF), F32)


def choose(low_is_own, own, other):
    return jax.tree.map(lambda a, b: jnp.where(low_is_own, a, b), own, other)


def ordered(low_is_own, own, other):
    return choose(low_is_own, own, other), choose(low_is_own, other, own)


def compose(low, high):
    lp, lb, lF, lB, lg = low
    hp, hb, hF, hB, hg = high
    at = [slice(v, v + 1) for v in range(NV)]
    return (
        [hF[at[v]] * lp[v] + hp[v] for v in range(NV)],
        [lb[v] + lB[at[v]] * (hb[v] + hg[at[v]] * lp[v]) for v in range(NV)],
        hF * lF,
        lB * hB,
        lg + lB * hg * lF,
    )


def f_after(agg, f):
    return [agg[2][v : v + 1] * f[v] + agg[0][v] for v in range(NV)]


def g_before(agg, f, u):
    return [agg[1][v] + agg[4][v : v + 1] * f[v] + agg[3][v : v + 1] * u[v] for v in range(NV)]


def bit_clear(z, n):
    return lax.rem(z // n, 2) == 0


def members(refs):
    m = lax.rem(place()[1], 4)
    parts = [load(r) for r in refs]
    return [
        jax.tree.map(lambda *x: pick(m, x), *(parts[r ^ own] for own in range(4)))
        for r in range(4)
    ]


def quad_kernel(*refs):
    a, b, c, d = members(refs[:4])
    store(refs[-1], compose(compose(a, b), compose(c, d)))


def ring_kernel(own_ref, got_ref, after_ref, out_ref, fore_ref):
    agg = compose(*ordered(bit_clear(place()[1], 4), load(own_ref), load(got_ref)))
    store(out_ref, agg)
    last = place()[2] == 3
    for v in range(NV):
        fore_ref[v * NI : v * NI + NI, :] = jnp.where(last, agg[1][v], agg[0][v])
    fore_ref[80:, :] = out_ref[160:, :]


def step_down(low, high, f, u):
    f_high = f_after(low, f)
    u_low = g_before(high, f_high, u)
    return (f, u_low), (f_high, u)


def put_states(ref, states):
    for v in range(NV):
        ref[v * 32 : v * 32 + NI, :] = states[0][v]
        ref[v * 32 + NI : v * 32 + 2 * NI, :] = states[1][v]


def down_kernel(
    own_ref, one_ref, three_ref, two_ref, own4_ref, got4_ref,
    q0_ref, q1_ref, q2_ref, q3_ref, low_ref, high_ref, after_ref, keep_ref, send_ref,
):
    core, z, y = place()
    own, two, three = (load(r) for r in (own_ref, two_ref, three_ref))
    x = [one_ref[v * NI : v * NI + NI, :] for v in range(NV)]
    one = (x, x, one_ref[80:85, :], one_ref[85:90, :], one_ref[90:95, :])

    def sort(*groups):
        return jax.tree.map(lambda *x: pick(y, x), *groups)

    ups = (own, one, two, three), (three, own, one, two), (two, three, own, one)
    ups = [sort(*group) for group in ups]
    downs = [three, choose(y == 0, two, three), sort(one, two, three)]
    zero = [jnp.zeros((NI, HALF), F32)] * NV
    fs = [zero, ups[0][0]]
    fs.append(f_after(ups[1], fs[1]))
    fs.append(f_after(ups[2], fs[2]))
    us = [None, None, None, zero]
    for n in (3, 2, 1):
        us[n - 1] = g_before(downs[n - 1], fs[n], us[n])
    f, u = sort(*fs), sort(*us)
    is_low = bit_clear(z, 4)
    low, high = ordered(is_low, load(own4_ref), load(got4_ref))
    f, u = choose(is_low, *step_down(low, high, f, u))
    parts = members((q0_ref, q1_ref, q2_ref, q3_ref))
    fs, us = [f], [None, None, None, u]
    for r in range(3):
        fs.append(f_after(parts[r], fs[r]))
    for r in (3, 2, 1):
        us[r - 1] = g_before(parts[r], fs[r], us[r])
    m = lax.rem(z, 4)
    f = [pick(m, [x[v] for x in fs]) for v in range(NV)]
    u = [pick(m, [x[v] for x in us]) for v in range(NV)]
    is_low = core == 0
    low, high = step_down(load(low_ref), load(high_ref), f, u)
    put_states(keep_ref, choose(is_low, low, high))
    put_states(send_ref, choose(is_low, high, low))


def final_kernel(g_ref, resp_ref, mine_ref, other_ref, out_ref, scr, fu_scr, sems):
    even = place()[0] == 0

    def copy(v):
        at = pl.ds(v * PLANE, PLANE)
        return pltpu.make_async_copy(scr.at[at], out_ref.at[at], sems.at[v])

    for v in range(NV):
        x, y = mine_ref[v * 32 : v * 32 + 32, :], other_ref[v * 32 : v * 32 + 32, :]
        fu_scr[v, :, :HALF] = jnp.where(even, x, y)
        fu_scr[v, :, HALF:] = jnp.where(even, y, x)
        a, b = resp_ref[v, 0], resp_ref[v, 1]
        for i in range(NI):
            at = slice(v * PLANE + i * NJ, v * PLANE + i * NJ + NJ)
            f, u = fu_scr[v, i : i + 1, :], fu_scr[v, NI + i : NI + i + 1, :]
            scr[at, :] = g_ref[at, :] + a * f + b * u
        copy(v).start()
    for v in range(NV):
        copy(v).wait()


def swap(x, axis, size, flip):
    return lax.ppermute(x, axis, [(i, i ^ flip) for i in range(size)])


def everyone(x, partner):
    places = [(p, q) for p in range(4) for q in range(64)]
    pairs = [(p * 64 + q, partner(p, q)) for p, q in places]
    return lax.ppermute(x, ("line", "plane"), [(n, p * 64 + q) for n, (p, q) in pairs])


def shift(x, axis, size, by):
    return lax.ppermute(x, axis, [(i, (i + by) % size) for i in range(size)])


def across(x):
    pairs = []
    for q in range(64):
        z = q // 2 % 8
        other = (6 - z if z % 2 == 0 else 8 - z) % 8
        pairs.append((q, q + 2 * (other - z)))
    return lax.ppermute(x, "plane", pairs)


def body(adjoint, forcing, eigen_values, face_masks, line_coeffs, cross_coeffs):
    flat = (NV * PLANE, NK)
    a, f, e = (x.reshape(flat) for x in (adjoint, forcing, eigen_values))
    i_face, j_face = (NV, NJ, NK), (NV, NI, NK)
    masks = jax.ShapeDtypeStruct(face_masks.shape, face_masks.dtype)
    w, ia, ib, ja, jb, x, m = call(
        faces_kernel, [flat, i_face, i_face, j_face, j_face, cross_coeffs.shape, masks],
        a, e, cross_coeffs, face_masks, in_hbm=4, name="faces",
        scratch=[
            pltpu.VMEM(flat, F32),
            pltpu.VMEM(flat, F32),
            pltpu.VMEM((NV, 2, PLANE, HALF), F32),
            pltpu.SemaphoreType.DMA((NV, 2)),
            pltpu.SemaphoreType.DMA((2,)),
        ],
    )
    ia = swap(ia, "line", 4, 1)
    ib = everyone(ib, lambda p, q: (3 - p, q) if p in (1, 2) else (p, q ^ 1))
    ja = swap(ja, "plane", 64, 1)
    jb = everyone(jb, lambda p, q: (p ^ 1, q) if q in (0, 63) else (p, q + 1 if q % 2 else q - 1))

    halves = (2, NV * PLANE, HALF)
    half, line_resp, maps, cross_resp, halo_resp, weights, co, s, t = call(
        prep_kernel,
        [
            line_coeffs.shape[:3] + (HALF,), halves, (64, NK), (NV, 2, NJ, NK), (NV, 2, NJ, NK),
            (NV, 2, NJ, NK), (16, NK), flat, flat,
        ],
        x, m, w, f, line_coeffs, name="prep", flops=10**7,
    )
    msg = (176, HALF)
    j_low, j_high, faces, keep, send = call(
        source_kernel, [j_face, j_face, (NV, 2, NJ, NK), msg, msg],
        t, ia, ib, ja, jb, halo_resp, weights, co, scratch=[pltpu.VMEM(halves, F32)], name="source",
    )
    got = swap(send, "plane", 64, 1)
    half_flat = (NV * PLANE, HALF)
    layers, small = call(
        layers_kernel, [half_flat, (MAPS + 64, HALF)], keep, got, half, maps,
        scratch=[pltpu.VMEM(half_flat, F32)], name="layers",
    )
    smalls = [small] + [swap(small, "line", 4, d) for d in (1, 2, 3)]
    low, high, chip = call(
        edges_kernel, [msg, msg, msg],
        layers, line_resp, keep, got, *smalls, name="edges",
    )
    quad = [chip] + [swap(chip, "plane", 64, d) for d in (2, 4, 6)]

    local, big = call(
        planes_kernel, [flat, (BIG + 64, NK)],
        line_coeffs, x, s, j_low, j_high, faces, maps,
        scratch=[pltpu.VMEM(flat, F32)], name="planes", flops=10**7,
    )
    got_big = swap(big, "line", 4, 1)
    last_big = call(plane_pair_kernel, [(LAST + 24, NK)], big, got_big, name="plane_pair")[0]
    got_last_big = swap(last_big, "line", 4, 3)
    solved = call(
        solved_kernel, [flat], local, line_resp, big, got_big, last_big, got_last_big,
        name="solved", flops=10**7,
    )[0]

    own4 = call(quad_kernel, [msg], *quad, big, name="quad")[0]
    got4 = across(own4)
    ring, fore = call(ring_kernel, [msg, (96, HALF)], own4, got4, last_big, name="ring")
    y1, y2, y3 = (
        shift(fore, "plane", 64, 16), shift(ring, "plane", 64, 32), shift(ring, "plane", 64, 48)
    )
    mine, send = call(
        down_kernel, [(160, HALF)] * 2,
        ring, y1, y3, y2, own4, got4, *quad, low, high, solved, name="down",
    )
    other = swap(send, "plane", 64, 1)
    out = call(
        final_kernel, [flat], solved, cross_resp, mine, other, out_hbm=True, name="final",
        scratch=[
            pltpu.VMEM(flat, F32),
            pltpu.VMEM((NV, 2 * NI, NK), F32),
            pltpu.SemaphoreType.DMA((NV,)),
        ],
    )[0]
    return out.reshape(NV, NI, NJ, NK)


def solution(mesh):
    return jax.shard_map(
        body,
        mesh=mesh,
        in_specs=(
            P(None, "line", "plane", None),
            P(None, "line", "plane", None),
            P(None, "line", "plane", None),
            P(None, "plane", None),
            P(None, None, "line", None),
            P(None, None, "plane", None),
        ),
        out_specs=P(None, "line", "plane", None),
        check_vma=False,
    )
```

```python
import jax
import jax.numpy as jnp
from jax import lax
from jax.experimental import pallas as pl
from jax.experimental.pallas import tpu as pltpu
from jax.sharding import PartitionSpec as P

F32 = jnp.float32
NV, NI, NJ, NK = 5, 16, 8, 256
HALF = NK // 2
PLANE = NI * NJ
TILE = (NJ, NK)
MAPS = NV * 16


def rows_of(shape):
    return lax.broadcasted_iota(jnp.int32, shape, len(shape) - 2)


def lanes_of(shape):
    return lax.broadcasted_iota(jnp.int32, shape, len(shape) - 1)


def call(kernel, outs, *args, scratch=(), in_hbm=0, out_hbm=False, name=None, flops=1000):
    outs = [s if isinstance(s, jax.ShapeDtypeStruct) else jax.ShapeDtypeStruct(s, F32) for s in outs]
    args = [
        pltpu.with_memory_space_constraint(x, pltpu.HBM) if n < in_hbm else x
        for n, x in enumerate(args)
    ]
    spaces = [pltpu.HBM] * in_hbm + [pltpu.VMEM] * (len(args) - in_hbm)
    return pl.pallas_call(
        kernel,
        out_shape=outs,
        in_specs=[pl.BlockSpec(memory_space=s) for s in spaces],
        out_specs=[pl.BlockSpec(memory_space=pltpu.HBM if out_hbm else pltpu.VMEM)] * len(outs),
        scratch_shapes=list(scratch),
        compiler_params=pltpu.CompilerParams(vmem_limit_bytes=40 * 1024 * 1024),
        cost_estimate=pl.CostEstimate(flops=flops, bytes_accessed=flops, transcendentals=0),
        name=name,
    )(*args)


def place():
    q = lax.axis_index("plane")
    return lax.rem(q, 2), lax.rem(q // 2, 8), q // 16


def pick(p, options):
    out = options[-1]
    for n in reversed(range(len(options) - 1)):
        out = jnp.where(p == n, options[n], out)
    return out


def faces_kernel(
    a_hbm, e_hbm, x_hbm, m_hbm,
    w_ref, ia_ref, ib_ref, ja_ref, jb_ref, x_ref, m_ref, a_scr, e_scr, scr, sems, more_sems,
):
    even_line = lax.rem(lax.axis_index("line"), 2) == 0
    even_plane = lax.rem(lax.axis_index("plane"), 2) == 0

    def fetch(v, n):
        src, dst = ((a_hbm, a_scr), (e_hbm, e_scr))[n % 2]
        at = pl.ds(v * PLANE + n // 2 * (PLANE // 2), PLANE // 2)
        return pltpu.make_async_copy(src.at[at], dst.at[at], sems.at[v, n])

    for v in range(NV):
        for n in range(4):
            fetch(v, n).start()
    more = [
        pltpu.make_async_copy(x_hbm, x_ref, more_sems.at[0]),
        pltpu.make_async_copy(m_hbm, m_ref, more_sems.at[1]),
    ]
    for copy in more:
        copy.start()
    for v in range(NV):
        for n in range(4):
            fetch(v, n).wait()
        base = v * PLANE
        for part in range(2):
            lane = slice(part * HALF, part * HALF + HALF)
            w = a_scr[base : base + PLANE, lane] * e_scr[base : base + PLANE, lane]
            w_ref[base : base + PLANE, lane] = w
            scr[v, part] = w
            low, high = w[:NJ], w[PLANE - NJ :]
            ia_ref[v, :, lane] = jnp.where(even_line, high, low)
            ib_ref[v, :, lane] = jnp.where(even_line, low, high)
            low = scr[v, part, pl.ds(0, NI, stride=NJ), :]
            high = scr[v, part, pl.ds(NJ - 1, NI, stride=NJ), :]
            ja_ref[v, :, lane] = jnp.where(even_plane, high, low)
            jb_ref[v, :, lane] = jnp.where(even_plane, low, high)
    for copy in more:
        copy.wait()


def prep_kernel(
    x_ref, m_ref, w_ref, f_ref, c_ref,
    half_ref, line_resp_ref, maps_ref, cross_resp_ref, halo_resp_ref, weight_ref, co_ref, s_ref, t_ref,
):
    even = place()[0] == 0
    for v in range(NV):
        for n in range(6):
            c = c_ref[v, n]
            half_ref[v, n] = jnp.where(even, c[:, :HALF], c[:, HALF:])
    line_coeffs_of(c_ref, line_resp_ref, maps_ref)
    cross_coeffs_of(x_ref, cross_resp_ref, halo_resp_ref, weight_ref, co_ref)
    local_source(w_ref, f_ref, m_ref, weight_ref, s_ref, t_ref)


def line_coeffs_of(c_ref, resp_ref, msg_ref):
    row = rows_of(TILE)
    unit = [jnp.where(row == n, 1.0, 0.0) for n in range(4)]
    one, two = [unit[0]] * NV, [unit[1]] * NV
    lower = [[None] * NI for _ in range(NV)]
    for i in range(NI):
        for v in range(NV):
            first, second = (c_ref[v, n, i : i + 1, :] for n in range(2))
            one[v], two[v] = first * one[v] + second * two[v], one[v]
            lower[v][i] = one[v]
    for v in range(NV):
        msg_ref[v * 12 : v * 12 + 2, :] = one[v][0:2]
        msg_ref[v * 12 + 2 : v * 12 + 4, :] = two[v][0:2]
    one, two = [unit[2]] * NV, [unit[3]] * NV
    for i in reversed(range(NI)):
        for v in range(NV):
            first, second, scale = (c_ref[v, n, i : i + 1, :] for n in range(3, 6))
            one[v], two[v] = scale * lower[v][i] + first * one[v] + second * two[v], one[v]
            at = v * PLANE + i * NJ
            for part in range(2):
                resp_ref[part, at : at + NJ, :] = one[v][:, part * HALF : part * HALF + HALF]
    for v in range(NV):
        msg_ref[v * 12 + 4 : v * 12 + 8, :] = one[v][0:4]
        msg_ref[v * 12 + 8 : v * 12 + 12, :] = two[v][0:4]
    msg_ref[60:, :] = jnp.zeros((4, NK), F32)


def up_steps(c):
    row = rows_of(TILE)
    one = jnp.where(row == 0, 0.0, c)
    two = one * pltpu.roll(one, 1, 0)
    return (one, two, two * pltpu.roll(two, 2, 0))


def down_steps(c):
    row = rows_of(TILE)
    one = jnp.where(row == NJ - 1, 0.0, c)
    two = one * pltpu.roll(one, NJ - 1, 0)
    return (one, two, two * pltpu.roll(two, NJ - 2, 0))


def scan_up(x, steps):
    for n, c in zip((1, 2, 4), steps):
        x = x + c * pltpu.roll(x, n, 0)
    return x


def scan_down(x, steps):
    for n, c in zip((1, 2, 4), steps):
        x = x + c * pltpu.roll(x, NJ - n, 0)
    return x


def cross_coeffs_of(x_ref, resp_ref, halo_ref, weight_ref, co_ref):
    row = rows_of(TILE)
    co_ref[15:, :] = jnp.zeros((1, NK), F32)
    for v in range(NV):
        fc, fd, bc, bd = (x_ref[v, n] for n in range(4))
        up, dn = up_steps(fc), down_steps(bc)
        f_resp = scan_up(jnp.where(row == 0, fc, 0.0), up)
        g_resp = scan_down(bd * f_resp, dn)
        b_resp = scan_down(jnp.where(row == NJ - 1, bc, 0.0), dn)
        resp_ref[v, 0] = g_resp
        resp_ref[v, 1] = b_resp
        following = down_steps(pltpu.roll(fc, NJ - 1, 0))
        before = up_steps(pltpu.roll(bc, 1, 0))
        phi = fd * scan_down(jnp.where(row == NJ - 1, 1.0, 0.0), following)
        beta = fd * scan_down(bd * scan_up(jnp.where(row == 0, 1.0, 0.0), before), following)
        weight_ref[v, 0] = phi
        weight_ref[v, 1] = beta
        for n, at, half in ((0, 0, 0.5), (1, NJ - 1, -0.5)):
            halo_ref[v, n] = half * jnp.where(row < 4, phi[at : at + 1], beta[at : at + 1])
        co_ref[v : v + 1, :] = f_resp[NJ - 1 : NJ]
        co_ref[NV + v : NV + v + 1, :] = b_resp[0:1]
        co_ref[2 * NV + v : 2 * NV + v + 1, :] = g_resp[0:1]


def edge_rows(weight_ref, v, s):
    a, b = weight_ref[v, 0] * s, weight_ref[v, 1] * s
    x = jnp.where(rows_of(TILE) < 4, a + pltpu.roll(a, 4, 0), b + pltpu.roll(b, 4, 0))
    x = x + pltpu.roll(x, NJ - 1, 0)
    return x + pltpu.roll(x, NJ - 2, 0)


def local_source(w_ref, f_ref, m_ref, weight_ref, s_ref, t_ref):
    p = lax.axis_index("line")
    row, lane = rows_of(TILE), lanes_of(TILE)
    zero = jnp.zeros(TILE, F32)
    low_mask = jnp.where(p == 0, m_ref[0].astype(F32), zero)
    high_mask = jnp.where(p == 3, m_ref[1].astype(F32), zero)

    def step(v, _):
        base = pl.multiple_of(v * PLANE, PLANE)
        at = [pl.ds(base + i * NJ, NJ) for i in range(NI)]
        w = [w_ref[at[i], :] for i in range(NI)]
        for i in range(NI):
            x = w[i]
            before = low_mask * x if i == 0 else w[i - 1]
            after = high_mask * x if i == NI - 1 else w[i + 1]
            j_before = jnp.where(row == 0, 0.0, pltpu.roll(x, 1, 0))
            j_after = jnp.where(row == NJ - 1, 0.0, pltpu.roll(x, NJ - 1, 0))
            k_before = jnp.where(lane == 0, 0.0, pltpu.roll(x, 1, 1))
            k_after = jnp.where(lane == NK - 1, 0.0, pltpu.roll(x, NK - 1, 1))
            s = f_ref[at[i], :] + 0.5 * (
                (before - after) + (j_before - j_after) + (k_before - k_after)
            )
            s_ref[at[i], :] = s
            t_ref[at[i], :] = edge_rows(weight_ref, v, s)
        return 0

    lax.fori_loop(0, NV, step, 0)


def source_kernel(
    t_in, ia_ref, ib_ref, ja_ref, jb_ref, halo_ref, weight_ref, co_ref,
    low_ref, high_ref, face_ref, keep_ref, send_ref, t_scr,
):
    p, q = lax.axis_index("line"), lax.axis_index("plane")
    even_line, even_plane = lax.rem(p, 2) == 0, lax.rem(q, 2) == 0
    for v in range(NV):
        ia, ib = ia_ref[v], ib_ref[v]
        low = jnp.where(p == 0, 0.0, jnp.where(even_line, ib, ia))
        high = jnp.where(p == 3, 0.0, jnp.where(even_line, ia, ib))
        ja, jb = ja_ref[v], jb_ref[v]
        j_low = jnp.where(q == 0, 0.0, jnp.where(even_plane, jb, ja))
        j_high = jnp.where(q == 63, 0.0, jnp.where(even_plane, ja, jb))
        low_ref[v] = j_low
        high_ref[v] = j_high
        ends = []
        for n, face in enumerate((0.5 * low, -0.5 * high)):
            face_ref[v, n] = face
            ends.append(edge_rows(weight_ref, v, face))
        a, b = halo_ref[v, 0], halo_ref[v, 1]
        for i in range(NI):
            at = slice(v * PLANE + i * NJ, v * PLANE + i * NJ + NJ)
            t = t_in[at, :] + a * j_low[i : i + 1] + b * j_high[i : i + 1]
            if i == 0:
                t = t + ends[0]
            if i == NI - 1:
                t = t + ends[1]
            for half in range(2):
                t_scr[half, at, :] = t[:, half * HALF : half * HALF + HALF]
        for n in range(2):
            a, b = (t_scr[half, pl.ds(v * PLANE + 4 * n, NI, stride=NJ), :] for half in range(2))
            at = slice(v * 32 + n * NI, v * 32 + n * NI + NI)
            keep_ref[at, :] = jnp.where(even_plane, a, b)
            send_ref[at, :] = jnp.where(even_plane, b, a)
    a, b = co_ref[:, :HALF], co_ref[:, HALF:]
    keep_ref[160:, :] = jnp.where(even_plane, a, b)
    send_ref[160:, :] = jnp.where(even_plane, b, a)


def layers_kernel(keep_ref, got_ref, c_ref, maps_ref, out_ref, msg_ref, t_scr):
    even = place()[0] == 0
    tile = (NJ, HALF)
    row = rows_of(tile)
    low, high = ordered(even, [keep_ref[...]], [got_ref[...]])
    low, high = low[0], high[0]
    for v in range(NV):
        for i in range(NI):
            a, b = v * 32 + i, v * 32 + NI + i
            t_scr[v * PLANE + i * NJ : v * PLANE + i * NJ + NJ, :] = jnp.where(
                row == 0,
                low[a : a + 1],
                jnp.where(row == 1, low[b : b + 1], jnp.where(row == 2, high[a : a + 1], high[b : b + 1])),
            )
    ends = local_sweeps(c_ref, t_scr, out_ref, out_ref)
    for v in range(NV):
        for n in range(2):
            a, b = ends[v][2 * n : 2 * n + 2]
            at = v * 16 + n * 8
            msg_ref[at : at + 8, :] = jnp.where(row < 4, a, pltpu.roll(b, 4, 0))
    msg_ref[MAPS:, :] = jnp.where(even, maps_ref[:, :HALF], maps_ref[:, HALF:])


def local_sweeps(c_ref, src_ref, tmp_ref, out_ref):
    zero = jnp.zeros((NJ, src_ref.shape[-1]), F32)
    one, two = [zero] * NV, [zero] * NV
    for i in range(NI):
        for v in range(NV):
            first, second, scale = (c_ref[v, n, i : i + 1, :] for n in range(3))
            at = slice(v * PLANE + i * NJ, v * PLANE + i * NJ + NJ)
            one[v], two[v] = scale * src_ref[at, :] + first * one[v] + second * two[v], one[v]
            tmp_ref[at, :] = one[v]
    ends = list(zip(one, two))
    one, two = [zero] * NV, [zero] * NV
    for i in reversed(range(NI)):
        for v in range(NV):
            first, second, scale = (c_ref[v, n, i : i + 1, :] for n in range(3, 6))
            at = slice(v * PLANE + i * NJ, v * PLANE + i * NJ + NJ)
            one[v], two[v] = scale * tmp_ref[at, :] + first * one[v] + second * two[v], one[v]
            out_ref[at, :] = one[v]
    return [ends[v] + (one[v], two[v]) for v in range(NV)]


def planes_kernel(
    c_ref, x_ref, s_ref, low_ref, high_ref, face_ref, maps_ref, out_ref, msg_ref, g_scr
):
    row = rows_of(TILE)
    for v in range(NV):
        fd, bd = x_ref[v, 1], x_ref[v, 3]
        up, dn = up_steps(x_ref[v, 0]), down_steps(x_ref[v, 2])
        for i in range(NI):
            at = slice(v * PLANE + i * NJ, v * PLANE + i * NJ + NJ)
            low, high = low_ref[v, i : i + 1, :], high_ref[v, i : i + 1, :]
            s = s_ref[at, :] + jnp.where(
                row == 0, 0.5 * low, jnp.where(row == NJ - 1, -0.5 * high, 0.0)
            )
            if i in (0, NI - 1):
                s = s + face_ref[v, 0 if i == 0 else 1]
            g_scr[at, :] = scan_down(bd * scan_up(fd * s, up), dn)
    ends = local_sweeps(c_ref, g_scr, out_ref, out_ref)
    for v in range(NV):
        for n, x in enumerate(ends[v]):
            msg_ref[v * 32 + n * NJ : v * 32 + n * NJ + NJ, :] = x
    msg_ref[BIG:, :] = maps_ref[...]


def maps_of(ref, v, at=MAPS):
    return ref[at + v * 12 : at + v * 12 + 12, :]


def line_pair(p, own, got):
    is_low = lax.rem(p, 2) == 0
    return (
        [jnp.where(is_low, a, b) for a, b in zip(own, got)],
        [jnp.where(is_low, b, a) for a, b in zip(own, got)],
    )


def l_after(m, phi, l):
    return (
        m[0:1] * l[0] + m[1:2] * l[1] + phi[0],
        m[2:3] * l[0] + m[3:4] * l[1] + phi[1],
    )


def u_before(m, beta, l, u):
    return (
        m[4:5] * l[0] + m[5:6] * l[1] + m[6:7] * u[0] + m[7:8] * u[1] + beta[0],
        m[8:9] * l[0] + m[9:10] * l[1] + m[10:11] * u[0] + m[11:12] * u[1] + beta[1],
    )


def pair_states(p, low, high):
    lm, la, lb, lc, ld = low
    hm, ha, hb, hc, hd = high
    phi = l_after(hm, (ha, hb), (la, lb))
    zero = jnp.zeros_like(la)
    beta = u_before(lm, (lc, ld), (zero, zero), u_before(hm, (hc, hd), (la, lb), (zero, zero)))
    upper = p >= 2
    return [jnp.where(upper, a, b) for a, b in zip(beta, phi)]


def pair_gamma(low_m, high_m):
    columns = []
    for c in range(2):
        l = (low_m[c : c + 1], low_m[2 + c : 3 + c])
        a = high_m[4:5] * l[0] + high_m[5:6] * l[1]
        b = high_m[8:9] * l[0] + high_m[9:10] * l[1]
        columns.append(
            (
                low_m[4 + c : 5 + c] + low_m[6:7] * a + low_m[7:8] * b,
                low_m[8 + c : 9 + c] + low_m[10:11] * a + low_m[11:12] * b,
            )
        )
    (raa, rba), (rab, rbb) = columns
    return raa, rab, rba, rbb


def entering(p, low, high, mine, got, gamma):
    upper, is_low = p >= 2, lax.rem(p, 2) == 0
    zero = jnp.zeros_like(mine[0])
    l = [jnp.where(upper, x, zero) for x in got]
    raa, rab, rba, rbb = gamma
    u = (
        got[0] + raa * mine[0] + rab * mine[1],
        got[1] + rba * mine[0] + rbb * mine[1],
    )
    u = [jnp.where(upper, zero, x) for x in u]
    l_high = l_after(low[0], low[1:3], l)
    u_low = u_before(high[0], high[3:5], l_high, u)
    return [jnp.where(is_low, a, b) for a, b in zip(l, l_high)] + [
        jnp.where(is_low, a, b) for a, b in zip(u_low, u)
    ]


def edges_kernel(
    layers_ref, resp_ref, keep_ref, gotc_ref, own_ref, got1_ref, got2_ref, got3_ref,
    low_ref, high_ref, chip_ref,
):
    p, core = lax.axis_index("line"), place()[0]
    refs = (own_ref, got1_ref, got2_ref, got3_ref)
    for v in range(NV):
        rows, maps = [], []
        for r in range(4):
            at = slice(v * 16, v * 16 + 16)
            rows.append(pick(p, [refs[r ^ own][at, :] for own in range(4)]))
            maps.append(pick(p, [maps_of(refs[r ^ own], v) for own in range(4)]))
        part = [[x[n * 4 : n * 4 + 4] for n in range(4)] for x in rows]
        zero = jnp.zeros((4, HALF), F32)
        low = [(zero, zero), (part[0][0], part[0][1])]
        for r in (1, 2):
            low.append(l_after(maps[r], part[r][:2], low[r]))
        high = [None, None, None, (zero, zero)]
        for r in (3, 2, 1):
            high[r - 1] = u_before(maps[r], part[r][2:], low[r], high[r])
        states = [pick(p, [x[t] for x in low]) for t in range(2)]
        states += [pick(p, [x[t] for x in high]) for t in range(2)]
        answers = [resp_ref[core, pl.ds(v * PLANE + n, NI, stride=NJ), :] for n in range(4)]
        for t in range(4):
            x = layers_ref[pl.ds(v * PLANE + t, NI, stride=NJ), :]
            for n in range(4):
                x = x + answers[n] * states[n][t : t + 1]
            at = v * 32 + (t % 2) * NI
            (low_ref, high_ref)[t // 2][at : at + NI, :] = x
    own, other = keep_ref[160:, :], gotc_ref[160:, :]
    low_ref[160:, :] = jnp.where(core == 0, own, other)
    high_ref[160:, :] = jnp.where(core == 0, other, own)
    store(chip_ref, compose(load(low_ref), load(high_ref)))


BIG = NV * 32
LAST = NV * 16


def big_parts(ref, v):
    at = v * 32
    return [maps_of(ref, v, BIG)] + [ref[at + n * NJ : at + n * NJ + NJ, :] for n in range(4)]


def last_parts(ref, v):
    at = v * 16
    return ref[at : at + NJ, :], ref[at + NJ : at + 2 * NJ, :]


def last_gamma(ref, v):
    return [ref[LAST + v * 4 + n : LAST + v * 4 + n + 1, :] for n in range(4)]


def plane_pair_kernel(own_ref, got_ref, out_ref):
    p = lax.axis_index("line")
    for v in range(NV):
        low, high = line_pair(p, big_parts(own_ref, v), big_parts(got_ref, v))
        a, b = pair_states(p, low, high)
        out_ref[v * 16 : v * 16 + NJ, :] = a
        out_ref[v * 16 + NJ : v * 16 + 2 * NJ, :] = b
        for n, x in enumerate(pair_gamma(low[0], high[0])):
            out_ref[LAST + v * 4 + n : LAST + v * 4 + n + 1, :] = x
    out_ref[LAST + 20 :, :] = jnp.zeros((4, NK), F32)


def solved_kernel(local_ref, resp_ref, own_ref, got_ref, mine2_ref, got2_ref, out_ref):
    p = lax.axis_index("line")
    for v in range(NV):
        low, high = line_pair(p, big_parts(own_ref, v), big_parts(got_ref, v))
        mine, got = last_parts(mine2_ref, v), last_parts(got2_ref, v)
        states = entering(p, low, high, mine, got, last_gamma(got2_ref, v))
        for i in range(NI):
            at = v * PLANE + i * NJ
            for part in range(2):
                lane = slice(part * HALF, part * HALF + HALF)
                x = local_ref[at : at + NJ, lane]
                for n in range(4):
                    x = x + resp_ref[part, at + n : at + n + 1, :] * states[n][:, lane]
                out_ref[at : at + NJ, lane] = x


def load(ref):
    phi = [ref[v * 32 : v * 32 + NI, :] for v in range(NV)]
    beta = [ref[v * 32 + NI : v * 32 + 2 * NI, :] for v in range(NV)]
    return (phi, beta, ref[160:165, :], ref[165:170, :], ref[170:175, :])


def store(ref, agg):
    phi, beta, F, B, g = agg
    for v in range(NV):
        ref[v * 32 : v * 32 + NI, :] = phi[v]
        ref[v * 32 + NI : v * 32 + 2 * NI, :] = beta[v]
    ref[160:165, :] = F
    ref[165:170, :] = B
    ref[170:175, :] = g
    ref[175:176, :] = jnp.zeros((1, HALF), F32)


def choose(low_is_own, own, other):
    return jax.tree.map(lambda a, b: jnp.where(low_is_own, a, b), own, other)


def ordered(low_is_own, own, other):
    return choose(low_is_own, own, other), choose(low_is_own, other, own)


def compose(low, high):
    lp, lb, lF, lB, lg = low
    hp, hb, hF, hB, hg = high
    at = [slice(v, v + 1) for v in range(NV)]
    return (
        [hF[at[v]] * lp[v] + hp[v] for v in range(NV)],
        [lb[v] + lB[at[v]] * (hb[v] + hg[at[v]] * lp[v]) for v in range(NV)],
        hF * lF,
        lB * hB,
        lg + lB * hg * lF,
    )


def f_after(agg, f):
    return [agg[2][v : v + 1] * f[v] + agg[0][v] for v in range(NV)]


def g_before(agg, f, u):
    return [agg[1][v] + agg[4][v : v + 1] * f[v] + agg[3][v : v + 1] * u[v] for v in range(NV)]


def bit_clear(z, n):
    return lax.rem(z // n, 2) == 0


def members(refs):
    m = lax.rem(place()[1], 4)
    parts = [load(r) for r in refs]
    return [
        jax.tree.map(lambda *x: pick(m, x), *(parts[r ^ own] for own in range(4)))
        for r in range(4)
    ]


def quad_kernel(*refs):
    a, b, c, d = members(refs[:4])
    store(refs[-1], compose(compose(a, b), compose(c, d)))


def ring_kernel(own_ref, got_ref, after_ref, out_ref, fore_ref):
    agg = compose(*ordered(bit_clear(place()[1], 4), load(own_ref), load(got_ref)))
    store(out_ref, agg)
    last = place()[2] == 3
    for v in range(NV):
        fore_ref[v * NI : v * NI + NI, :] = jnp.where(last, agg[1][v], agg[0][v])
    fore_ref[80:, :] = out_ref[160:, :]


def step_down(low, high, f, u):
    f_high = f_after(low, f)
    u_low = g_before(high, f_high, u)
    return (f, u_low), (f_high, u)


def put_states(ref, states):
    for v in range(NV):
        ref[v * 32 : v * 32 + NI, :] = states[0][v]
        ref[v * 32 + NI : v * 32 + 2 * NI, :] = states[1][v]


def down_kernel(
    own_ref, one_ref, three_ref, two_ref, own4_ref, got4_ref,
    q0_ref, q1_ref, q2_ref, q3_ref, low_ref, high_ref, after_ref, keep_ref, send_ref,
):
    core, z, y = place()
    own, two, three = (load(r) for r in (own_ref, two_ref, three_ref))
    x = [one_ref[v * NI : v * NI + NI, :] for v in range(NV)]
    one = (x, x, one_ref[80:85, :], one_ref[85:90, :], one_ref[90:95, :])

    def sort(*groups):
        return jax.tree.map(lambda *x: pick(y, x), *groups)

    ups = (own, one, two, three), (three, own, one, two), (two, three, own, one)
    ups = [sort(*group) for group in ups]
    downs = [three, choose(y == 0, two, three), sort(one, two, three)]
    zero = [jnp.zeros((NI, HALF), F32)] * NV
    fs = [zero, ups[0][0]]
    fs.append(f_after(ups[1], fs[1]))
    fs.append(f_after(ups[2], fs[2]))
    us = [None, None, None, zero]
    for n in (3, 2, 1):
        us[n - 1] = g_before(downs[n - 1], fs[n], us[n])
    f, u = sort(*fs), sort(*us)
    is_low = bit_clear(z, 4)
    low, high = ordered(is_low, load(own4_ref), load(got4_ref))
    f, u = choose(is_low, *step_down(low, high, f, u))
    parts = members((q0_ref, q1_ref, q2_ref, q3_ref))
    fs, us = [f], [None, None, None, u]
    for r in range(3):
        fs.append(f_after(parts[r], fs[r]))
    for r in (3, 2, 1):
        us[r - 1] = g_before(parts[r], fs[r], us[r])
    m = lax.rem(z, 4)
    f = [pick(m, [x[v] for x in fs]) for v in range(NV)]
    u = [pick(m, [x[v] for x in us]) for v in range(NV)]
    is_low = core == 0
    low, high = step_down(load(low_ref), load(high_ref), f, u)
    put_states(keep_ref, choose(is_low, low, high))
    put_states(send_ref, choose(is_low, high, low))


def final_kernel(g_ref, resp_ref, mine_ref, other_ref, out_ref, scr, fu_scr, sems):
    even = place()[0] == 0

    def copy(v):
        at = pl.ds(v * PLANE, PLANE)
        return pltpu.make_async_copy(scr.at[at], out_ref.at[at], sems.at[v])

    for v in range(NV):
        x, y = mine_ref[v * 32 : v * 32 + 32, :], other_ref[v * 32 : v * 32 + 32, :]
        fu_scr[v, :, :HALF] = jnp.where(even, x, y)
        fu_scr[v, :, HALF:] = jnp.where(even, y, x)
        a, b = resp_ref[v, 0], resp_ref[v, 1]
        for i in range(NI):
            at = slice(v * PLANE + i * NJ, v * PLANE + i * NJ + NJ)
            f, u = fu_scr[v, i : i + 1, :], fu_scr[v, NI + i : NI + i + 1, :]
            scr[at, :] = g_ref[at, :] + a * f + b * u
        copy(v).start()
    for v in range(NV):
        copy(v).wait()


def swap(x, axis, size, flip):
    return lax.ppermute(x, axis, [(i, i ^ flip) for i in range(size)])


def everyone(x, partner):
    places = [(p, q) for p in range(4) for q in range(64)]
    pairs = [(p * 64 + q, partner(p, q)) for p, q in places]
    return lax.ppermute(x, ("line", "plane"), [(n, p * 64 + q) for n, (p, q) in pairs])


def shift(x, axis, size, by):
    return lax.ppermute(x, axis, [(i, (i + by) % size) for i in range(size)])


def across(x):
    pairs = []
    for q in range(64):
        z = q // 2 % 8
        other = (6 - z if z % 2 == 0 else 8 - z) % 8
        pairs.append((q, q + 2 * (other - z)))
    return lax.ppermute(x, "plane", pairs)


def body(adjoint, forcing, eigen_values, face_masks, line_coeffs, cross_coeffs):
    flat = (NV * PLANE, NK)
    a, f, e = (x.reshape(flat) for x in (adjoint, forcing, eigen_values))
    i_face, j_face = (NV, NJ, NK), (NV, NI, NK)
    masks = jax.ShapeDtypeStruct(face_masks.shape, face_masks.dtype)
    w, ia, ib, ja, jb, x, m = call(
        faces_kernel, [flat, i_face, i_face, j_face, j_face, cross_coeffs.shape, masks],
        a, e, cross_coeffs, face_masks, in_hbm=4, name="faces",
        scratch=[
            pltpu.VMEM(flat, F32),
            pltpu.VMEM(flat, F32),
            pltpu.VMEM((NV, 2, PLANE, HALF), F32),
            pltpu.SemaphoreType.DMA((NV, 4)),
            pltpu.SemaphoreType.DMA((2,)),
        ],
    )
    ia = swap(ia, "line", 4, 1)
    ib = everyone(ib, lambda p, q: (3 - p, q) if p in (1, 2) else (p, q ^ 1))
    ja = swap(ja, "plane", 64, 1)
    jb = everyone(jb, lambda p, q: (p ^ 1, q) if q in (0, 63) else (p, q + 1 if q % 2 else q - 1))

    halves = (2, NV * PLANE, HALF)
    half, line_resp, maps, cross_resp, halo_resp, weights, co, s, t = call(
        prep_kernel,
        [
            line_coeffs.shape[:3] + (HALF,), halves, (64, NK), (NV, 2, NJ, NK), (NV, 2, NJ, NK),
            (NV, 2, NJ, NK), (16, NK), flat, flat,
        ],
        x, m, w, f, line_coeffs, name="prep", flops=10**7,
    )
    msg = (176, HALF)
    j_low, j_high, faces, keep, send = call(
        source_kernel, [j_face, j_face, (NV, 2, NJ, NK), msg, msg],
        t, ia, ib, ja, jb, halo_resp, weights, co, scratch=[pltpu.VMEM(halves, F32)], name="source",
    )
    got = swap(send, "plane", 64, 1)
    half_flat = (NV * PLANE, HALF)
    layers, small = call(
        layers_kernel, [half_flat, (MAPS + 64, HALF)], keep, got, half, maps,
        scratch=[pltpu.VMEM(half_flat, F32)], name="layers",
    )
    smalls = [small] + [swap(small, "line", 4, d) for d in (1, 2, 3)]
    low, high, chip = call(
        edges_kernel, [msg, msg, msg],
        layers, line_resp, keep, got, *smalls, name="edges",
    )
    quad = [chip] + [swap(chip, "plane", 64, d) for d in (2, 4, 6)]

    local, big = call(
        planes_kernel, [flat, (BIG + 64, NK)],
        line_coeffs, x, s, j_low, j_high, faces, maps,
        scratch=[pltpu.VMEM(flat, F32)], name="planes", flops=10**7,
    )
    got_big = swap(big, "line", 4, 1)
    last_big = call(plane_pair_kernel, [(LAST + 24, NK)], big, got_big, name="plane_pair")[0]
    got_last_big = swap(last_big, "line", 4, 3)
    solved = call(
        solved_kernel, [flat], local, line_resp, big, got_big, last_big, got_last_big,
        name="solved", flops=10**7,
    )[0]

    own4 = call(quad_kernel, [msg], *quad, big, name="quad")[0]
    got4 = across(own4)
    ring, fore = call(ring_kernel, [msg, (96, HALF)], own4, got4, last_big, name="ring")
    y1, y2, y3 = (
        shift(fore, "plane", 64, 16), shift(ring, "plane", 64, 32), shift(ring, "plane", 64, 48)
    )
    mine, send = call(
        down_kernel, [(160, HALF)] * 2,
        ring, y1, y3, y2, own4, got4, *quad, low, high, solved, name="down",
    )
    other = swap(send, "plane", 64, 1)
    out = call(
        final_kernel, [flat], solved, cross_resp, mine, other, out_hbm=True, name="final",
        scratch=[
            pltpu.VMEM(flat, F32),
            pltpu.VMEM((NV, 2 * NI, NK), F32),
            pltpu.SemaphoreType.DMA((NV,)),
        ],
    )[0]
    return out.reshape(NV, NI, NJ, NK)


def solution(mesh):
    return jax.shard_map(
        body,
        mesh=mesh,
        in_specs=(
            P(None, "line", "plane", None),
            P(None, "line", "plane", None),
            P(None, "line", "plane", None),
            P(None, "plane", None),
            P(None, None, "line", None),
            P(None, None, "plane", None),
        ),
        out_specs=P(None, "line", "plane", None),
        check_vma=False,
    )
```
